32 devices in a mesh: curve: 16 (over z, y, x), sub: 2 (over core).
Axes of the slice: x: 2, y: 2, z: 4, core: 2. Of those that a mesh axis runs over, the one named last changes fastest.
Arguments:
- pressure: float32 [128, 4096], P(('curve', 'sub')), may hold values from -6 to 6
- source_term: float32 [128, 4096], P(('curve', 'sub')), may hold values from -7 to 7
- coefficient: float32 [128, 4096], P(('curve', 'sub')), may hold values from 0.05 to 2
- new_slot: int32 [128], P(('curve', 'sub')), may hold values from 0 to 7, as said below
- face_links: int32 [128, 6], P(('curve', 'sub')), may hold values from -1 to 127, as said below
Outputs:
- corrected: float32 [128, 4096], P(('curve', 'sub'))
The draws below stay inside these ranges and needn't reach their ends.
Inputs may be any that keep to these rules, and one draw needn't show every extreme that they name: `new_slot`: every block stays within its Z-order range of 8 blocks; within a range the slots form a permutation, each device receives exactly 4 blocks, and one device hands at most 2 blocks to one device, a bound reached by every device. `face_links`: A neighbour of block b lies in range b // 8 - 1, b // 8 or b // 8 + 1.
All inputs are finite; a program needn't handle non-finite values.
Results may differ from the reference program's by a relative error of at most 0.0001.
Values sent between devices are 32-bit elements; how exact they have to be, the bound alone decides.
A program may use at most 64 MiB of HBM per device.

```python
import math
import jax
import jax.numpy as jnp

B_DEV = 4
PRE_SWEEPS = 2
COARSE_SWEEPS = 4
MOST = 2
GROUP = 8
BLOCKS = 128


def draw_new_slot(key, part):
    ngroups = BLOCKS // GROUP
    nsub = GROUP // B_DEV
    kinds = B_DEV // MOST
    first_key, second_key = jax.random.split(jax.random.fold_in(key, 11))
    offsets = jax.vmap(lambda k: jax.random.permutation(k, nsub))(jax.random.split(first_key, ngroups))[:, :kinds]
    orders = jax.vmap(lambda k: jax.random.permutation(k, B_DEV))(jax.random.split(second_key, ngroups * nsub))
    orders = orders.reshape(ngroups, nsub, B_DEV)
    kind_of = orders // MOST
    within = orders % MOST
    spread = jnp.broadcast_to(offsets[:, None, :], (ngroups, nsub, kinds))
    chosen = jnp.take_along_axis(spread, kind_of, axis=2)
    sub_index = jnp.arange(nsub, dtype=jnp.int32)[None, :, None]
    target_dev = (sub_index + chosen) % nsub
    position = kind_of * MOST + within
    return (target_dev * B_DEV + position).reshape(-1).astype(jnp.int32)


def draw_face_links(key, part):
    ngroups = BLOCKS // GROUP
    first_key, second_key, third_key = jax.random.split(jax.random.fold_in(key, 23), 3)
    ranges = (jnp.arange(BLOCKS, dtype=jnp.int32) // GROUP)[:, None]
    moves = jax.random.randint(first_key, (BLOCKS, 6), -1, 2)
    inner = jax.random.randint(second_key, (BLOCKS, 6), 0, GROUP)
    walls = jax.random.randint(third_key, (BLOCKS, 6), 0, 8) == 0
    other = ranges + moves
    usable = (other >= 0) & (other < ngroups) & jnp.logical_not(walls)
    links = jnp.where(usable, other * GROUP + inner, -1)
    links = links.at[0, 0].set(-1).at[BLOCKS - 2, 1].set(BLOCKS - 1)
    return links.astype(jnp.int32)


def draw_source_term(key, part):
    noise_key, level_key, sign_key = jax.random.split(jax.random.fold_in(key, 37), 3)
    noise = jnp.clip(jax.random.normal(noise_key, (BLOCKS, 4096), jnp.float32), -4.0, 4.0)
    magnitude = jax.random.uniform(level_key, (BLOCKS, 1), jnp.float32, 0.5, 3.0)
    signs = jnp.where(jax.random.uniform(sign_key, (BLOCKS, 1), jnp.float32) < 0.5, -1.0, 1.0)
    level = magnitude * signs
    return (noise + level).astype(jnp.float32)


def shard_levels(own_key, dims, shards, low, largest):
    def one(dim, parts):
        heights = jax.random.uniform(jax.random.fold_in(jax.random.fold_in(own_key, 6), dim), (parts,), jnp.float32, low / len(shards), largest / len(shards))
        return jnp.repeat(jnp.exp(heights), dims[dim] // parts).reshape((-1,) + (1,) * (len(dims) - dim - 1))

    gain = one(*shards[0])
    for cut in shards[1:]:
        gain = gain * one(*cut)
    return gain


def scatter_about(stream_key, dims, deviation, limit, cuts=(), kind=jnp.bfloat16):
    gain = shard_levels(stream_key, dims, cuts, -0.22, 0.18) if cuts else 1.0
    entries = jax.random.normal(stream_key, dims, jnp.float32) * deviation * gain
    return jnp.minimum(jnp.maximum(entries, -limit), limit).astype(kind)


def setup_inputs(seed: int = 0) -> dict:
    key_of = jax.random.split(jax.random.key(seed), 6)
    pressure = scatter_about(key_of[0], (BLOCKS, 4096), 1.0, 6.0, ((0, 32),), jnp.float32)
    source_term = draw_source_term(jax.random.fold_in(key_of[5], 71), 0)
    coefficient = jnp.clip(jnp.exp(math.log(2.0) - 3.6888794 * jax.random.uniform(key_of[2], (BLOCKS, 4096), jnp.float32) ** shard_levels(key_of[2], (BLOCKS, 4096), ((0, 32),), -0.2, 0.2)), 0.05, 2.0)
    new_slot = draw_new_slot(jax.random.fold_in(key_of[5], 71), 0)
    face_links = draw_face_links(jax.random.fold_in(key_of[5], 71), 0)
    return dict(pressure=pressure, source_term=source_term, coefficient=coefficient, new_slot=new_slot, face_links=face_links)


relaxation = 0.8


def face_stack(field):
    cubes = field.reshape(-1, 16, 16, 16)
    layers = [cubes[:, 0], cubes[:, -1], cubes[:, :, 0], cubes[:, :, -1], cubes[:, :, :, 0], cubes[:, :, :, -1]]
    return jnp.stack(layers, axis=1).reshape(-1, 6, 256)


def apply_operator(field, ghosts, coefficient):
    cubes = field.reshape(-1, 16, 16, 16)
    sides = ghosts.reshape(-1, 6, 16, 16)
    padded = jnp.pad(cubes, ((0, 0), (1, 1), (1, 1), (1, 1)))
    padded = padded.at[:, 0, 1:-1, 1:-1].set(sides[:, 0]).at[:, -1, 1:-1, 1:-1].set(sides[:, 1])
    padded = padded.at[:, 1:-1, 0, 1:-1].set(sides[:, 2]).at[:, 1:-1, -1, 1:-1].set(sides[:, 3])
    padded = padded.at[:, 1:-1, 1:-1, 0].set(sides[:, 4]).at[:, 1:-1, 1:-1, -1].set(sides[:, 5])
    beside = padded[:, 2:, 1:-1, 1:-1] + padded[:, :-2, 1:-1, 1:-1]
    beside = beside + padded[:, 1:-1, 2:, 1:-1] + padded[:, 1:-1, :-2, 1:-1]
    beside = beside + padded[:, 1:-1, 1:-1, 2:] + padded[:, 1:-1, 1:-1, :-2]
    return (6.0 + coefficient) * field - beside.reshape(-1, 4096)


def ghost_layers(field, face_links):
    faces = face_stack(field)
    opposite = faces[:, jnp.array([1, 0, 3, 2, 5, 4], dtype=jnp.int32)]
    clipped = jnp.clip(face_links, 0, faces.shape[0] - 1)
    picked = opposite[clipped, jnp.arange(6, dtype=jnp.int32)[None, :]]
    return picked * (face_links >= 0).astype(jnp.float32)[:, :, None]


def sweep(field, source, coefficient, face_links):
    image = apply_operator(field, ghost_layers(field, face_links), coefficient)
    return field + relaxation * (source - image) / (6.0 + coefficient)


def reference(pressure, source_term, coefficient, new_slot, face_links):
    ranges = jnp.arange(BLOCKS, dtype=jnp.int32) // GROUP
    target = (ranges * GROUP + new_slot).astype(jnp.int32)
    empty = jnp.zeros((BLOCKS, 4096), jnp.float32)
    moved_p = empty.at[target].set(pressure)
    moved_f = empty.at[target].set(source_term)
    moved_c = empty.at[target].set(coefficient)
    smoothed = moved_p
    for step in range(PRE_SWEEPS):
        smoothed = sweep(smoothed, moved_f, moved_c, face_links)
    residual = moved_f - apply_operator(smoothed, ghost_layers(smoothed, face_links), moved_c)
    block_residual = jnp.mean(residual, axis=1)
    block_diag = 6.0 + jnp.mean(moved_c, axis=1)
    block_error = jnp.zeros((BLOCKS,), jnp.float32)
    valid = face_links >= 0
    clipped = jnp.clip(face_links, 0, BLOCKS - 1)
    for step in range(COARSE_SWEEPS):
        beside = jnp.sum(jnp.where(valid, block_error[clipped], 0.0), axis=1)
        block_error = block_error + relaxation * (block_residual - block_diag * block_error + beside) / block_diag
    lifted = smoothed + block_error[:, None]
    return sweep(lifted, moved_f, moved_c, face_links)
```

```python
import functools

import jax
import jax.numpy as jnp
from jax import lax
from jax.experimental import pallas as pl
from jax.experimental.pallas import tpu as pltpu
from jax.sharding import PartitionSpec as P

PRE_SWEEPS = 2
COARSE_SWEEPS = 4
SIDE = 16
FACE = SIDE * SIDE
FACES = 6
LANES = 128
FLIP = (1, 0, 3, 2, 5, 4)

relaxation = 0.8
MESH = pl.DeviceIdType.MESH


def kernel(
    count,
    nsub,
    blocks,
    slot_ref,
    link_ref,
    p_ref,
    f_ref,
    c_ref,
    out_ref,
    raw,
    first,
    window_a,
    window_b,
    ghosts,
    peer_p,
    peer_f,
    peer_c,
    mf,
    mc,
    inv,
    u_a,
    u_b,
    base,
    coarse,
    raw_send,
    raw_recv,
    face_send,
    face_recv,
    peer_send,
    peer_recv,
    coarse_send,
    coarse_recv,
):
    pos = lax.axis_index("curve")
    sub = lax.axis_index("sub")
    group = nsub * blocks
    reach = COARSE_SWEEPS
    wall = 3 * nsub
    windows = (window_a, window_b)

    def partners(radius):
        for t in range(-radius, radius + 1):
            for ds in range(nsub):
                if t or ds:
                    yield t, lax.rem(sub + ds, nsub)

    def guarded(t, action):
        if t == 0:
            action()
        else:
            there = pos + t
            pl.when((there >= 0) & (there < count))(action)

    for window in (first, *windows):
        window[wall] = jnp.zeros(window.shape[1:], jnp.float32)
        for t in (-1, 1):

            @pl.when((pos + t < 0) | (pos + t >= count))
            def _(window=window, t=t):
                for s in range(nsub):
                    window[(t + 1) * nsub + s] = jnp.zeros(window.shape[1:], jnp.float32)

    for t in (-1, 1):

        @pl.when((pos + t < 0) | (pos + t >= count))
        def _(t=t):
            for s in range(nsub):
                raw[(t + 1) * nsub + s] = jnp.zeros(raw.shape[1:], jnp.float32)

    for t in range(-reach, reach + 1):
        if t:

            @pl.when((pos + t < 0) | (pos + t >= count))
            def _(t=t):
                for s in range(nsub):
                    coarse[(t + reach) * nsub + s] = jnp.zeros(coarse.shape[1:], jnp.float32)

    barrier = pltpu.get_barrier_semaphore()
    for t, s in partners(reach):

        def greet(t=t, s=s):
            pl.semaphore_signal(barrier, inc=1, device_id=(pos + t, s), device_id_type=MESH)

        guarded(t, greet)
    low = jnp.minimum(pos, reach)
    high = jnp.minimum(count - 1 - pos, reach)
    pl.semaphore_wait(barrier, (low + high + 1) * nsub - 1)

    def descriptor(source, window, sends, recvs, radius, t, s):
        slot = (radius - t) * nsub + sub
        return pltpu.make_async_remote_copy(
            src_ref=source,
            dst_ref=window.at[slot],
            send_sem=sends.at[(t + radius) * nsub + s],
            recv_sem=recvs.at[slot],
            device_id=(pos + t, s),
            device_id_type=MESH,
        )

    def send_all(window, sends, recvs, radius):
        own = window.at[radius * nsub + sub]
        for t, s in partners(radius):

            def go(t=t, s=s):
                descriptor(own, window, sends, recvs, radius, t, s).start()

            guarded(t, go)

    def wait_all(window, sends, recvs, radius):
        own = window.at[radius * nsub + sub]
        for t, s in partners(radius):

            def hold(t=t, s=s):
                slot = (t + radius) * nsub + s
                pltpu.make_async_remote_copy(
                    src_ref=own,
                    dst_ref=window.at[slot],
                    send_sem=sends.at[slot],
                    recv_sem=recvs.at[slot],
                    device_id=(pos + t, s),
                    device_id_type=MESH,
                ).wait_recv()

            guarded(t, hold)

    def wait_sends(window, sends, recvs, radius):
        own = window.at[radius * nsub + sub]
        for t, s in partners(radius):

            def hold(t=t, s=s):
                descriptor(own, window, sends, recvs, radius, t, s).wait_send()

            guarded(t, hold)

    lane = lax.broadcasted_iota(jnp.int32, (blocks, FACE), 1)
    strip = lane // SIDE
    within = lane % SIDE

    def pack(field, target, lead):
        def column(x):
            return field[:, x * FACE : (x + 1) * FACE]

        target[lead, :, 0:FACE] = column(0)
        target[lead, :, FACE : 2 * FACE] = column(SIDE - 1)
        y_low = y_high = z_low = z_high = jnp.zeros((blocks, FACE), jnp.float32)
        for x in range(SIDE):
            part = column(x)
            y_low = jnp.where(strip == x, pltpu.roll(part, SIDE * x, 1), y_low)
            y_high = jnp.where(strip == x, pltpu.roll(part, (SIDE * (x + 1)) % FACE, 1), y_high)
            z_low = jnp.where(within == x, pltpu.roll(part, x, 1), z_low)
            z_high = jnp.where(within == x, pltpu.roll(part, (x - SIDE + 1) % FACE, 1), z_high)
        target[lead, :, 2 * FACE : 3 * FACE] = y_low
        target[lead, :, 3 * FACE : 4 * FACE] = y_high
        target[lead, :, 4 * FACE : 5 * FACE] = z_low
        target[lead, :, 5 * FACE : 6 * FACE] = z_high

    peers = []
    for ds in range(1, nsub):
        there = lax.rem(sub + ds, nsub)
        for k, (source, landing) in enumerate(((p_ref, peer_p), (f_ref, peer_f), (c_ref, peer_c))):
            copy = pltpu.make_async_remote_copy(
                src_ref=source,
                dst_ref=landing.at[nsub - ds - 1],
                send_sem=peer_send.at[k, ds - 1],
                recv_sem=peer_recv.at[k, nsub - ds - 1],
                device_id=(pos, there),
                device_id_type=MESH,
            )
            peers.append((ds, k, landing, copy))

    own_slot = nsub + sub
    pack(p_ref, raw, own_slot)
    row = lax.broadcasted_iota(jnp.int32, (blocks, LANES), 0)
    slots = jnp.zeros((blocks, LANES), jnp.int32)
    for j in range(blocks):
        slots = jnp.where(row == j, slot_ref[j], slots)
    raw[own_slot, :, FACES * FACE :] = slots.astype(jnp.float32)
    send_all(raw, raw_send, raw_recv, 1)
    for _, _, _, copy in peers:
        copy.start()

    start = (pos - 1) * group
    places = []
    for b in range(blocks):
        for d in range(FACES):
            link = link_ref[b, d]
            offset = jnp.maximum(link - start, 0)
            places.append(
                (
                    b,
                    d,
                    jnp.where(link < 0, wall, offset // blocks),
                    jnp.where(link < 0, 0, offset % blocks),
                )
            )

    def gather(window):
        for b, d, device, place in places:
            flipped = FLIP[d]
            ghosts[d, pl.ds(b, 1), :] = window[
                device, pl.ds(place, 1), flipped * FACE : (flipped + 1) * FACE
            ]

    mine = (sub * blocks + row).astype(jnp.float32)

    def chosen(slot, j):
        return (raw[slot, j : j + 1, FACES * FACE :] == mine).astype(jnp.float32)

    def wide(select, length):
        return jnp.concatenate([select] * (length // LANES), axis=1)

    length = p_ref.shape[1]
    picks = [wide(chosen(own_slot, j), length) for j in range(blocks)]
    for source, target in ((p_ref, u_a), (f_ref, mf), (c_ref, mc)):
        total = picks[0] * source[0:1, :]
        for j in range(1, blocks):
            total = total + picks[j] * source[j : j + 1, :]
        target[...] = total

    wait_all(raw, raw_send, raw_recv, 1)

    group_row = lax.broadcasted_iota(jnp.int32, (group, LANES), 0).astype(jnp.float32)
    for t in range(3):
        total = jnp.zeros((group, FACES * FACE), jnp.float32)
        for s in range(nsub):
            slot = t * nsub + s
            for j in range(blocks):
                select = (raw[slot, j : j + 1, FACES * FACE :] == group_row).astype(jnp.float32)
                total = total + wide(select, FACES * FACE) * raw[slot, j : j + 1, : FACES * FACE]
        for s in range(nsub):
            first[t * nsub + s] = total[s * blocks : (s + 1) * blocks]
    gather(first)

    for ds in range(1, nsub):
        slot = nsub + lax.rem(sub + ds, nsub)
        picks = [wide(chosen(slot, j), length) for j in range(blocks)]
        for k, (landing, target) in enumerate(((peer_p, u_a), (peer_f, mf), (peer_c, mc))):
            pltpu.make_async_remote_copy(
                src_ref=p_ref,
                dst_ref=landing.at[ds - 1],
                send_sem=peer_send.at[k, ds - 1],
                recv_sem=peer_recv.at[k, ds - 1],
                device_id=(pos, lax.rem(sub + ds, nsub)),
                device_id_type=MESH,
            ).wait_recv()
            total = target[...]
            for j in range(blocks):
                total = total + picks[j] * landing[ds - 1, j : j + 1, :]
            target[...] = total

    inv[...] = relaxation / (6.0 + mc[...])

    def beside(field, x):
        def column(k):
            return field[:, k * FACE : (k + 1) * FACE]

        part = column(x)
        total = ghosts[0] if x == 0 else column(x - 1)
        total = total + (ghosts[1] if x == SIDE - 1 else column(x + 1))
        total = total + jnp.where(
            strip == 0,
            pltpu.roll(ghosts[2], (-SIDE * x) % FACE, 1),
            pltpu.roll(part, SIDE, 1),
        )
        total = total + jnp.where(
            strip == SIDE - 1,
            pltpu.roll(ghosts[3], SIDE * (SIDE - 1 - x), 1),
            pltpu.roll(part, FACE - SIDE, 1),
        )
        total = total + jnp.where(
            within == 0,
            pltpu.roll(ghosts[4], (-x) % FACE, 1),
            pltpu.roll(part, 1, 1),
        )
        total = total + jnp.where(
            within == SIDE - 1,
            pltpu.roll(ghosts[5], SIDE - 1 - x, 1),
            pltpu.roll(part, FACE - 1, 1),
        )
        return part, total

    def sweep(field, target):
        for x in range(SIDE):
            here = slice(x * FACE, (x + 1) * FACE)
            part, total = beside(field, x)
            target[:, here] = (1.0 - relaxation) * part + inv[:, here] * (mf[:, here] + total)

    fields = (u_a, u_b)
    for step in range(PRE_SWEEPS):
        sweep(fields[step % 2], fields[(step + 1) % 2])
        field = fields[(step + 1) % 2]
        window = windows[step]
        pack(field, window, own_slot)
        send_all(window, face_send.at[step], face_recv.at[step], 1)
        wait_all(window, face_send.at[step], face_recv.at[step], 1)
        gather(window)

    left = jnp.zeros((blocks, FACE), jnp.float32)
    added = jnp.zeros((blocks, FACE), jnp.float32)
    for x in range(SIDE):
        here = slice(x * FACE, (x + 1) * FACE)
        part, total = beside(field, x)
        driven = mf[:, here] + total
        coefficient = mc[:, here]
        left = left + (driven - (6.0 + coefficient) * part)
        added = added + coefficient
        base[:, here] = (1.0 - relaxation) * part + inv[:, here] * driven
    size = SIDE * FACE
    block_residual = jnp.sum(left, axis=1, keepdims=True) / size
    block_diag = 6.0 + jnp.sum(added, axis=1, keepdims=True) / size

    narrow = lax.broadcasted_iota(jnp.int32, (blocks, LANES), 1)
    links = jnp.zeros((blocks, LANES), jnp.int32)
    for b in range(blocks):
        for d in range(FACES):
            links = jnp.where((row == b) & (narrow == d), link_ref[b, d], links)
    message = links.astype(jnp.float32)
    message = jnp.where(narrow == FACES, block_residual, message)
    message = jnp.where(narrow == FACES + 1, block_diag, message)
    coarse[reach * nsub + sub] = message
    send_all(coarse, coarse_send, coarse_recv, reach)
    wait_all(coarse, coarse_send, coarse_recv, reach)

    shown = coarse[...]
    devices = shown.shape[0]
    shape = (devices, blocks, LANES)
    far = lax.broadcasted_iota(jnp.int32, shape, 2)
    index = lax.broadcasted_iota(jnp.int32, shape, 0) * blocks + lax.broadcasted_iota(
        jnp.int32, shape, 1
    )
    origin = ((pos - reach) * group).astype(jnp.float32)
    far_block = far.astype(jnp.float32) + origin
    linked = jnp.zeros(shape, jnp.float32)
    for d in range(FACES):
        link = shown[:, :, d : d + 1]
        linked = linked + ((link == far_block) & (link >= 0.0)).astype(jnp.float32)
    residuals = shown[:, :, FACES : FACES + 1]
    diags = shown[:, :, FACES + 1 : FACES + 2]
    diags = jnp.where(diags > 0.0, diags, 1.0)

    def turned(values):
        spread = jnp.where(index == far, values, 0.0)
        return jnp.sum(jnp.sum(spread, axis=0), axis=0, keepdims=True)

    errors = relaxation * residuals / diags
    for step in range(1, COARSE_SWEEPS):
        around = jnp.sum(linked * turned(errors)[None], axis=2, keepdims=True)
        errors = errors + relaxation * (residuals - diags * errors + around) / diags
    known = turned(errors)

    narrow_block = narrow.astype(jnp.float32) + origin
    own_row = (reach * nsub + sub) * blocks + row
    own_error = jnp.sum(jnp.where(narrow == own_row, known, 0.0), axis=1, keepdims=True)
    jumps = []
    for d in range(FACES):
        link = message[:, d : d + 1]
        hit = (link == narrow_block) & (link >= 0.0)
        jumps.append(jnp.sum(jnp.where(hit, known, 0.0), axis=1, keepdims=True) - own_error)
    plane = jnp.zeros((blocks, FACE), jnp.float32) + 6.0 * own_error
    plane = plane + jnp.where(strip == 0, jumps[2], 0.0)
    plane = plane + jnp.where(strip == SIDE - 1, jumps[3], 0.0)
    plane = plane + jnp.where(within == 0, jumps[4], 0.0)
    plane = plane + jnp.where(within == SIDE - 1, jumps[5], 0.0)
    kept = (1.0 - relaxation) * own_error
    for x in range(SIDE):
        here = slice(x * FACE, (x + 1) * FACE)
        extra = plane
        if x == 0:
            extra = extra + jumps[0]
        if x == SIDE - 1:
            extra = extra + jumps[1]
        out_ref[:, here] = base[:, here] + kept + inv[:, here] * extra

    for _, _, _, copy in peers:
        copy.wait_send()
    wait_sends(raw, raw_send, raw_recv, 1)
    for step in range(PRE_SWEEPS):
        wait_sends(windows[step], face_send.at[step], face_recv.at[step], 1)
    wait_sends(coarse, coarse_send, coarse_recv, reach)


def on_device(pressure, source_term, coefficient, new_slot, face_links):
    blocks, size = pressure.shape
    count = lax.axis_size("curve")
    nsub = lax.axis_size("sub")
    near = 3 * nsub
    wide = (2 * COARSE_SWEEPS + 1) * nsub
    others = max(1, nsub - 1)
    field = pltpu.VMEM((blocks, size), jnp.float32)
    landing = pltpu.VMEM((others, blocks, size), jnp.float32)
    dma = pltpu.SemaphoreType.DMA
    vmem = pl.BlockSpec(memory_space=pltpu.VMEM)
    smem = pl.BlockSpec(memory_space=pltpu.SMEM)
    return pl.pallas_call(
        functools.partial(kernel, count, nsub, blocks),
        out_shape=jax.ShapeDtypeStruct((blocks, size), jnp.float32),
        in_specs=[smem, smem, vmem, vmem, vmem],
        out_specs=vmem,
        scratch_shapes=[
            pltpu.VMEM((near, blocks, FACES * FACE + LANES), jnp.float32),
            pltpu.VMEM((near + 1, blocks, FACES * FACE), jnp.float32),
            pltpu.VMEM((near + 1, blocks, FACES * FACE), jnp.float32),
            pltpu.VMEM((near + 1, blocks, FACES * FACE), jnp.float32),
            pltpu.VMEM((FACES, blocks, FACE), jnp.float32),
            landing,
            landing,
            landing,
            field,
            field,
            field,
            field,
            field,
            field,
            pltpu.VMEM((wide, blocks, LANES), jnp.float32),
            dma((near,)),
            dma((near,)),
            dma((PRE_SWEEPS, near)),
            dma((PRE_SWEEPS, near)),
            dma((3, others)),
            dma((3, others)),
            dma((wide,)),
            dma((wide,)),
        ],
        compiler_params=pltpu.CompilerParams(
            collective_id=0, has_side_effects=True, vmem_limit_bytes=32 * 1024 * 1024
        ),
    )(new_slot, face_links, pressure, source_term, coefficient)


def solution(mesh):
    placed = (
        P(("curve", "sub"), None),
        P(("curve", "sub"), None),
        P(("curve", "sub"), None),
        P(("curve", "sub")),
        P(("curve", "sub"), None),
    )
    return jax.shard_map(
        on_device, mesh=mesh, in_specs=placed, out_specs=P(("curve", "sub"), None), check_vma=False
    )
```

```python
import functools

import jax
import jax.numpy as jnp
from jax import lax
from jax.experimental import pallas as pl
from jax.experimental.pallas import tpu as pltpu
from jax.sharding import PartitionSpec as P

PRE_SWEEPS = 2
COARSE_SWEEPS = 4
SIDE = 16
FACE = SIDE * SIDE
FACES = 6
LANES = 128
FLIP = (1, 0, 3, 2, 5, 4)

relaxation = 0.8
MESH = pl.DeviceIdType.MESH


def kernel(
    count,
    nsub,
    blocks,
    slot_hbm,
    link_hbm,
    p_hbm,
    f_hbm,
    c_hbm,
    out_ref,
    slot_ref,
    link_ref,
    stage_p,
    stage_f,
    stage_c,
    raw,
    first,
    window_a,
    window_b,
    ghosts,
    mf,
    mc,
    inv,
    field,
    base,
    coarse,
    local_sem,
    raw_send,
    raw_recv,
    face_send,
    face_recv,
    peer_send,
    peer_recv,
    coarse_send,
    coarse_recv,
):
    pos = lax.axis_index("curve")
    sub = lax.axis_index("sub")
    group = nsub * blocks
    reach = COARSE_SWEEPS
    wall = 3 * group
    near = (-1, 1)
    far = [t for t in range(-reach, reach + 1) if t]

    def exists(t):
        return (pos + t >= 0) & (pos + t < count)

    def guarded(t, action):
        if t == 0:
            action()
        else:
            pl.when(exists(t))(action)

    inputs = (
        (p_hbm, stage_p),
        (f_hbm, stage_f),
        (c_hbm, stage_c),
        (link_hbm, link_ref),
    )
    own_copies = [
        pltpu.make_async_copy(source, stage.at[sub], local_sem.at[k])
        for k, (source, stage) in enumerate(inputs)
    ]
    own_slots = pltpu.make_async_copy(slot_hbm, slot_ref, local_sem.at[len(inputs)])
    own_copies[0].start()
    own_slots.start()
    for copy in own_copies[1:]:
        copy.start()

    def clear(window, rows):
        window[rows] = jnp.zeros((rows.stop - rows.start,) + window.shape[1:], jnp.float32)

    for window in (first, window_a, window_b):
        clear(window, slice(wall, wall + 8))
    for t in near:

        @pl.when(jnp.logical_not(exists(t)))
        def _(t=t):
            for window in (window_a, window_b):
                clear(window, slice((t + 1) * group, (t + 2) * group))
            clear(raw, slice((t + 1) * nsub, (t + 2) * nsub))

    for t in far:

        @pl.when(jnp.logical_not(exists(t)))
        def _(t=t):
            clear(coarse, slice(t + reach, t + reach + 1))

    barrier = pltpu.get_barrier_semaphore()
    expected = 0
    for t in range(-reach, reach + 1):
        for ds in range(nsub if abs(t) <= 1 else 1):
            if t or ds:

                def greet(t=t, ds=ds):
                    pl.semaphore_signal(
                        barrier,
                        inc=1,
                        device_id=(pos + t, lax.rem(sub + ds, nsub)),
                        device_id_type=MESH,
                    )

                guarded(t, greet)
                expected = expected + (exists(t).astype(jnp.int32) if t else 1)
    pl.semaphore_wait(barrier, expected)

    def peer_copy(ds, k):
        source, stage = inputs[k]
        return pltpu.make_async_remote_copy(
            src_ref=source,
            dst_ref=stage.at[sub],
            send_sem=peer_send.at[k, ds - 1],
            recv_sem=peer_recv.at[k, nsub - ds - 1],
            device_id=(pos, lax.rem(sub + ds, nsub)),
            device_id_type=MESH,
        )

    def peer_landing(ds, k):
        source, stage = inputs[k]
        there = lax.rem(sub + ds, nsub)
        return pltpu.make_async_remote_copy(
            src_ref=source,
            dst_ref=stage.at[there],
            send_sem=peer_send.at[k, ds - 1],
            recv_sem=peer_recv.at[k, ds - 1],
            device_id=(pos, there),
            device_id_type=MESH,
        )

    for k in range(len(inputs)):
        for ds in range(1, nsub):
            peer_copy(ds, k).start()

    lane = lax.broadcasted_iota(jnp.int32, (blocks, LANES), 1)
    row = lax.broadcasted_iota(jnp.int32, (blocks, LANES), 0)
    group_lane = lax.broadcasted_iota(jnp.int32, (group, LANES), 1)
    group_row = lax.broadcasted_iota(jnp.int32, (group, LANES), 0)
    half = SIDE // 2

    def pack(tile, rows, at, store):
        strip = at // SIDE
        within = at % SIDE
        zero = jnp.zeros((rows, LANES), jnp.float32)
        y_low = [zero, zero]
        y_high = [zero, zero]
        z_low = [zero, zero]
        z_high = [zero, zero]
        for x in range(SIDE):
            part = tile(x, 0), tile(x, 1)
            k, m = divmod(x, half)
            for h in range(2):
                if x == 0:
                    store(0, h, part[h])
                if x == SIDE - 1:
                    store(1, h, part[h])
                z_low[h] = jnp.where(within == x, pltpu.roll(part[h], x, 1), z_low[h])
                z_high[h] = jnp.where(
                    within == x, pltpu.roll(part[h], (x - SIDE + 1) % LANES, 1), z_high[h]
                )
            y_low[k] = jnp.where(strip == m, pltpu.roll(part[0], SIDE * m, 1), y_low[k])
            y_high[k] = jnp.where(
                strip == m, pltpu.roll(part[1], (SIDE * (m + 1)) % LANES, 1), y_high[k]
            )
        for d, packed in ((2, y_low), (3, y_high), (4, z_low), (5, z_high)):
            for h in range(2):
                store(d, h, packed[h])

    def spot(d, h):
        return slice(d * FACE + h * LANES, d * FACE + (h + 1) * LANES)

    def cells(x, h):
        return slice(x * FACE + h * LANES, x * FACE + (h + 1) * LANES)

    own_slot = nsub + sub
    own_copies[0].wait()

    def store_raw(d, h, value):
        raw[own_slot, :, spot(d, h)] = value

    pack(lambda x, h: stage_p[sub, :, cells(x, h)], blocks, lane, store_raw)
    own_slots.wait()
    slots = jnp.zeros((blocks, LANES), jnp.int32)
    for j in range(blocks):
        slots = jnp.where(row == j, slot_ref[j], slots)
    raw[own_slot, :, FACES * FACE :] = slots.astype(jnp.float32)

    def raw_copy(t, ds):
        there = lax.rem(sub + ds, nsub)
        return pltpu.make_async_remote_copy(
            src_ref=raw.at[own_slot],
            dst_ref=raw.at[(1 - t) * nsub + sub],
            send_sem=raw_send.at[(1 + t) * nsub + there],
            recv_sem=raw_recv.at[(1 - t) * nsub + sub],
            device_id=(pos + t, there),
            device_id_type=MESH,
        )

    def raw_landing(t, ds):
        there = lax.rem(sub + ds, nsub)
        slot = (1 + t) * nsub + there
        return pltpu.make_async_remote_copy(
            src_ref=raw.at[own_slot],
            dst_ref=raw.at[slot],
            send_sem=raw_send.at[slot],
            recv_sem=raw_recv.at[slot],
            device_id=(pos + t, there),
            device_id_type=MESH,
        )

    raw_partners = [(t, ds) for t in (-1, 1, 0) for ds in range(nsub) if t or ds]
    for t, ds in raw_partners:
        guarded(t, lambda t=t, ds=ds: raw_copy(t, ds).start())

    for copy in own_copies[1:]:
        copy.wait()
    for t, ds in raw_partners:
        if t == 0:
            raw_landing(t, ds).wait_recv()
    order = group_row.astype(jnp.float32)

    def chosen(t):
        return [
            (s, j, raw[(1 + t) * nsub + s, j : j + 1, FACES * FACE :] == order)
            for s in range(nsub)
            for j in range(blocks)
        ]

    picks = chosen(0)
    for k, target in enumerate((field, mf, mc)):
        stage = inputs[k][1]
        for ds in range(1, nsub):
            peer_landing(ds, k).wait_recv()
        for x in range(SIDE):
            for h in range(2):
                total = jnp.zeros((group, LANES), jnp.float32)
                for s, j, pick in picks:
                    total = jnp.where(pick, stage[s, j : j + 1, cells(x, h)], total)
                target[:, cells(x, h)] = total
    for ds in range(1, nsub):
        peer_landing(ds, len(inputs) - 1).wait_recv()

    start = (pos - 1) * group
    places = []
    for s in range(nsub):
        for b in range(blocks):
            for d in range(FACES):
                link = link_ref[s, b, d]
                place = jnp.where(link < 0, wall, jnp.clip(link - start, 0, wall - 1))
                places.append((s * blocks + b, d, place))

    def gather(window):
        for b, d, place in places:
            flipped = FLIP[d]
            ghosts[d, pl.ds(b, 1), :] = window[
                pl.ds(place, 1), flipped * FACE : (flipped + 1) * FACE
            ]

    strip = group_lane // SIDE
    within = group_lane % SIDE

    def interior(x, tile):
        part = tile(x, 0), tile(x, 1)
        up = [pltpu.roll(v, SIDE, 1) for v in part]
        down = [pltpu.roll(v, LANES - SIDE, 1) for v in part]
        found = []
        for h in range(2):
            total = jnp.where(within == 0, 0.0, pltpu.roll(part[h], 1, 1))
            total = total + jnp.where(within == SIDE - 1, 0.0, pltpu.roll(part[h], LANES - 1, 1))
            total = total + jnp.where(strip == 0, up[0] if h else 0.0, up[h])
            total = total + jnp.where(
                strip == half - 1, 0.0 if h else down[1], down[h]
            )
            if x > 0:
                total = total + tile(x - 1, h)
            if x < SIDE - 1:
                total = total + tile(x + 1, h)
            found.append(total)
        return part, found

    def outside(x, h):
        k, m = divmod(x, half)
        halves = slice(h * LANES, (h + 1) * LANES)
        total = jnp.where(within == 0, pltpu.roll(ghosts[4, :, halves], (-x) % LANES, 1), 0.0)
        total = jnp.where(
            within == SIDE - 1, pltpu.roll(ghosts[5, :, halves], SIDE - 1 - x, 1), total
        )
        source = slice(k * LANES, (k + 1) * LANES)
        if h == 0:
            side = pltpu.roll(ghosts[2, :, source], (-SIDE * m) % LANES, 1)
            total = total + jnp.where(strip == 0, side, 0.0)
        else:
            side = pltpu.roll(ghosts[3, :, source], SIDE * (half - 1 - m), 1)
            total = total + jnp.where(strip == half - 1, side, 0.0)
        if x == 0:
            total = total + ghosts[0, :, halves]
        if x == SIDE - 1:
            total = total + ghosts[1, :, halves]
        return total

    def value(x, h):
        return field[:, cells(x, h)]

    def prepare():
        for x in range(SIDE):
            part, found = interior(x, value)
            for h in range(2):
                here = cells(x, h)
                base[:, here] = (1.0 - relaxation) * part[h] + inv[:, here] * (
                    mf[:, here] + found[h]
                )

    for x in range(SIDE):
        for h in range(2):
            inv[:, cells(x, h)] = relaxation / (6.0 + mc[:, cells(x, h)])
    prepare()

    for t in (0, -1, 1):
        if t:
            for ds in range(nsub):
                guarded(t, lambda t=t, ds=ds: raw_landing(t, ds).wait_recv())
        picks = chosen(t)
        for d in range(FACES):
            for h in range(2):
                total = jnp.zeros((group, LANES), jnp.float32)
                for s, j, pick in picks:
                    total = jnp.where(
                        pick, raw[(1 + t) * nsub + s, j : j + 1, spot(d, h)], total
                    )
                first[(1 + t) * group : (2 + t) * group, spot(d, h)] = total
    gather(first)

    def face_copy(window, step, t):
        return pltpu.make_async_remote_copy(
            src_ref=window.at[pl.ds(group, group)],
            dst_ref=window.at[pl.ds((1 - t) * group, group)],
            send_sem=face_send.at[step, 1 + t],
            recv_sem=face_recv.at[step, 1 - t],
            device_id=(pos + t, sub),
            device_id_type=MESH,
        )

    def face_landing(window, step, t):
        return pltpu.make_async_remote_copy(
            src_ref=window.at[pl.ds(group, group)],
            dst_ref=window.at[pl.ds((1 + t) * group, group)],
            send_sem=face_send.at[step, 1 + t],
            recv_sem=face_recv.at[step, 1 + t],
            device_id=(pos + t, sub),
            device_id_type=MESH,
        )

    windows = (window_a, window_b)
    for step in range(PRE_SWEEPS):
        window = windows[step]

        def store_faces(d, h, packed):
            window[group : 2 * group, spot(d, h)] = packed

        def swept(x, h):
            here = cells(x, h)
            fresh = base[:, here] + inv[:, here] * outside(x, h)
            field[:, here] = fresh
            return fresh

        pack(swept, group, group_lane, store_faces)
        for t in near:
            guarded(t, lambda t=t: face_copy(window, step, t).start())
        prepare()
        for t in near:
            guarded(t, lambda t=t: face_landing(window, step, t).wait_recv())
        gather(window)

    left = jnp.zeros((group, LANES), jnp.float32)
    added = jnp.zeros((group, LANES), jnp.float32)
    for x in range(SIDE):
        for h in range(2):
            here = cells(x, h)
            fresh = base[:, here] + inv[:, here] * outside(x, h)
            diagonal = 6.0 + mc[:, here]
            left = left + (fresh - field[:, here]) * diagonal
            added = added + mc[:, here]
            base[:, here] = fresh
    size = SIDE * FACE
    block_residual = jnp.sum(left, axis=1, keepdims=True) / (size * relaxation)
    block_diag = 6.0 + jnp.sum(added, axis=1, keepdims=True) / size

    links = jnp.zeros((group, LANES), jnp.int32)
    for s in range(nsub):
        for b in range(blocks):
            for d in range(FACES):
                links = jnp.where(
                    (group_row == s * blocks + b) & (group_lane == d), link_ref[s, b, d], links
                )
    message = links.astype(jnp.float32)
    message = jnp.where(group_lane == FACES, block_residual, message)
    message = jnp.where(group_lane == FACES + 1, block_diag, message)
    coarse[reach] = message

    def coarse_copy(t):
        return pltpu.make_async_remote_copy(
            src_ref=coarse.at[reach],
            dst_ref=coarse.at[reach - t],
            send_sem=coarse_send.at[reach + t],
            recv_sem=coarse_recv.at[reach - t],
            device_id=(pos + t, sub),
            device_id_type=MESH,
        )

    def coarse_landing(t):
        return pltpu.make_async_remote_copy(
            src_ref=coarse.at[reach],
            dst_ref=coarse.at[reach + t],
            send_sem=coarse_send.at[reach + t],
            recv_sem=coarse_recv.at[reach + t],
            device_id=(pos + t, sub),
            device_id_type=MESH,
        )

    for t in far:
        guarded(t, lambda t=t: coarse_copy(t).start())
    for t in far:
        guarded(t, lambda t=t: coarse_landing(t).wait_recv())

    shown = coarse[...]
    shape = (2 * reach + 1, group, LANES)
    column = lax.broadcasted_iota(jnp.int32, shape, 2)
    index = lax.broadcasted_iota(jnp.int32, shape, 0) * group + lax.broadcasted_iota(
        jnp.int32, shape, 1
    )
    origin = ((pos - reach) * group).astype(jnp.float32)
    numbered = column.astype(jnp.float32) + origin
    linked = jnp.zeros(shape, jnp.float32)
    for d in range(FACES):
        link = shown[:, :, d : d + 1]
        linked = linked + ((link == numbered) & (link >= 0.0)).astype(jnp.float32)
    residuals = shown[:, :, FACES : FACES + 1]
    diags = shown[:, :, FACES + 1 : FACES + 2]
    diags = jnp.where(diags > 0.0, diags, 1.0)

    def turned(values):
        spread = jnp.where(index == column, values, 0.0)
        return jnp.sum(jnp.sum(spread, axis=0), axis=0, keepdims=True)

    scaled = relaxation / diags
    driven = scaled * residuals
    errors = driven
    for step in range(1, COARSE_SWEEPS):
        around = jnp.sum(linked * turned(errors)[None], axis=2, keepdims=True)
        errors = (1.0 - relaxation) * errors + driven + scaled * around
    known = turned(errors)

    own_numbered = group_lane.astype(jnp.float32) + origin
    own_error = jnp.sum(
        jnp.where(group_lane == reach * group + group_row, known, 0.0), axis=1, keepdims=True
    )
    jumps = []
    for d in range(FACES):
        link = message[:, d : d + 1]
        hit = (link == own_numbered) & (link >= 0.0)
        jumps.append(jnp.sum(jnp.where(hit, known, 0.0), axis=1, keepdims=True) - own_error)
    plane = jnp.zeros((group, LANES), jnp.float32) + 6.0 * own_error
    plane = plane + jnp.where(within == 0, jumps[4], 0.0)
    plane = plane + jnp.where(within == SIDE - 1, jumps[5], 0.0)
    planes = (
        plane + jnp.where(strip == 0, jumps[2], 0.0),
        plane + jnp.where(strip == half - 1, jumps[3], 0.0),
    )
    kept = (1.0 - relaxation) * own_error + jnp.zeros((group, LANES), jnp.float32)
    for x in range(SIDE):
        for h in range(2):
            here = cells(x, h)
            extra = planes[h]
            if x == 0:
                extra = extra + jumps[0]
            if x == SIDE - 1:
                extra = extra + jumps[1]
            whole = base[:, here] + kept + inv[:, here] * extra
            result = whole[:blocks]
            for s in range(1, nsub):
                result = jnp.where(sub == s, whole[s * blocks : (s + 1) * blocks], result)
            out_ref[:, here] = result

    for k in range(len(inputs)):
        for ds in range(1, nsub):
            peer_copy(ds, k).wait_send()
    for t, ds in raw_partners:
        guarded(t, lambda t=t, ds=ds: raw_copy(t, ds).wait_send())
    for step in range(PRE_SWEEPS):
        for t in near:
            guarded(t, lambda t=t: face_copy(windows[step], step, t).wait_send())
    for t in far:
        guarded(t, lambda t=t: coarse_copy(t).wait_send())


def on_device(pressure, source_term, coefficient, new_slot, face_links):
    blocks, size = pressure.shape
    count = lax.axis_size("curve")
    nsub = lax.axis_size("sub")
    group = nsub * blocks
    others = max(1, nsub - 1)
    stage = pltpu.VMEM((nsub, blocks, size), jnp.float32)
    field = pltpu.VMEM((group, size), jnp.float32)
    window = pltpu.VMEM((3 * group + 8, FACES * FACE), jnp.float32)
    dma = pltpu.SemaphoreType.DMA
    hbm = pl.BlockSpec(memory_space=pltpu.HBM)
    return pl.pallas_call(
        functools.partial(kernel, count, nsub, blocks),
        out_shape=jax.ShapeDtypeStruct((blocks, size), jnp.float32),
        in_specs=[hbm] * 5,
        out_specs=pl.BlockSpec(memory_space=pltpu.VMEM),
        scratch_shapes=[
            pltpu.SMEM((blocks,), jnp.int32),
            pltpu.SMEM((nsub, blocks, FACES), jnp.int32),
            stage,
            stage,
            stage,
            pltpu.VMEM((3 * nsub, blocks, FACES * FACE + LANES), jnp.float32),
            window,
            window,
            window,
            pltpu.VMEM((FACES, group, FACE), jnp.float32),
            field,
            field,
            field,
            field,
            field,
            pltpu.VMEM((2 * COARSE_SWEEPS + 1, group, LANES), jnp.float32),
            dma((5,)),
            dma((3 * nsub,)),
            dma((3 * nsub,)),
            dma((PRE_SWEEPS, 3)),
            dma((PRE_SWEEPS, 3)),
            dma((4, others)),
            dma((4, others)),
            dma((2 * COARSE_SWEEPS + 1,)),
            dma((2 * COARSE_SWEEPS + 1,)),
        ],
        compiler_params=pltpu.CompilerParams(
            collective_id=0, has_side_effects=True, vmem_limit_bytes=63 * 1024 * 1024
        ),
    )(new_slot, face_links, pressure, source_term, coefficient)


def solution(mesh):
    placed = (
        P(("curve", "sub"), None),
        P(("curve", "sub"), None),
        P(("curve", "sub"), None),
        P(("curve", "sub")),
        P(("curve", "sub"), None),
    )
    return jax.shard_map(
        on_device, mesh=mesh, in_specs=placed, out_specs=P(("curve", "sub"), None), check_vma=False
    )
```

```python
import functools

import jax
import jax.numpy as jnp
from jax import lax
from jax.experimental import pallas as pl
from jax.experimental.pallas import tpu as pltpu
from jax.sharding import PartitionSpec as P

PRE_SWEEPS = 2
COARSE_SWEEPS = 4
SIDE = 16
GREETED = 3
FACE = SIDE * SIDE
FACES = 6
LANES = 128
FLIP = (1, 0, 3, 2, 5, 4)

relaxation = 0.8
MESH = pl.DeviceIdType.MESH


def kernel(
    count,
    nsub,
    blocks,
    slot_hbm,
    link_hbm,
    p_hbm,
    f_hbm,
    c_hbm,
    out_ref,
    slot_ref,
    link_ref,
    stage_p,
    stage_f,
    stage_c,
    raw,
    first,
    window_a,
    window_b,
    ghosts,
    mf,
    mc,
    inv,
    field,
    base,
    coarse,
    local_sem,
    raw_send,
    raw_recv,
    face_send,
    face_recv,
    peer_send,
    peer_recv,
    coarse_send,
    coarse_recv,
):
    pos = lax.axis_index("curve")
    sub = lax.axis_index("sub")
    group = nsub * blocks
    reach = COARSE_SWEEPS + 1
    greeted = GREETED
    wall = 3 * group
    near = (-1, 1)
    far = [t for t in range(-reach, reach + 1) if t]

    def exists(t):
        return (pos + t >= 0) & (pos + t < count)

    def guarded(t, action):
        if t == 0:
            action()
        else:
            pl.when(exists(t))(action)

    barrier = pltpu.get_barrier_semaphore()
    expected = 0
    for t in sorted(range(-greeted, greeted + 1), key=abs):
        for ds in range(nsub if abs(t) <= 1 else 1):
            if t or ds:

                def greet(t=t, ds=ds):
                    pl.semaphore_signal(
                        barrier,
                        inc=1,
                        device_id=(pos + t, lax.rem(sub + ds, nsub)),
                        device_id_type=MESH,
                    )

                guarded(t, greet)
                expected = expected + (exists(t).astype(jnp.int32) if t else 1)

    inputs = (
        (p_hbm, stage_p),
        (f_hbm, stage_f),
        (c_hbm, stage_c),
        (link_hbm, link_ref),
    )
    own_copies = [
        pltpu.make_async_copy(source, stage.at[sub], local_sem.at[k])
        for k, (source, stage) in enumerate(inputs)
    ]
    own_slots = pltpu.make_async_copy(slot_hbm, slot_ref, local_sem.at[len(inputs)])
    own_copies[0].start()
    own_slots.start()
    for copy in own_copies[1:]:
        copy.start()

    def clear(window, rows):
        window[rows] = jnp.zeros((rows.stop - rows.start,) + window.shape[1:], jnp.float32)

    for window in (first, window_a, window_b):
        clear(window, slice(wall, wall + 8))
    for t in near:

        @pl.when(jnp.logical_not(exists(t)))
        def _(t=t):
            for window in (window_a, window_b):
                clear(window, slice((t + 1) * group, (t + 2) * group))
            clear(raw, slice((t + 1) * nsub, (t + 2) * nsub))

    for t in far:

        @pl.when(jnp.logical_not(exists(t)))
        def _(t=t):
            clear(coarse, slice(t + reach, t + reach + 1))

    def peer_copy(ds, k):
        source, stage = inputs[k]
        return pltpu.make_async_remote_copy(
            src_ref=source,
            dst_ref=stage.at[sub],
            send_sem=peer_send.at[k, ds - 1],
            recv_sem=peer_recv.at[k, nsub - ds - 1],
            device_id=(pos, lax.rem(sub + ds, nsub)),
            device_id_type=MESH,
        )

    def peer_landing(ds, k):
        source, stage = inputs[k]
        there = lax.rem(sub + ds, nsub)
        return pltpu.make_async_remote_copy(
            src_ref=source,
            dst_ref=stage.at[there],
            send_sem=peer_send.at[k, ds - 1],
            recv_sem=peer_recv.at[k, ds - 1],
            device_id=(pos, there),
            device_id_type=MESH,
        )

    lane = lax.broadcasted_iota(jnp.int32, (blocks, LANES), 1)
    row = lax.broadcasted_iota(jnp.int32, (blocks, LANES), 0)
    group_lane = lax.broadcasted_iota(jnp.int32, (group, LANES), 1)
    group_row = lax.broadcasted_iota(jnp.int32, (group, LANES), 0)
    half = SIDE // 2

    def pack(tile, rows, at, store):
        strip = at // SIDE
        within = at % SIDE
        zero = jnp.zeros((rows, LANES), jnp.float32)
        y_low = [zero, zero]
        y_high = [zero, zero]
        z_low = [zero, zero]
        z_high = [zero, zero]
        for x in range(SIDE):
            part = tile(x, 0), tile(x, 1)
            k, m = divmod(x, half)
            for h in range(2):
                if x == 0:
                    store(0, h, part[h])
                if x == SIDE - 1:
                    store(1, h, part[h])
                z_low[h] = jnp.where(within == x, pltpu.roll(part[h], x, 1), z_low[h])
                z_high[h] = jnp.where(
                    within == x, pltpu.roll(part[h], (x - SIDE + 1) % LANES, 1), z_high[h]
                )
            y_low[k] = jnp.where(strip == m, pltpu.roll(part[0], SIDE * m, 1), y_low[k])
            y_high[k] = jnp.where(
                strip == m, pltpu.roll(part[1], (SIDE * (m + 1)) % LANES, 1), y_high[k]
            )
        for d, packed in ((2, y_low), (3, y_high), (4, z_low), (5, z_high)):
            for h in range(2):
                store(d, h, packed[h])

    def spot(d, h):
        return slice(d * FACE + h * LANES, d * FACE + (h + 1) * LANES)

    def cells(x, h):
        return slice(x * FACE + h * LANES, x * FACE + (h + 1) * LANES)

    own_slot = nsub + sub
    own_copies[0].wait()

    def store_raw(d, h, value):
        raw[own_slot, :, spot(d, h)] = value

    pack(lambda x, h: stage_p[sub, :, cells(x, h)], blocks, lane, store_raw)
    own_slots.wait()
    slots = jnp.zeros((blocks, LANES), jnp.int32)
    for j in range(blocks):
        slots = jnp.where(row == j, slot_ref[j], slots)
    raw[own_slot, :, FACES * FACE :] = slots.astype(jnp.float32)

    def raw_copy(t, ds):
        there = lax.rem(sub + ds, nsub)
        return pltpu.make_async_remote_copy(
            src_ref=raw.at[own_slot],
            dst_ref=raw.at[(1 - t) * nsub + sub],
            send_sem=raw_send.at[(1 + t) * nsub + there],
            recv_sem=raw_recv.at[(1 - t) * nsub + sub],
            device_id=(pos + t, there),
            device_id_type=MESH,
        )

    def raw_landing(t, ds):
        there = lax.rem(sub + ds, nsub)
        slot = (1 + t) * nsub + there
        return pltpu.make_async_remote_copy(
            src_ref=raw.at[own_slot],
            dst_ref=raw.at[slot],
            send_sem=raw_send.at[slot],
            recv_sem=raw_recv.at[slot],
            device_id=(pos + t, there),
            device_id_type=MESH,
        )

    raw_partners = [(t, ds) for t in (-1, 1, 0) for ds in range(nsub) if t or ds]
    pl.semaphore_wait(barrier, expected)
    for t, ds in raw_partners:
        guarded(t, lambda t=t, ds=ds: raw_copy(t, ds).start())
    for k in range(len(inputs)):
        for ds in range(1, nsub):
            peer_copy(ds, k).start()

    for copy in own_copies[1:]:
        copy.wait()
    for t, ds in raw_partners:
        if t == 0:
            raw_landing(t, ds).wait_recv()
    order = group_row.astype(jnp.float32)

    def chosen(t):
        return [
            (s, j, raw[(1 + t) * nsub + s, j : j + 1, FACES * FACE :] == order)
            for s in range(nsub)
            for j in range(blocks)
        ]

    picks = chosen(0)
    for k, target in enumerate((field, mf, mc)):
        stage = inputs[k][1]
        for ds in range(1, nsub):
            peer_landing(ds, k).wait_recv()
        for x in range(SIDE):
            for h in range(2):
                total = jnp.zeros((group, LANES), jnp.float32)
                for s, j, pick in picks:
                    total = jnp.where(pick, stage[s, j : j + 1, cells(x, h)], total)
                target[:, cells(x, h)] = total
    for ds in range(1, nsub):
        peer_landing(ds, len(inputs) - 1).wait_recv()

    start = (pos - 1) * group
    places = []
    for s in range(nsub):
        for b in range(blocks):
            for d in range(FACES):
                link = link_ref[s, b, d]
                place = jnp.where(link < 0, wall, jnp.clip(link - start, 0, wall - 1))
                places.append((s * blocks + b, d, place))

    def gather(window):
        for b, d, place in places:
            flipped = FLIP[d]
            ghosts[d, pl.ds(b, 1), :] = window[
                pl.ds(place, 1), flipped * FACE : (flipped + 1) * FACE
            ]

    strip = group_lane // SIDE
    within = group_lane % SIDE

    def interior(x, tile):
        part = tile(x, 0), tile(x, 1)
        up = [pltpu.roll(v, SIDE, 1) for v in part]
        down = [pltpu.roll(v, LANES - SIDE, 1) for v in part]
        found = []
        for h in range(2):
            total = jnp.where(within == 0, 0.0, pltpu.roll(part[h], 1, 1))
            total = total + jnp.where(within == SIDE - 1, 0.0, pltpu.roll(part[h], LANES - 1, 1))
            total = total + jnp.where(strip == 0, up[0] if h else 0.0, up[h])
            total = total + jnp.where(
                strip == half - 1, 0.0 if h else down[1], down[h]
            )
            if x > 0:
                total = total + tile(x - 1, h)
            if x < SIDE - 1:
                total = total + tile(x + 1, h)
            found.append(total)
        return part, found

    def outside(x, h):
        k, m = divmod(x, half)
        halves = slice(h * LANES, (h + 1) * LANES)
        total = jnp.where(within == 0, pltpu.roll(ghosts[4, :, halves], (-x) % LANES, 1), 0.0)
        total = jnp.where(
            within == SIDE - 1, pltpu.roll(ghosts[5, :, halves], SIDE - 1 - x, 1), total
        )
        source = slice(k * LANES, (k + 1) * LANES)
        if h == 0:
            side = pltpu.roll(ghosts[2, :, source], (-SIDE * m) % LANES, 1)
            total = total + jnp.where(strip == 0, side, 0.0)
        else:
            side = pltpu.roll(ghosts[3, :, source], SIDE * (half - 1 - m), 1)
            total = total + jnp.where(strip == half - 1, side, 0.0)
        if x == 0:
            total = total + ghosts[0, :, halves]
        if x == SIDE - 1:
            total = total + ghosts[1, :, halves]
        return total

    def value(x, h):
        return field[:, cells(x, h)]

    def prepare():
        for x in range(SIDE):
            part, found = interior(x, value)
            for h in range(2):
                here = cells(x, h)
                base[:, here] = (1.0 - relaxation) * part[h] + inv[:, here] * (
                    mf[:, here] + found[h]
                )

    for x in range(SIDE):
        for h in range(2):
            inv[:, cells(x, h)] = relaxation / (6.0 + mc[:, cells(x, h)])
    prepare()

    size = SIDE * FACE
    links = jnp.zeros((group, LANES), jnp.int32)
    for s in range(nsub):
        for b in range(blocks):
            for d in range(FACES):
                links = jnp.where(
                    (group_row == s * blocks + b) & (group_lane == d), link_ref[s, b, d], links
                )
    links = links.astype(jnp.float32)
    added = jnp.zeros((group, LANES), jnp.float32)
    for x in range(SIDE):
        for h in range(2):
            added = added + mc[:, cells(x, h)]
    block_diag = 6.0 + jnp.sum(added, axis=1, keepdims=True) / size
    message = jnp.where(group_lane == FACES + 1, block_diag, links)

    for t in (0, -1, 1):
        if t:
            for ds in range(nsub):
                guarded(t, lambda t=t, ds=ds: raw_landing(t, ds).wait_recv())
        picks = chosen(t)
        for d in range(FACES):
            for h in range(2):
                total = jnp.zeros((group, LANES), jnp.float32)
                for s, j, pick in picks:
                    total = jnp.where(
                        pick, raw[(1 + t) * nsub + s, j : j + 1, spot(d, h)], total
                    )
                first[(1 + t) * group : (2 + t) * group, spot(d, h)] = total
    gather(first)

    def face_copy(window, step, t):
        return pltpu.make_async_remote_copy(
            src_ref=window.at[pl.ds(group, group)],
            dst_ref=window.at[pl.ds((1 - t) * group, group)],
            send_sem=face_send.at[step, 1 + t],
            recv_sem=face_recv.at[step, 1 - t],
            device_id=(pos + t, sub),
            device_id_type=MESH,
        )

    def face_landing(window, step, t):
        return pltpu.make_async_remote_copy(
            src_ref=window.at[pl.ds(group, group)],
            dst_ref=window.at[pl.ds((1 + t) * group, group)],
            send_sem=face_send.at[step, 1 + t],
            recv_sem=face_recv.at[step, 1 + t],
            device_id=(pos + t, sub),
            device_id_type=MESH,
        )

    def coarse_copy(t):
        return pltpu.make_async_remote_copy(
            src_ref=coarse.at[reach],
            dst_ref=coarse.at[reach - t],
            send_sem=coarse_send.at[reach + t],
            recv_sem=coarse_recv.at[reach - t],
            device_id=(pos + t, sub),
            device_id_type=MESH,
        )

    def coarse_landing(t):
        return pltpu.make_async_remote_copy(
            src_ref=coarse.at[reach],
            dst_ref=coarse.at[reach + t],
            send_sem=coarse_send.at[reach + t],
            recv_sem=coarse_recv.at[reach + t],
            device_id=(pos + t, sub),
            device_id_type=MESH,
        )

    def send_coarse(window):
        own = slice(group, 2 * group)
        left = jnp.zeros((group, LANES), jnp.float32)
        for x in range(SIDE):
            for h in range(2):
                here = cells(x, h)
                left = left + (mf[:, here] - mc[:, here] * field[:, here])
        block = group_lane % group == group_row
        lanes_row = lax.broadcasted_iota(jnp.int32, (8, LANES), 0)
        sums = jnp.zeros((8, LANES), jnp.float32)
        for d in range(FACES):
            both = window[own, spot(d, 0)] + window[own, spot(d, 1)]
            left = left - both
            total = jnp.sum(both, axis=1, keepdims=True) / size
            line = jnp.sum(jnp.where(block, total, 0.0), axis=0, keepdims=True)
            sums = jnp.where(lanes_row == d, line, sums)
        own_part = jnp.sum(left, axis=1, keepdims=True) / size
        coarse[reach, 0:group, :] = jnp.where(group_lane == FACES, own_part, message)
        coarse[reach, group : group + 8, :] = sums
        for t in sorted(far, key=lambda t: -abs(t)):
            guarded(t, lambda t=t: coarse_copy(t).start())

    windows = (window_a, window_b)
    for step in range(PRE_SWEEPS):
        window = windows[step]

        def store_faces(d, h, packed):
            window[group : 2 * group, spot(d, h)] = packed

        def swept(x, h):
            here = cells(x, h)
            fresh = base[:, here] + inv[:, here] * outside(x, h)
            field[:, here] = fresh
            return fresh

        pack(swept, group, group_lane, store_faces)
        if step == PRE_SWEEPS - 1:
            send_coarse(window)
        for t in near:
            guarded(t, lambda t=t: face_copy(window, step, t).start())
        prepare()
        if step == PRE_SWEEPS - 1:
            break
        for t in near:
            guarded(t, lambda t=t: face_landing(window, step, t).wait_recv())
        gather(window)

    for t in far:
        guarded(t, lambda t=t: coarse_landing(t).wait_recv())

    shown = coarse[:, 0:group, :]
    shape = (2 * reach + 1, group, LANES)
    column = lax.broadcasted_iota(jnp.int32, shape, 2)
    index = lax.broadcasted_iota(jnp.int32, shape, 0) * group + lax.broadcasted_iota(
        jnp.int32, shape, 1
    )
    origin = ((pos - reach) * group).astype(jnp.float32)
    numbered = column.astype(jnp.float32) + origin
    face_sums = jnp.zeros((8, LANES), jnp.float32)
    narrow = lax.broadcasted_iota(jnp.int32, (8, LANES), 1)
    for k in range(2 * reach + 1):
        face_sums = jnp.where(narrow // group == k, coarse[k, group : group + 8, :], face_sums)
    linked = jnp.zeros(shape, jnp.float32)
    entering = jnp.zeros(shape, jnp.float32)
    for d in range(FACES):
        link = shown[:, :, d : d + 1]
        hit = (link == numbered) & (link >= 0.0)
        linked = linked + hit.astype(jnp.float32)
        flipped = FLIP[d]
        entering = entering + jnp.where(hit, face_sums[flipped : flipped + 1][None], 0.0)
    residuals = shown[:, :, FACES : FACES + 1] + jnp.sum(entering, axis=2, keepdims=True)
    diags = shown[:, :, FACES + 1 : FACES + 2]
    diags = jnp.where(diags > 0.0, diags, 1.0)

    def turned(values):
        spread = jnp.where(index == column, values, 0.0)
        return jnp.sum(jnp.sum(spread, axis=0), axis=0, keepdims=True)

    scaled = relaxation / diags
    driven = scaled * residuals
    errors = driven
    for step in range(1, COARSE_SWEEPS):
        around = jnp.sum(linked * turned(errors)[None], axis=2, keepdims=True)
        errors = (1.0 - relaxation) * errors + driven + scaled * around
    known = turned(errors)

    own_numbered = group_lane.astype(jnp.float32) + origin
    own_error = jnp.sum(
        jnp.where(group_lane == reach * group + group_row, known, 0.0), axis=1, keepdims=True
    )
    jumps = []
    for d in range(FACES):
        link = message[:, d : d + 1]
        hit = (link == own_numbered) & (link >= 0.0)
        jumps.append(jnp.sum(jnp.where(hit, known, 0.0), axis=1, keepdims=True) - own_error)
    plane = jnp.zeros((group, LANES), jnp.float32) + 6.0 * own_error
    plane = plane + jnp.where(within == 0, jumps[4], 0.0)
    plane = plane + jnp.where(within == SIDE - 1, jumps[5], 0.0)
    planes = (
        plane + jnp.where(strip == 0, jumps[2], 0.0),
        plane + jnp.where(strip == half - 1, jumps[3], 0.0),
    )
    kept = (1.0 - relaxation) * own_error + jnp.zeros((group, LANES), jnp.float32)
    last = PRE_SWEEPS - 1
    for t in near:
        guarded(t, lambda t=t: face_landing(windows[last], last, t).wait_recv())
    gather(windows[last])
    for x in range(SIDE):
        for h in range(2):
            here = cells(x, h)
            extra = planes[h] + outside(x, h)
            if x == 0:
                extra = extra + jumps[0]
            if x == SIDE - 1:
                extra = extra + jumps[1]
            whole = base[:, here] + kept + inv[:, here] * extra
            result = whole[:blocks]
            for s in range(1, nsub):
                result = jnp.where(sub == s, whole[s * blocks : (s + 1) * blocks], result)
            out_ref[:, here] = result

    for k in range(len(inputs)):
        for ds in range(1, nsub):
            peer_copy(ds, k).wait_send()
    for t, ds in raw_partners:
        guarded(t, lambda t=t, ds=ds: raw_copy(t, ds).wait_send())
    for step in range(PRE_SWEEPS):
        for t in near:
            guarded(t, lambda t=t: face_copy(windows[step], step, t).wait_send())
    for t in far:
        guarded(t, lambda t=t: coarse_copy(t).wait_send())


def on_device(pressure, source_term, coefficient, new_slot, face_links):
    blocks, size = pressure.shape
    count = lax.axis_size("curve")
    nsub = lax.axis_size("sub")
    group = nsub * blocks
    others = max(1, nsub - 1)
    stage = pltpu.VMEM((nsub, blocks, size), jnp.float32)
    field = pltpu.VMEM((group, size), jnp.float32)
    window = pltpu.VMEM((3 * group + 8, FACES * FACE), jnp.float32)
    dma = pltpu.SemaphoreType.DMA
    hbm = pl.BlockSpec(memory_space=pltpu.HBM)
    return pl.pallas_call(
        functools.partial(kernel, count, nsub, blocks),
        out_shape=jax.ShapeDtypeStruct((blocks, size), jnp.float32),
        in_specs=[hbm] * 5,
        out_specs=pl.BlockSpec(memory_space=pltpu.VMEM),
        scratch_shapes=[
            pltpu.SMEM((blocks,), jnp.int32),
            pltpu.SMEM((nsub, blocks, FACES), jnp.int32),
            stage,
            stage,
            stage,
            pltpu.VMEM((3 * nsub, blocks, FACES * FACE + LANES), jnp.float32),
            window,
            window,
            window,
            pltpu.VMEM((FACES, group, FACE), jnp.float32),
            field,
            field,
            field,
            field,
            field,
            pltpu.VMEM((2 * COARSE_SWEEPS + 3, group + 8, LANES), jnp.float32),
            dma((5,)),
            dma((3 * nsub,)),
            dma((3 * nsub,)),
            dma((PRE_SWEEPS, 3)),
            dma((PRE_SWEEPS, 3)),
            dma((4, others)),
            dma((4, others)),
            dma((2 * COARSE_SWEEPS + 3,)),
            dma((2 * COARSE_SWEEPS + 3,)),
        ],
        compiler_params=pltpu.CompilerParams(
            collective_id=0, has_side_effects=True, vmem_limit_bytes=63 * 1024 * 1024
        ),
    )(new_slot, face_links, pressure, source_term, coefficient)


def solution(mesh):
    placed = (
        P(("curve", "sub"), None),
        P(("curve", "sub"), None),
        P(("curve", "sub"), None),
        P(("curve", "sub")),
        P(("curve", "sub"), None),
    )
    return jax.shard_map(
        on_device, mesh=mesh, in_specs=placed, out_specs=P(("curve", "sub"), None), check_vma=False
    )
```

```python
import functools

import jax
import jax.numpy as jnp
from jax import lax
from jax.experimental import pallas as pl
from jax.experimental.pallas import tpu as pltpu
from jax.sharding import PartitionSpec as P

PRE_SWEEPS = 2
COARSE_SWEEPS = 4
SIDE = 16
GREETED = 3
FACE = SIDE * SIDE
FACES = 6
LANES = 128
FLIP = (1, 0, 3, 2, 5, 4)

relaxation = 0.8
MESH = pl.DeviceIdType.MESH


def kernel(
    count,
    nsub,
    blocks,
    slot_hbm,
    link_hbm,
    p_hbm,
    f_hbm,
    c_hbm,
    out_ref,
    slot_ref,
    link_ref,
    near_links,
    stage_p,
    stage_f,
    stage_c,
    raw,
    first,
    window,
    last_faces,
    parts_out,
    parts_in,
    ghosts,
    own_ghosts,
    mf,
    mc,
    inv,
    field,
    base,
    coarse,
    local_sem,
    raw_send,
    raw_recv,
    face_send,
    face_recv,
    peer_send,
    peer_recv,
    coarse_send,
    coarse_recv,
    link_send,
    link_recv,
):
    pos = lax.axis_index("curve")
    sub = lax.axis_index("sub")
    group = nsub * blocks
    reach = COARSE_SWEEPS + 1
    greeted = GREETED
    wall = 3 * group
    near = (-1, 1)
    far = [t for t in range(-reach, reach + 1) if t]

    def exists(t):
        return (pos + t >= 0) & (pos + t < count)

    def guarded(t, action):
        if t == 0:
            action()
        else:
            pl.when(exists(t))(action)

    barrier = pltpu.get_barrier_semaphore()
    expected = 0
    for t in sorted(range(-greeted, greeted + 1), key=abs):
        for ds in range(nsub if abs(t) <= 1 else 1):
            if t or ds:

                def greet(t=t, ds=ds):
                    pl.semaphore_signal(
                        barrier,
                        inc=1,
                        device_id=(pos + t, lax.rem(sub + ds, nsub)),
                        device_id_type=MESH,
                    )

                guarded(t, greet)
                expected = expected + (exists(t).astype(jnp.int32) if t else 1)

    inputs = (
        (p_hbm, stage_p),
        (f_hbm, stage_f),
        (c_hbm, stage_c),
        (link_hbm, link_ref),
    )
    own_copies = [
        pltpu.make_async_copy(source, stage.at[sub], local_sem.at[k])
        for k, (source, stage) in enumerate(inputs)
    ]
    own_slots = pltpu.make_async_copy(slot_hbm, slot_ref, local_sem.at[len(inputs)])
    own_copies[0].start()
    own_slots.start()
    for copy in own_copies[1:]:
        copy.start()

    def clear(window, rows):
        window[rows] = jnp.zeros((rows.stop - rows.start,) + window.shape[1:], jnp.float32)

    clear(first, slice(wall, wall + 8))
    clear(window, slice(wall, wall + 8))
    clear(last_faces, slice(group, group + 8))
    for t in near:

        @pl.when(jnp.logical_not(exists(t)))
        def _(t=t):
            clear(window, slice((t + 1) * group, (t + 2) * group))
            clear(parts_in, slice((t + 1) // 2, (t + 1) // 2 + 1))
            clear(raw, slice((t + 1) * nsub, (t + 2) * nsub))

    for t in far:

        @pl.when(jnp.logical_not(exists(t)))
        def _(t=t):
            clear(coarse, slice(t + reach, t + reach + 1))

    def peer_copy(ds, k):
        source, stage = inputs[k]
        return pltpu.make_async_remote_copy(
            src_ref=source,
            dst_ref=stage.at[sub],
            send_sem=peer_send.at[k, ds - 1],
            recv_sem=peer_recv.at[k, nsub - ds - 1],
            device_id=(pos, lax.rem(sub + ds, nsub)),
            device_id_type=MESH,
        )

    def peer_landing(ds, k):
        source, stage = inputs[k]
        there = lax.rem(sub + ds, nsub)
        return pltpu.make_async_remote_copy(
            src_ref=source,
            dst_ref=stage.at[there],
            send_sem=peer_send.at[k, ds - 1],
            recv_sem=peer_recv.at[k, ds - 1],
            device_id=(pos, there),
            device_id_type=MESH,
        )

    lane = lax.broadcasted_iota(jnp.int32, (blocks, LANES), 1)
    row = lax.broadcasted_iota(jnp.int32, (blocks, LANES), 0)
    group_lane = lax.broadcasted_iota(jnp.int32, (group, LANES), 1)
    group_row = lax.broadcasted_iota(jnp.int32, (group, LANES), 0)
    half = SIDE // 2

    def pack(tile, rows, at, store):
        strip = at // SIDE
        within = at % SIDE
        zero = jnp.zeros((rows, LANES), jnp.float32)
        y_low = [zero, zero]
        y_high = [zero, zero]
        z_low = [zero, zero]
        z_high = [zero, zero]
        for x in range(SIDE):
            part = tile(x, 0), tile(x, 1)
            k, m = divmod(x, half)
            for h in range(2):
                if x == 0:
                    store(0, h, part[h])
                if x == SIDE - 1:
                    store(1, h, part[h])
                z_low[h] = jnp.where(within == x, pltpu.roll(part[h], x, 1), z_low[h])
                z_high[h] = jnp.where(
                    within == x, pltpu.roll(part[h], (x - SIDE + 1) % LANES, 1), z_high[h]
                )
            y_low[k] = jnp.where(strip == m, pltpu.roll(part[0], SIDE * m, 1), y_low[k])
            y_high[k] = jnp.where(
                strip == m, pltpu.roll(part[1], (SIDE * (m + 1)) % LANES, 1), y_high[k]
            )
        for d, packed in ((2, y_low), (3, y_high), (4, z_low), (5, z_high)):
            for h in range(2):
                store(d, h, packed[h])

    def spot(d, h):
        return slice(d * FACE + h * LANES, d * FACE + (h + 1) * LANES)

    def cells(x, h):
        return slice(x * FACE + h * LANES, x * FACE + (h + 1) * LANES)

    own_slot = nsub + sub
    own_copies[0].wait()

    def store_raw(d, h, value):
        raw[own_slot, :, spot(d, h)] = value

    pack(lambda x, h: stage_p[sub, :, cells(x, h)], blocks, lane, store_raw)
    own_slots.wait()
    slots = jnp.zeros((blocks, LANES), jnp.int32)
    for j in range(blocks):
        slots = jnp.where(row == j, slot_ref[j], slots)
    raw[own_slot, :, FACES * FACE :] = slots.astype(jnp.float32)

    def raw_copy(t, ds):
        there = lax.rem(sub + ds, nsub)
        return pltpu.make_async_remote_copy(
            src_ref=raw.at[own_slot],
            dst_ref=raw.at[(1 - t) * nsub + sub],
            send_sem=raw_send.at[(1 + t) * nsub + there],
            recv_sem=raw_recv.at[(1 - t) * nsub + sub],
            device_id=(pos + t, there),
            device_id_type=MESH,
        )

    def raw_landing(t, ds):
        there = lax.rem(sub + ds, nsub)
        slot = (1 + t) * nsub + there
        return pltpu.make_async_remote_copy(
            src_ref=raw.at[own_slot],
            dst_ref=raw.at[slot],
            send_sem=raw_send.at[slot],
            recv_sem=raw_recv.at[slot],
            device_id=(pos + t, there),
            device_id_type=MESH,
        )

    raw_partners = [(t, ds) for t in (-1, 1, 0) for ds in range(nsub) if t or ds]
    pl.semaphore_wait(barrier, expected)
    for t, ds in raw_partners:
        guarded(t, lambda t=t, ds=ds: raw_copy(t, ds).start())
    for k in range(len(inputs)):
        for ds in range(1, nsub):
            peer_copy(ds, k).start()

    def link_copy(t):
        return pltpu.make_async_remote_copy(
            src_ref=link_hbm,
            dst_ref=near_links.at[(1 - t) // 2],
            send_sem=link_send.at[(1 + t) // 2],
            recv_sem=link_recv.at[(1 - t) // 2],
            device_id=(pos + t, sub),
            device_id_type=MESH,
        )

    def link_landing(t):
        return pltpu.make_async_remote_copy(
            src_ref=link_hbm,
            dst_ref=near_links.at[(1 + t) // 2],
            send_sem=link_send.at[(1 + t) // 2],
            recv_sem=link_recv.at[(1 + t) // 2],
            device_id=(pos + t, sub),
            device_id_type=MESH,
        )

    for t in near:
        guarded(t, lambda t=t: link_copy(t).start())

    for copy in own_copies[1:]:
        copy.wait()
    for t, ds in raw_partners:
        if t == 0:
            raw_landing(t, ds).wait_recv()
    order = group_row.astype(jnp.float32)

    def chosen(t):
        return [
            (s, j, raw[(1 + t) * nsub + s, j : j + 1, FACES * FACE :] == order)
            for s in range(nsub)
            for j in range(blocks)
        ]

    picks = chosen(0)
    for k, target in enumerate((field, mf, mc)):
        stage = inputs[k][1]
        for ds in range(1, nsub):
            peer_landing(ds, k).wait_recv()
        for x in range(SIDE):
            for h in range(2):
                total = jnp.zeros((group, LANES), jnp.float32)
                for s, j, pick in picks:
                    total = jnp.where(pick, stage[s, j : j + 1, cells(x, h)], total)
                target[:, cells(x, h)] = total
    for ds in range(1, nsub):
        peer_landing(ds, len(inputs) - 1).wait_recv()

    start = (pos - 1) * group
    places = []
    for s in range(nsub):
        for b in range(blocks):
            for d in range(FACES):
                link = link_ref[s, b, d]
                place = jnp.where(link < 0, wall, jnp.clip(link - start, 0, wall - 1))
                places.append((s * blocks + b, d, place))

    def gather(window):
        for b, d, place in places:
            flipped = FLIP[d]
            ghosts[d, pl.ds(b, 1), :] = window[
                pl.ds(place, 1), flipped * FACE : (flipped + 1) * FACE
            ]

    strip = group_lane // SIDE
    within = group_lane % SIDE

    def interior(x, tile):
        part = tile(x, 0), tile(x, 1)
        up = [pltpu.roll(v, SIDE, 1) for v in part]
        down = [pltpu.roll(v, LANES - SIDE, 1) for v in part]
        found = []
        for h in range(2):
            total = jnp.where(within == 0, 0.0, pltpu.roll(part[h], 1, 1))
            total = total + jnp.where(within == SIDE - 1, 0.0, pltpu.roll(part[h], LANES - 1, 1))
            total = total + jnp.where(strip == 0, up[0] if h else 0.0, up[h])
            total = total + jnp.where(
                strip == half - 1, 0.0 if h else down[1], down[h]
            )
            if x > 0:
                total = total + tile(x - 1, h)
            if x < SIDE - 1:
                total = total + tile(x + 1, h)
            found.append(total)
        return part, found

    def outside(x, h, ghost, at):
        strip = at // SIDE
        within = at % SIDE
        k, m = divmod(x, half)
        halves = slice(h * LANES, (h + 1) * LANES)
        total = jnp.where(within == 0, pltpu.roll(ghost(4, halves), (-x) % LANES, 1), 0.0)
        total = jnp.where(
            within == SIDE - 1, pltpu.roll(ghost(5, halves), SIDE - 1 - x, 1), total
        )
        source = slice(k * LANES, (k + 1) * LANES)
        if h == 0:
            side = pltpu.roll(ghost(2, source), (-SIDE * m) % LANES, 1)
            total = total + jnp.where(strip == 0, side, 0.0)
        else:
            side = pltpu.roll(ghost(3, source), SIDE * (half - 1 - m), 1)
            total = total + jnp.where(strip == half - 1, side, 0.0)
        if x == 0:
            total = total + ghost(0, halves)
        if x == SIDE - 1:
            total = total + ghost(1, halves)
        return total

    def group_ghost(d, at):
        return ghosts[d, :, at]

    def value(x, h):
        return field[:, cells(x, h)]

    def prepare():
        for x in range(SIDE):
            part, found = interior(x, value)
            for h in range(2):
                here = cells(x, h)
                base[:, here] = (1.0 - relaxation) * part[h] + inv[:, here] * (
                    mf[:, here] + found[h]
                )

    for x in range(SIDE):
        for h in range(2):
            inv[:, cells(x, h)] = relaxation / (6.0 + mc[:, cells(x, h)])
    prepare()

    size = SIDE * FACE
    links = jnp.zeros((group, LANES), jnp.int32)
    for s in range(nsub):
        for b in range(blocks):
            for d in range(FACES):
                links = jnp.where(
                    (group_row == s * blocks + b) & (group_lane == d), link_ref[s, b, d], links
                )
    links = links.astype(jnp.float32)
    added = jnp.zeros((group, LANES), jnp.float32)
    for x in range(SIDE):
        for h in range(2):
            added = added + mc[:, cells(x, h)]
    block_diag = 6.0 + jnp.sum(added, axis=1, keepdims=True) / size
    message = jnp.where(group_lane == FACES + 1, block_diag, links)

    for t in (0, -1, 1):
        if t:
            for ds in range(nsub):
                guarded(t, lambda t=t, ds=ds: raw_landing(t, ds).wait_recv())
        picks = chosen(t)
        for d in range(FACES):
            for h in range(2):
                total = jnp.zeros((group, LANES), jnp.float32)
                for s, j, pick in picks:
                    total = jnp.where(
                        pick, raw[(1 + t) * nsub + s, j : j + 1, spot(d, h)], total
                    )
                first[(1 + t) * group : (2 + t) * group, spot(d, h)] = total
    gather(first)

    def face_copy(t):
        return pltpu.make_async_remote_copy(
            src_ref=window.at[pl.ds(group, group)],
            dst_ref=window.at[pl.ds((1 - t) * group, group)],
            send_sem=face_send.at[0, 1 + t],
            recv_sem=face_recv.at[0, 1 - t],
            device_id=(pos + t, sub),
            device_id_type=MESH,
        )

    def face_landing(t):
        return pltpu.make_async_remote_copy(
            src_ref=window.at[pl.ds(group, group)],
            dst_ref=window.at[pl.ds((1 + t) * group, group)],
            send_sem=face_send.at[0, 1 + t],
            recv_sem=face_recv.at[0, 1 + t],
            device_id=(pos + t, sub),
            device_id_type=MESH,
        )

    def coarse_copy(t):
        return pltpu.make_async_remote_copy(
            src_ref=coarse.at[reach],
            dst_ref=coarse.at[reach - t],
            send_sem=coarse_send.at[reach + t],
            recv_sem=coarse_recv.at[reach - t],
            device_id=(pos + t, sub),
            device_id_type=MESH,
        )

    def coarse_landing(t):
        return pltpu.make_async_remote_copy(
            src_ref=coarse.at[reach],
            dst_ref=coarse.at[reach + t],
            send_sem=coarse_send.at[reach + t],
            recv_sem=coarse_recv.at[reach + t],
            device_id=(pos + t, sub),
            device_id_type=MESH,
        )

    def send_coarse():
        left = jnp.zeros((group, LANES), jnp.float32)
        for x in range(SIDE):
            for h in range(2):
                here = cells(x, h)
                left = left + (mf[:, here] - mc[:, here] * field[:, here])
        block = group_lane % group == group_row
        lanes_row = lax.broadcasted_iota(jnp.int32, (8, LANES), 0)
        sums = jnp.zeros((8, LANES), jnp.float32)
        for d in range(FACES):
            both = last_faces[0:group, spot(d, 0)] + last_faces[0:group, spot(d, 1)]
            left = left - both
            total = jnp.sum(both, axis=1, keepdims=True) / size
            line = jnp.sum(jnp.where(block, total, 0.0), axis=0, keepdims=True)
            sums = jnp.where(lanes_row == d, line, sums)
        own_part = jnp.sum(left, axis=1, keepdims=True) / size
        coarse[reach, 0:group, :] = jnp.where(group_lane == FACES, own_part, message)
        coarse[reach, group : group + 8, :] = sums
        for t in sorted(far, key=lambda t: -abs(t)):
            guarded(t, lambda t=t: coarse_copy(t).start())

    def part_copy(t):
        return pltpu.make_async_remote_copy(
            src_ref=parts_out.at[(1 + t) // 2],
            dst_ref=parts_in.at[(1 - t) // 2],
            send_sem=face_send.at[1, 1 + t],
            recv_sem=face_recv.at[1, 1 - t],
            device_id=(pos + t, sub),
            device_id_type=MESH,
        )

    def part_landing(t):
        return pltpu.make_async_remote_copy(
            src_ref=parts_out.at[(1 + t) // 2],
            dst_ref=parts_in.at[(1 + t) // 2],
            send_sem=face_send.at[1, 1 + t],
            recv_sem=face_recv.at[1, 1 + t],
            device_id=(pos + t, sub),
            device_id_type=MESH,
        )

    def own_rows(link, store):
        for b in range(blocks):
            for d in range(FACES):
                place = link(b, d) - pos * group
                place = jnp.where((place < 0) | (place >= group), group, place)
                flipped = FLIP[d]
                store(
                    d * blocks + b,
                    last_faces[pl.ds(place, 1), flipped * FACE : (flipped + 1) * FACE],
                )

    def send_part(t):
        k = (1 + t) // 2

        def store(place, value):
            parts_out[k, place : place + 1, :] = value

        own_rows(lambda b, d: near_links[k, b, d], store)
        part_copy(t).start()

    def swept(x, h):
        here = cells(x, h)
        fresh = base[:, here] + inv[:, here] * outside(x, h, group_ghost, group_lane)
        field[:, here] = fresh
        return fresh

    for step in range(PRE_SWEEPS):
        if step < PRE_SWEEPS - 1:

            def store_faces(d, h, packed):
                window[group : 2 * group, spot(d, h)] = packed

            pack(swept, group, group_lane, store_faces)
            for t in near:
                guarded(t, lambda t=t: face_copy(t).start())
            prepare()
            for t in near:
                guarded(t, lambda t=t: link_landing(t).wait_recv())
            for t in near:
                guarded(t, lambda t=t: face_landing(t).wait_recv())
            gather(window)
        else:

            def store_last(d, h, packed):
                last_faces[0:group, spot(d, h)] = packed

            pack(swept, group, group_lane, store_last)
            send_coarse()
            for t in near:
                guarded(t, lambda t=t: send_part(t))
            prepare()

    def store_own(place, value):
        own_ghosts[place : place + 1, :] = value

    own_rows(lambda b, d: link_ref[sub, b, d], store_own)
    own_links = jnp.zeros((blocks, LANES), jnp.int32)
    for b in range(blocks):
        for d in range(FACES):
            own_links = jnp.where((row == b) & (lane == d), link_ref[sub, b, d], own_links)
    own_links = own_links.astype(jnp.float32)

    for t in far:
        guarded(t, lambda t=t: coarse_landing(t).wait_recv())

    shown = coarse[:, 0:group, :]
    shape = (2 * reach + 1, group, LANES)
    column = lax.broadcasted_iota(jnp.int32, shape, 2)
    index = lax.broadcasted_iota(jnp.int32, shape, 0) * group + lax.broadcasted_iota(
        jnp.int32, shape, 1
    )
    origin = ((pos - reach) * group).astype(jnp.float32)
    numbered = column.astype(jnp.float32) + origin
    face_sums = jnp.zeros((8, LANES), jnp.float32)
    narrow = lax.broadcasted_iota(jnp.int32, (8, LANES), 1)
    for k in range(2 * reach + 1):
        face_sums = jnp.where(narrow // group == k, coarse[k, group : group + 8, :], face_sums)
    linked = jnp.zeros(shape, jnp.float32)
    entering = jnp.zeros(shape, jnp.float32)
    for d in range(FACES):
        link = shown[:, :, d : d + 1]
        hit = (link == numbered) & (link >= 0.0)
        linked = linked + hit.astype(jnp.float32)
        flipped = FLIP[d]
        entering = entering + jnp.where(hit, face_sums[flipped : flipped + 1][None], 0.0)
    residuals = shown[:, :, FACES : FACES + 1] + jnp.sum(entering, axis=2, keepdims=True)
    diags = shown[:, :, FACES + 1 : FACES + 2]
    diags = jnp.where(diags > 0.0, diags, 1.0)

    def turned(values):
        spread = jnp.where(index == column, values, 0.0)
        return jnp.sum(jnp.sum(spread, axis=0), axis=0, keepdims=True)

    scaled = relaxation / diags
    driven = scaled * residuals
    errors = driven
    for step in range(1, COARSE_SWEEPS):
        around = jnp.sum(linked * turned(errors)[None], axis=2, keepdims=True)
        errors = (1.0 - relaxation) * errors + driven + scaled * around
    known = turned(errors)

    own_numbered = lane.astype(jnp.float32) + origin
    own_at = reach * group + sub * blocks + row
    own_error = jnp.sum(jnp.where(lane == own_at, known, 0.0), axis=1, keepdims=True)
    jumps = []
    for d in range(FACES):
        link = own_links[:, d : d + 1]
        hit = (link == own_numbered) & (link >= 0.0)
        jumps.append(jnp.sum(jnp.where(hit, known, 0.0), axis=1, keepdims=True) - own_error)
    own_strip = lane // SIDE
    own_within = lane % SIDE
    plane = jnp.zeros((blocks, LANES), jnp.float32) + 6.0 * own_error
    plane = plane + jnp.where(own_within == 0, jumps[4], 0.0)
    plane = plane + jnp.where(own_within == SIDE - 1, jumps[5], 0.0)
    planes = (
        plane + jnp.where(own_strip == 0, jumps[2], 0.0),
        plane + jnp.where(own_strip == half - 1, jumps[3], 0.0),
    )
    kept = (1.0 - relaxation) * own_error + jnp.zeros((blocks, LANES), jnp.float32)

    def own(whole):
        result = whole[:blocks]
        for s in range(1, nsub):
            result = jnp.where(sub == s, whole[s * blocks : (s + 1) * blocks], result)
        return result

    for t in near:
        guarded(t, lambda t=t: part_landing(t).wait_recv())
    own_ghosts[...] = own_ghosts[...] + parts_in[0] + parts_in[1]

    def own_ghost(d, at):
        return own_ghosts[d * blocks : (d + 1) * blocks, at]

    for x in range(SIDE):
        for h in range(2):
            here = cells(x, h)
            extra = planes[h] + outside(x, h, own_ghost, lane)
            if x == 0:
                extra = extra + jumps[0]
            if x == SIDE - 1:
                extra = extra + jumps[1]
            out_ref[:, here] = own(base[:, here]) + kept + own(inv[:, here]) * extra

    for k in range(len(inputs)):
        for ds in range(1, nsub):
            peer_copy(ds, k).wait_send()
    for t, ds in raw_partners:
        guarded(t, lambda t=t, ds=ds: raw_copy(t, ds).wait_send())
    for t in near:
        guarded(t, lambda t=t: link_copy(t).wait_send())
        guarded(t, lambda t=t: face_copy(t).wait_send())
        guarded(t, lambda t=t: part_copy(t).wait_send())
    for t in far:
        guarded(t, lambda t=t: coarse_copy(t).wait_send())


def on_device(pressure, source_term, coefficient, new_slot, face_links):
    blocks, size = pressure.shape
    count = lax.axis_size("curve")
    nsub = lax.axis_size("sub")
    group = nsub * blocks
    others = max(1, nsub - 1)
    stage = pltpu.VMEM((nsub, blocks, size), jnp.float32)
    field = pltpu.VMEM((group, size), jnp.float32)
    window = pltpu.VMEM((3 * group + 8, FACES * FACE), jnp.float32)
    dma = pltpu.SemaphoreType.DMA
    hbm = pl.BlockSpec(memory_space=pltpu.HBM)
    return pl.pallas_call(
        functools.partial(kernel, count, nsub, blocks),
        out_shape=jax.ShapeDtypeStruct((blocks, size), jnp.float32),
        in_specs=[hbm] * 5,
        out_specs=pl.BlockSpec(memory_space=pltpu.VMEM),
        scratch_shapes=[
            pltpu.SMEM((blocks,), jnp.int32),
            pltpu.SMEM((nsub, blocks, FACES), jnp.int32),
            pltpu.SMEM((2, blocks, FACES), jnp.int32),
            stage,
            stage,
            stage,
            pltpu.VMEM((3 * nsub, blocks, FACES * FACE + LANES), jnp.float32),
            window,
            window,
            pltpu.VMEM((group + 8, FACES * FACE), jnp.float32),
            pltpu.VMEM((2, FACES * blocks, FACE), jnp.float32),
            pltpu.VMEM((2, FACES * blocks, FACE), jnp.float32),
            pltpu.VMEM((FACES, group, FACE), jnp.float32),
            pltpu.VMEM((FACES * blocks, FACE), jnp.float32),
            field,
            field,
            field,
            field,
            field,
            pltpu.VMEM((2 * COARSE_SWEEPS + 3, group + 8, LANES), jnp.float32),
            dma((5,)),
            dma((3 * nsub,)),
            dma((3 * nsub,)),
            dma((PRE_SWEEPS, 3)),
            dma((PRE_SWEEPS, 3)),
            dma((4, others)),
            dma((4, others)),
            dma((2 * COARSE_SWEEPS + 3,)),
            dma((2 * COARSE_SWEEPS + 3,)),
            dma((2,)),
            dma((2,)),
        ],
        compiler_params=pltpu.CompilerParams(
            collective_id=0, has_side_effects=True, vmem_limit_bytes=32 * 1024 * 1024
        ),
    )(
        *(
            pltpu.with_memory_space_constraint(array, pltpu.HBM)
            for array in (new_slot, face_links, pressure, source_term, coefficient)
        )
    )


def solution(mesh):
    placed = (
        P(("curve", "sub"), None),
        P(("curve", "sub"), None),
        P(("curve", "sub"), None),
        P(("curve", "sub")),
        P(("curve", "sub"), None),
    )
    return jax.shard_map(
        on_device, mesh=mesh, in_specs=placed, out_specs=P(("curve", "sub"), None), check_vma=False
    )
```

```python
import functools

import jax
import jax.numpy as jnp
from jax import lax
from jax.experimental import pallas as pl
from jax.experimental.pallas import tpu as pltpu
from jax.sharding import PartitionSpec as P

PRE_SWEEPS = 2
COARSE_SWEEPS = 4
SIDE = 16
GREETED = 3
UNROLL = 2
FACE = SIDE * SIDE
FACES = 6
LANES = 128
FLIP = (1, 0, 3, 2, 5, 4)

relaxation = 0.8
MESH = pl.DeviceIdType.MESH


def kernel(
    count,
    nsub,
    blocks,
    slot_hbm,
    link_hbm,
    p_hbm,
    f_hbm,
    c_hbm,
    out_ref,
    slot_ref,
    link_ref,
    near_links,
    stage_p,
    stage_f,
    stage_c,
    raw,
    first,
    window,
    last_faces,
    parts_out,
    parts_in,
    ghosts,
    own_ghosts,
    mf,
    mc,
    inv,
    field,
    base,
    coarse,
    local_sem,
    raw_send,
    raw_recv,
    face_send,
    face_recv,
    peer_send,
    peer_recv,
    coarse_send,
    coarse_recv,
    link_send,
    link_recv,
):
    pos = lax.axis_index("curve")
    sub = lax.axis_index("sub")
    group = nsub * blocks
    reach = COARSE_SWEEPS + 1
    greeted = GREETED
    wall = 3 * group
    near = (-1, 1)
    far = [t for t in range(-reach, reach + 1) if t]

    def exists(t):
        return (pos + t >= 0) & (pos + t < count)

    def guarded(t, action):
        if t == 0:
            action()
        else:
            pl.when(exists(t))(action)

    barrier = pltpu.get_barrier_semaphore()
    expected = 0
    for t in sorted(range(-greeted, greeted + 1), key=abs):
        for ds in range(nsub if abs(t) <= 1 else 1):
            if t or ds:

                def greet(t=t, ds=ds):
                    pl.semaphore_signal(
                        barrier,
                        inc=1,
                        device_id=(pos + t, lax.rem(sub + ds, nsub)),
                        device_id_type=MESH,
                    )

                guarded(t, greet)
                expected = expected + (exists(t).astype(jnp.int32) if t else 1)

    inputs = (
        (p_hbm, stage_p),
        (f_hbm, stage_f),
        (c_hbm, stage_c),
        (link_hbm, link_ref),
    )
    own_copies = [
        pltpu.make_async_copy(source, stage.at[sub], local_sem.at[k])
        for k, (source, stage) in enumerate(inputs)
    ]
    own_slots = pltpu.make_async_copy(slot_hbm, slot_ref, local_sem.at[len(inputs)])
    own_copies[0].start()
    own_slots.start()
    for copy in own_copies[1:]:
        copy.start()

    def clear(window, rows):
        window[rows] = jnp.zeros((rows.stop - rows.start,) + window.shape[1:], jnp.float32)

    clear(first, slice(wall, wall + 8))
    clear(window, slice(wall, wall + 8))
    clear(last_faces, slice(group, group + 8))
    for t in near:

        @pl.when(jnp.logical_not(exists(t)))
        def _(t=t):
            clear(window, slice((t + 1) * group, (t + 2) * group))
            clear(parts_in, slice((t + 1) // 2, (t + 1) // 2 + 1))
            clear(raw, slice((t + 1) * nsub, (t + 2) * nsub))

    for t in far:

        @pl.when(jnp.logical_not(exists(t)))
        def _(t=t):
            clear(coarse, slice(t + reach, t + reach + 1))

    def peer_copy(ds, k):
        source, stage = inputs[k]
        return pltpu.make_async_remote_copy(
            src_ref=source,
            dst_ref=stage.at[sub],
            send_sem=peer_send.at[k, ds - 1],
            recv_sem=peer_recv.at[k, nsub - ds - 1],
            device_id=(pos, lax.rem(sub + ds, nsub)),
            device_id_type=MESH,
        )

    def peer_landing(ds, k):
        source, stage = inputs[k]
        there = lax.rem(sub + ds, nsub)
        return pltpu.make_async_remote_copy(
            src_ref=source,
            dst_ref=stage.at[there],
            send_sem=peer_send.at[k, ds - 1],
            recv_sem=peer_recv.at[k, ds - 1],
            device_id=(pos, there),
            device_id_type=MESH,
        )

    lane = lax.broadcasted_iota(jnp.int32, (blocks, LANES), 1)
    row = lax.broadcasted_iota(jnp.int32, (blocks, LANES), 0)
    group_lane = lax.broadcasted_iota(jnp.int32, (group, LANES), 1)
    group_row = lax.broadcasted_iota(jnp.int32, (group, LANES), 0)
    half = SIDE // 2

    def pack(tile, rows, at, store):
        strip = at // SIDE
        within = at % SIDE
        zero = jnp.zeros((rows, LANES), jnp.float32)
        y_low = [zero, zero]
        y_high = [zero, zero]
        z_low = [zero, zero]
        z_high = [zero, zero]
        for x in range(SIDE):
            part = tile(x, 0), tile(x, 1)
            k, m = divmod(x, half)
            for h in range(2):
                if x == 0:
                    store(0, h, part[h])
                if x == SIDE - 1:
                    store(1, h, part[h])
                z_low[h] = jnp.where(within == x, pltpu.roll(part[h], x, 1), z_low[h])
                z_high[h] = jnp.where(
                    within == x, pltpu.roll(part[h], (x - SIDE + 1) % LANES, 1), z_high[h]
                )
            y_low[k] = jnp.where(strip == m, pltpu.roll(part[0], SIDE * m, 1), y_low[k])
            y_high[k] = jnp.where(
                strip == m, pltpu.roll(part[1], (SIDE * (m + 1)) % LANES, 1), y_high[k]
            )
        for d, packed in ((2, y_low), (3, y_high), (4, z_low), (5, z_high)):
            for h in range(2):
                store(d, h, packed[h])

    def spot(d, h):
        return slice(d * FACE + h * LANES, d * FACE + (h + 1) * LANES)

    def cells(x, h, shift=0):
        return pl.ds((x + shift) * FACE + h * LANES, LANES)

    def each_x(body):
        def several(i, carried):
            for k in range(UNROLL):
                body(pl.multiple_of(i * (UNROLL * FACE), FACE), k)
            return carried

        lax.fori_loop(0, SIDE // UNROLL, several, 0)

    def at_x(first, k, h, shift=0):
        return pl.ds(pl.multiple_of(first + (k + shift) * FACE + h * LANES, LANES), LANES)

    own_slot = nsub + sub
    own_copies[0].wait()

    def store_raw(d, h, value):
        raw[own_slot, :, spot(d, h)] = value

    pack(lambda x, h: stage_p[sub, :, cells(x, h)], blocks, lane, store_raw)
    own_slots.wait()
    slots = jnp.zeros((blocks, LANES), jnp.int32)
    for j in range(blocks):
        slots = jnp.where(row == j, slot_ref[j], slots)
    raw[own_slot, :, FACES * FACE :] = slots.astype(jnp.float32)

    def raw_copy(t, ds):
        there = lax.rem(sub + ds, nsub)
        return pltpu.make_async_remote_copy(
            src_ref=raw.at[own_slot],
            dst_ref=raw.at[(1 - t) * nsub + sub],
            send_sem=raw_send.at[(1 + t) * nsub + there],
            recv_sem=raw_recv.at[(1 - t) * nsub + sub],
            device_id=(pos + t, there),
            device_id_type=MESH,
        )

    def raw_landing(t, ds):
        there = lax.rem(sub + ds, nsub)
        slot = (1 + t) * nsub + there
        return pltpu.make_async_remote_copy(
            src_ref=raw.at[own_slot],
            dst_ref=raw.at[slot],
            send_sem=raw_send.at[slot],
            recv_sem=raw_recv.at[slot],
            device_id=(pos + t, there),
            device_id_type=MESH,
        )

    raw_partners = [(t, ds) for t in (-1, 1, 0) for ds in range(nsub) if t or ds]
    pl.semaphore_wait(barrier, expected)
    for t, ds in raw_partners:
        guarded(t, lambda t=t, ds=ds: raw_copy(t, ds).start())
    for k in range(len(inputs)):
        for ds in range(1, nsub):
            peer_copy(ds, k).start()

    def link_copy(t):
        return pltpu.make_async_remote_copy(
            src_ref=link_hbm,
            dst_ref=near_links.at[(1 - t) // 2],
            send_sem=link_send.at[(1 + t) // 2],
            recv_sem=link_recv.at[(1 - t) // 2],
            device_id=(pos + t, sub),
            device_id_type=MESH,
        )

    def link_landing(t):
        return pltpu.make_async_remote_copy(
            src_ref=link_hbm,
            dst_ref=near_links.at[(1 + t) // 2],
            send_sem=link_send.at[(1 + t) // 2],
            recv_sem=link_recv.at[(1 + t) // 2],
            device_id=(pos + t, sub),
            device_id_type=MESH,
        )

    for t in near:
        guarded(t, lambda t=t: link_copy(t).start())

    for copy in own_copies[1:]:
        copy.wait()
    for t, ds in raw_partners:
        if t == 0:
            raw_landing(t, ds).wait_recv()
    order = group_row.astype(jnp.float32)

    def chosen(t):
        return [
            (s, j, raw[(1 + t) * nsub + s, j : j + 1, FACES * FACE :] == order)
            for s in range(nsub)
            for j in range(blocks)
        ]

    picks = chosen(0)
    field[:, 0:FACE] = jnp.zeros((group, FACE), jnp.float32)
    field[:, (SIDE + 1) * FACE :] = jnp.zeros((group, FACE), jnp.float32)
    for k in range(3):
        for ds in range(1, nsub):
            peer_landing(ds, k).wait_recv()

    def regrid(first, k):
        for h in range(2):
            for stage, target, shift in ((stage_p, field, 1), (stage_f, mf, 0), (stage_c, mc, 0)):
                total = jnp.zeros((group, LANES), jnp.float32)
                for s, j, pick in picks:
                    total = jnp.where(pick, stage[s, j : j + 1, at_x(first, k, h)], total)
                target[:, at_x(first, k, h, shift)] = total
                if target is mc:
                    inv[:, at_x(first, k, h)] = relaxation / (6.0 + total)

    each_x(regrid)
    for ds in range(1, nsub):
        peer_landing(ds, len(inputs) - 1).wait_recv()

    start = (pos - 1) * group
    places = []
    for s in range(nsub):
        for b in range(blocks):
            for d in range(FACES):
                link = link_ref[s, b, d]
                place = jnp.where(link < 0, wall, jnp.clip(link - start, 0, wall - 1))
                places.append((s * blocks + b, d, place))

    def gather(window):
        for b, d, place in places:
            flipped = FLIP[d]
            ghosts[d, pl.ds(b, 1), :] = window[
                pl.ds(place, 1), flipped * FACE : (flipped + 1) * FACE
            ]

    strip = group_lane // SIDE
    within = group_lane % SIDE

    def interior(first, k):
        def tile(shift, h):
            return field[:, at_x(first, k, h, 1 + shift)]

        part = tile(0, 0), tile(0, 1)
        up = [pltpu.roll(v, SIDE, 1) for v in part]
        down = [pltpu.roll(v, LANES - SIDE, 1) for v in part]
        for h in range(2):
            total = jnp.where(within == 0, 0.0, pltpu.roll(part[h], 1, 1))
            total = total + jnp.where(within == SIDE - 1, 0.0, pltpu.roll(part[h], LANES - 1, 1))
            total = total + jnp.where(strip == 0, up[0] if h else 0.0, up[h])
            total = total + jnp.where(strip == half - 1, 0.0 if h else down[1], down[h])
            total = total + tile(-1, h) + tile(1, h)
            here = at_x(first, k, h)
            base[:, here] = (1.0 - relaxation) * part[h] + inv[:, here] * (mf[:, here] + total)

    def outside(x, h, ghost, at):
        strip = at // SIDE
        within = at % SIDE
        k, m = divmod(x, half)
        halves = slice(h * LANES, (h + 1) * LANES)
        total = jnp.where(within == 0, pltpu.roll(ghost(4, halves), (-x) % LANES, 1), 0.0)
        total = jnp.where(
            within == SIDE - 1, pltpu.roll(ghost(5, halves), SIDE - 1 - x, 1), total
        )
        source = slice(k * LANES, (k + 1) * LANES)
        if h == 0:
            side = pltpu.roll(ghost(2, source), (-SIDE * m) % LANES, 1)
            total = total + jnp.where(strip == 0, side, 0.0)
        else:
            side = pltpu.roll(ghost(3, source), SIDE * (half - 1 - m), 1)
            total = total + jnp.where(strip == half - 1, side, 0.0)
        if x == 0:
            total = total + ghost(0, halves)
        if x == SIDE - 1:
            total = total + ghost(1, halves)
        return total

    def group_ghost(d, at):
        return ghosts[d, :, at]

    def prepare():
        each_x(interior)

    prepare()

    size = SIDE * FACE
    links = jnp.zeros((group, LANES), jnp.int32)
    for s in range(nsub):
        for b in range(blocks):
            for d in range(FACES):
                links = jnp.where(
                    (group_row == s * blocks + b) & (group_lane == d), link_ref[s, b, d], links
                )
    links = links.astype(jnp.float32)
    added = jnp.zeros((group, LANES), jnp.float32)
    for x in range(SIDE):
        for h in range(2):
            added = added + mc[:, cells(x, h)]
    block_diag = 6.0 + jnp.sum(added, axis=1, keepdims=True) / size
    message = jnp.where(group_lane == FACES + 1, block_diag, links)

    for t in (0, -1, 1):
        if t:
            for ds in range(nsub):
                guarded(t, lambda t=t, ds=ds: raw_landing(t, ds).wait_recv())
        picks = chosen(t)
        for d in range(FACES):
            for h in range(2):
                total = jnp.zeros((group, LANES), jnp.float32)
                for s, j, pick in picks:
                    total = jnp.where(
                        pick, raw[(1 + t) * nsub + s, j : j + 1, spot(d, h)], total
                    )
                first[(1 + t) * group : (2 + t) * group, spot(d, h)] = total
    gather(first)

    def face_copy(t):
        return pltpu.make_async_remote_copy(
            src_ref=window.at[pl.ds(group, group)],
            dst_ref=window.at[pl.ds((1 - t) * group, group)],
            send_sem=face_send.at[0, 1 + t],
            recv_sem=face_recv.at[0, 1 - t],
            device_id=(pos + t, sub),
            device_id_type=MESH,
        )

    def face_landing(t):
        return pltpu.make_async_remote_copy(
            src_ref=window.at[pl.ds(group, group)],
            dst_ref=window.at[pl.ds((1 + t) * group, group)],
            send_sem=face_send.at[0, 1 + t],
            recv_sem=face_recv.at[0, 1 + t],
            device_id=(pos + t, sub),
            device_id_type=MESH,
        )

    def coarse_copy(t):
        return pltpu.make_async_remote_copy(
            src_ref=coarse.at[reach],
            dst_ref=coarse.at[reach - t],
            send_sem=coarse_send.at[reach + t],
            recv_sem=coarse_recv.at[reach - t],
            device_id=(pos + t, sub),
            device_id_type=MESH,
        )

    def coarse_landing(t):
        return pltpu.make_async_remote_copy(
            src_ref=coarse.at[reach],
            dst_ref=coarse.at[reach + t],
            send_sem=coarse_send.at[reach + t],
            recv_sem=coarse_recv.at[reach + t],
            device_id=(pos + t, sub),
            device_id_type=MESH,
        )

    def send_coarse():
        left = jnp.zeros((group, LANES), jnp.float32)
        for x in range(SIDE):
            for h in range(2):
                here = cells(x, h)
                left = left + (mf[:, here] - mc[:, here] * field[:, cells(x, h, 1)])
        block = group_lane % group == group_row
        lanes_row = lax.broadcasted_iota(jnp.int32, (8, LANES), 0)
        sums = jnp.zeros((8, LANES), jnp.float32)
        for d in range(FACES):
            both = last_faces[0:group, spot(d, 0)] + last_faces[0:group, spot(d, 1)]
            left = left - both
            total = jnp.sum(both, axis=1, keepdims=True) / size
            line = jnp.sum(jnp.where(block, total, 0.0), axis=0, keepdims=True)
            sums = jnp.where(lanes_row == d, line, sums)
        own_part = jnp.sum(left, axis=1, keepdims=True) / size
        coarse[reach, 0:group, :] = jnp.where(group_lane == FACES, own_part, message)
        coarse[reach, group : group + 8, :] = sums
        for t in sorted(far, key=lambda t: -abs(t)):
            guarded(t, lambda t=t: coarse_copy(t).start())

    def part_copy(t):
        return pltpu.make_async_remote_copy(
            src_ref=parts_out.at[(1 + t) // 2],
            dst_ref=parts_in.at[(1 - t) // 2],
            send_sem=face_send.at[1, 1 + t],
            recv_sem=face_recv.at[1, 1 - t],
            device_id=(pos + t, sub),
            device_id_type=MESH,
        )

    def part_landing(t):
        return pltpu.make_async_remote_copy(
            src_ref=parts_out.at[(1 + t) // 2],
            dst_ref=parts_in.at[(1 + t) // 2],
            send_sem=face_send.at[1, 1 + t],
            recv_sem=face_recv.at[1, 1 + t],
            device_id=(pos + t, sub),
            device_id_type=MESH,
        )

    def own_rows(link, store):
        for b in range(blocks):
            for d in range(FACES):
                place = link(b, d) - pos * group
                place = jnp.where((place < 0) | (place >= group), group, place)
                flipped = FLIP[d]
                store(
                    d * blocks + b,
                    last_faces[pl.ds(place, 1), flipped * FACE : (flipped + 1) * FACE],
                )

    def send_part(t):
        k = (1 + t) // 2

        def store(place, value):
            parts_out[k, place : place + 1, :] = value

        own_rows(lambda b, d: near_links[k, b, d], store)
        part_copy(t).start()

    def swept(x, h):
        here = cells(x, h)
        fresh = base[:, here] + inv[:, here] * outside(x, h, group_ghost, group_lane)
        field[:, cells(x, h, 1)] = fresh
        return fresh

    for step in range(PRE_SWEEPS):
        if step < PRE_SWEEPS - 1:

            def store_faces(d, h, packed):
                window[group : 2 * group, spot(d, h)] = packed

            pack(swept, group, group_lane, store_faces)
            for t in near:
                guarded(t, lambda t=t: face_copy(t).start())
            prepare()
            for t in near:
                guarded(t, lambda t=t: link_landing(t).wait_recv())
            for t in near:
                guarded(t, lambda t=t: face_landing(t).wait_recv())
            gather(window)
        else:

            def store_last(d, h, packed):
                last_faces[0:group, spot(d, h)] = packed

            pack(swept, group, group_lane, store_last)
            send_coarse()
            for t in near:
                guarded(t, lambda t=t: send_part(t))
            prepare()

    def store_own(place, value):
        own_ghosts[place : place + 1, :] = value

    own_rows(lambda b, d: link_ref[sub, b, d], store_own)
    own_links = jnp.zeros((blocks, LANES), jnp.int32)
    for b in range(blocks):
        for d in range(FACES):
            own_links = jnp.where((row == b) & (lane == d), link_ref[sub, b, d], own_links)
    own_links = own_links.astype(jnp.float32)

    for t in far:
        guarded(t, lambda t=t: coarse_landing(t).wait_recv())

    shown = coarse[:, 0:group, :]
    shape = (2 * reach + 1, group, LANES)
    column = lax.broadcasted_iota(jnp.int32, shape, 2)
    index = lax.broadcasted_iota(jnp.int32, shape, 0) * group + lax.broadcasted_iota(
        jnp.int32, shape, 1
    )
    origin = ((pos - reach) * group).astype(jnp.float32)
    numbered = column.astype(jnp.float32) + origin
    face_sums = jnp.zeros((8, LANES), jnp.float32)
    narrow = lax.broadcasted_iota(jnp.int32, (8, LANES), 1)
    for k in range(2 * reach + 1):
        face_sums = jnp.where(narrow // group == k, coarse[k, group : group + 8, :], face_sums)
    linked = jnp.zeros(shape, jnp.float32)
    entering = jnp.zeros(shape, jnp.float32)
    for d in range(FACES):
        link = shown[:, :, d : d + 1]
        hit = (link == numbered) & (link >= 0.0)
        linked = linked + hit.astype(jnp.float32)
        flipped = FLIP[d]
        entering = entering + jnp.where(hit, face_sums[flipped : flipped + 1][None], 0.0)
    residuals = shown[:, :, FACES : FACES + 1] + jnp.sum(entering, axis=2, keepdims=True)
    diags = shown[:, :, FACES + 1 : FACES + 2]
    diags = jnp.where(diags > 0.0, diags, 1.0)

    def turned(values):
        spread = jnp.where(index == column, values, 0.0)
        return jnp.sum(jnp.sum(spread, axis=0), axis=0, keepdims=True)

    scaled = relaxation / diags
    driven = scaled * residuals
    errors = driven
    for step in range(1, COARSE_SWEEPS):
        around = jnp.sum(linked * turned(errors)[None], axis=2, keepdims=True)
        errors = (1.0 - relaxation) * errors + driven + scaled * around
    known = turned(errors)

    own_numbered = lane.astype(jnp.float32) + origin
    own_at = reach * group + sub * blocks + row
    own_error = jnp.sum(jnp.where(lane == own_at, known, 0.0), axis=1, keepdims=True)
    jumps = []
    for d in range(FACES):
        link = own_links[:, d : d + 1]
        hit = (link == own_numbered) & (link >= 0.0)
        jumps.append(jnp.sum(jnp.where(hit, known, 0.0), axis=1, keepdims=True) - own_error)
    own_strip = lane // SIDE
    own_within = lane % SIDE
    plane = jnp.zeros((blocks, LANES), jnp.float32) + 6.0 * own_error
    plane = plane + jnp.where(own_within == 0, jumps[4], 0.0)
    plane = plane + jnp.where(own_within == SIDE - 1, jumps[5], 0.0)
    planes = (
        plane + jnp.where(own_strip == 0, jumps[2], 0.0),
        plane + jnp.where(own_strip == half - 1, jumps[3], 0.0),
    )
    kept = (1.0 - relaxation) * own_error + jnp.zeros((blocks, LANES), jnp.float32)

    def own(whole):
        result = whole[:blocks]
        for s in range(1, nsub):
            result = jnp.where(sub == s, whole[s * blocks : (s + 1) * blocks], result)
        return result

    for t in near:
        guarded(t, lambda t=t: part_landing(t).wait_recv())
    own_ghosts[...] = own_ghosts[...] + parts_in[0] + parts_in[1]

    def own_ghost(d, at):
        return own_ghosts[d * blocks : (d + 1) * blocks, at]

    for x in range(SIDE):
        for h in range(2):
            here = cells(x, h)
            extra = planes[h] + outside(x, h, own_ghost, lane)
            if x == 0:
                extra = extra + jumps[0]
            if x == SIDE - 1:
                extra = extra + jumps[1]
            out_ref[:, here] = own(base[:, here]) + kept + own(inv[:, here]) * extra

    for k in range(len(inputs)):
        for ds in range(1, nsub):
            peer_copy(ds, k).wait_send()
    for t, ds in raw_partners:
        guarded(t, lambda t=t, ds=ds: raw_copy(t, ds).wait_send())
    for t in near:
        guarded(t, lambda t=t: link_copy(t).wait_send())
        guarded(t, lambda t=t: face_copy(t).wait_send())
        guarded(t, lambda t=t: part_copy(t).wait_send())
    for t in far:
        guarded(t, lambda t=t: coarse_copy(t).wait_send())


def on_device(pressure, source_term, coefficient, new_slot, face_links):
    blocks, size = pressure.shape
    count = lax.axis_size("curve")
    nsub = lax.axis_size("sub")
    group = nsub * blocks
    others = max(1, nsub - 1)
    stage = pltpu.VMEM((nsub, blocks, size), jnp.float32)
    field = pltpu.VMEM((group, size), jnp.float32)
    padded = pltpu.VMEM((group, size + 2 * FACE), jnp.float32)
    window = pltpu.VMEM((3 * group + 8, FACES * FACE), jnp.float32)
    dma = pltpu.SemaphoreType.DMA
    hbm = pl.BlockSpec(memory_space=pltpu.HBM)
    return pl.pallas_call(
        functools.partial(kernel, count, nsub, blocks),
        out_shape=jax.ShapeDtypeStruct((blocks, size), jnp.float32),
        in_specs=[hbm] * 5,
        out_specs=pl.BlockSpec(memory_space=pltpu.VMEM),
        scratch_shapes=[
            pltpu.SMEM((blocks,), jnp.int32),
            pltpu.SMEM((nsub, blocks, FACES), jnp.int32),
            pltpu.SMEM((2, blocks, FACES), jnp.int32),
            stage,
            stage,
            stage,
            pltpu.VMEM((3 * nsub, blocks, FACES * FACE + LANES), jnp.float32),
            window,
            window,
            pltpu.VMEM((group + 8, FACES * FACE), jnp.float32),
            pltpu.VMEM((2, FACES * blocks, FACE), jnp.float32),
            pltpu.VMEM((2, FACES * blocks, FACE), jnp.float32),
            pltpu.VMEM((FACES, group, FACE), jnp.float32),
            pltpu.VMEM((FACES * blocks, FACE), jnp.float32),
            field,
            field,
            field,
            padded,
            field,
            pltpu.VMEM((2 * COARSE_SWEEPS + 3, group + 8, LANES), jnp.float32),
            dma((5,)),
            dma((3 * nsub,)),
            dma((3 * nsub,)),
            dma((PRE_SWEEPS, 3)),
            dma((PRE_SWEEPS, 3)),
            dma((4, others)),
            dma((4, others)),
            dma((2 * COARSE_SWEEPS + 3,)),
            dma((2 * COARSE_SWEEPS + 3,)),
            dma((2,)),
            dma((2,)),
        ],
        compiler_params=pltpu.CompilerParams(
            collective_id=0, has_side_effects=True, vmem_limit_bytes=32 * 1024 * 1024
        ),
    )(
        *(
            pltpu.with_memory_space_constraint(array, pltpu.HBM)
            for array in (new_slot, face_links, pressure, source_term, coefficient)
        )
    )


def solution(mesh):
    placed = (
        P(("curve", "sub"), None),
        P(("curve", "sub"), None),
        P(("curve", "sub"), None),
        P(("curve", "sub")),
        P(("curve", "sub"), None),
    )
    return jax.shard_map(
        on_device, mesh=mesh, in_specs=placed, out_specs=P(("curve", "sub"), None), check_vma=False
    )
```

```python
import functools

import jax
import jax.numpy as jnp
from jax import lax
from jax.experimental import pallas as pl
from jax.experimental.pallas import tpu as pltpu
from jax.sharding import PartitionSpec as P

PRE_SWEEPS = 2
COARSE_SWEEPS = 4
SIDE = 16
GREETED = 3
UNROLL = 2
FACE = SIDE * SIDE
FACES = 6
LANES = 128
FLIP = (1, 0, 3, 2, 5, 4)

relaxation = 0.8
MESH = pl.DeviceIdType.MESH


def kernel(
    count,
    nsub,
    blocks,
    slot_hbm,
    link_hbm,
    p_hbm,
    f_hbm,
    c_hbm,
    out_ref,
    slot_ref,
    link_ref,
    near_links,
    stage_p,
    stage_f,
    stage_c,
    raw,
    first,
    window,
    last_faces,
    parts_out,
    parts_in,
    ghosts,
    own_ghosts,
    mf,
    mc,
    inv,
    field,
    base,
    coarse,
    local_sem,
    raw_send,
    raw_recv,
    face_send,
    face_recv,
    peer_send,
    peer_recv,
    coarse_send,
    coarse_recv,
    link_send,
    link_recv,
):
    pos = lax.axis_index("curve")
    sub = lax.axis_index("sub")
    group = nsub * blocks
    reach = COARSE_SWEEPS + 1
    greeted = GREETED
    wall = 3 * group
    near = (-1, 1)
    far = [t for t in range(-reach, reach + 1) if t]

    def exists(t):
        return (pos + t >= 0) & (pos + t < count)

    def guarded(t, action):
        if t == 0:
            action()
        else:
            pl.when(exists(t))(action)

    inputs = (
        (p_hbm, stage_p),
        (f_hbm, stage_f),
        (c_hbm, stage_c),
        (link_hbm, link_ref),
    )
    own_copies = [
        pltpu.make_async_copy(source, stage.at[sub], local_sem.at[k])
        for k, (source, stage) in enumerate(inputs)
    ]
    own_slots = pltpu.make_async_copy(slot_hbm, slot_ref, local_sem.at[len(inputs)])
    own_copies[0].start()

    barrier = pltpu.get_barrier_semaphore()
    expected = 0
    for t in sorted(range(-greeted, greeted + 1), key=abs):
        for ds in range(nsub if abs(t) <= 1 else 1):
            if t or ds:

                def greet(t=t, ds=ds):
                    pl.semaphore_signal(
                        barrier,
                        inc=1,
                        device_id=(pos + t, lax.rem(sub + ds, nsub)),
                        device_id_type=MESH,
                    )

                guarded(t, greet)
                expected = expected + (exists(t).astype(jnp.int32) if t else 1)

    own_slots.start()
    for copy in own_copies[1:]:
        copy.start()

    def clear(window, rows):
        window[rows] = jnp.zeros((rows.stop - rows.start,) + window.shape[1:], jnp.float32)

    clear(first, slice(wall, wall + 8))
    clear(window, slice(wall, wall + 8))
    clear(last_faces, slice(group, group + 8))
    for t in near:

        @pl.when(jnp.logical_not(exists(t)))
        def _(t=t):
            clear(window, slice((t + 1) * group, (t + 2) * group))
            clear(parts_in, slice((t + 1) // 2, (t + 1) // 2 + 1))
            clear(raw, slice((t + 1) * nsub, (t + 2) * nsub))

    for t in far:

        @pl.when(jnp.logical_not(exists(t)))
        def _(t=t):
            clear(coarse, slice(t + reach, t + reach + 1))

    def peer_copy(ds, k):
        source, stage = inputs[k]
        return pltpu.make_async_remote_copy(
            src_ref=source,
            dst_ref=stage.at[sub],
            send_sem=peer_send.at[k, ds - 1],
            recv_sem=peer_recv.at[k, nsub - ds - 1],
            device_id=(pos, lax.rem(sub + ds, nsub)),
            device_id_type=MESH,
        )

    def peer_landing(ds, k):
        source, stage = inputs[k]
        there = lax.rem(sub + ds, nsub)
        return pltpu.make_async_remote_copy(
            src_ref=source,
            dst_ref=stage.at[there],
            send_sem=peer_send.at[k, ds - 1],
            recv_sem=peer_recv.at[k, ds - 1],
            device_id=(pos, there),
            device_id_type=MESH,
        )

    lane = lax.broadcasted_iota(jnp.int32, (blocks, LANES), 1)
    row = lax.broadcasted_iota(jnp.int32, (blocks, LANES), 0)
    group_lane = lax.broadcasted_iota(jnp.int32, (group, LANES), 1)
    group_row = lax.broadcasted_iota(jnp.int32, (group, LANES), 0)
    half = SIDE // 2

    def pack(tile, rows, at, store):
        strip = at // SIDE
        within = at % SIDE
        zero = jnp.zeros((rows, LANES), jnp.float32)
        y_low = [zero, zero]
        y_high = [zero, zero]
        z_low = [zero, zero]
        z_high = [zero, zero]
        for x in range(SIDE):
            part = tile(x, 0), tile(x, 1)
            k, m = divmod(x, half)
            for h in range(2):
                if x == 0:
                    store(0, h, part[h])
                if x == SIDE - 1:
                    store(1, h, part[h])
                z_low[h] = jnp.where(within == x, pltpu.roll(part[h], x, 1), z_low[h])
                z_high[h] = jnp.where(
                    within == x, pltpu.roll(part[h], (x - SIDE + 1) % LANES, 1), z_high[h]
                )
            y_low[k] = jnp.where(strip == m, pltpu.roll(part[0], SIDE * m, 1), y_low[k])
            y_high[k] = jnp.where(
                strip == m, pltpu.roll(part[1], (SIDE * (m + 1)) % LANES, 1), y_high[k]
            )
        for d, packed in ((2, y_low), (3, y_high), (4, z_low), (5, z_high)):
            for h in range(2):
                store(d, h, packed[h])

    def spot(d, h):
        return slice(d * FACE + h * LANES, d * FACE + (h + 1) * LANES)

    def cells(x, h, shift=0):
        return pl.ds((x + shift) * FACE + h * LANES, LANES)

    def each_x(body):
        def several(i, carried):
            for k in range(UNROLL):
                body(pl.multiple_of(i * (UNROLL * FACE), FACE), k)
            return carried

        lax.fori_loop(0, SIDE // UNROLL, several, 0)

    def at_x(first, k, h, shift=0):
        return pl.ds(pl.multiple_of(first + (k + shift) * FACE + h * LANES, LANES), LANES)

    own_slot = nsub + sub
    own_copies[0].wait()

    def store_raw(d, h, value):
        raw[own_slot, :, spot(d, h)] = value

    pack(lambda x, h: stage_p[sub, :, cells(x, h)], blocks, lane, store_raw)
    own_slots.wait()
    slots = jnp.zeros((blocks, LANES), jnp.int32)
    for j in range(blocks):
        slots = jnp.where(row == j, slot_ref[j], slots)
    raw[own_slot, :, FACES * FACE :] = slots.astype(jnp.float32)

    def raw_copy(t, ds):
        there = lax.rem(sub + ds, nsub)
        return pltpu.make_async_remote_copy(
            src_ref=raw.at[own_slot],
            dst_ref=raw.at[(1 - t) * nsub + sub],
            send_sem=raw_send.at[(1 + t) * nsub + there],
            recv_sem=raw_recv.at[(1 - t) * nsub + sub],
            device_id=(pos + t, there),
            device_id_type=MESH,
        )

    def raw_landing(t, ds):
        there = lax.rem(sub + ds, nsub)
        slot = (1 + t) * nsub + there
        return pltpu.make_async_remote_copy(
            src_ref=raw.at[own_slot],
            dst_ref=raw.at[slot],
            send_sem=raw_send.at[slot],
            recv_sem=raw_recv.at[slot],
            device_id=(pos + t, there),
            device_id_type=MESH,
        )

    def link_copy(t):
        return pltpu.make_async_remote_copy(
            src_ref=link_hbm,
            dst_ref=near_links.at[(1 - t) // 2],
            send_sem=link_send.at[(1 + t) // 2],
            recv_sem=link_recv.at[(1 - t) // 2],
            device_id=(pos + t, sub),
            device_id_type=MESH,
        )

    def link_landing(t):
        return pltpu.make_async_remote_copy(
            src_ref=link_hbm,
            dst_ref=near_links.at[(1 + t) // 2],
            send_sem=link_send.at[(1 + t) // 2],
            recv_sem=link_recv.at[(1 + t) // 2],
            device_id=(pos + t, sub),
            device_id_type=MESH,
        )

    raw_partners = [(t, ds) for t in (-1, 1, 0) for ds in range(nsub) if t or ds]
    pl.semaphore_wait(barrier, expected)
    for t in near:

        @pl.when(exists(t))
        def _(t=t):
            for ds in range(nsub):
                raw_copy(t, ds).start()
            link_copy(t).start()

    for ds in range(1, nsub):
        raw_copy(0, ds).start()
    for k in range(len(inputs)):
        for ds in range(1, nsub):
            peer_copy(ds, k).start()

    for copy in own_copies[1:]:
        copy.wait()
    for t, ds in raw_partners:
        if t == 0:
            raw_landing(t, ds).wait_recv()
    order = group_row.astype(jnp.float32)

    def chosen(t):
        return [
            (s, j, raw[(1 + t) * nsub + s, j : j + 1, FACES * FACE :] == order)
            for s in range(nsub)
            for j in range(blocks)
        ]

    picks = chosen(0)
    field[:, 0:FACE] = jnp.zeros((group, FACE), jnp.float32)
    field[:, (SIDE + 1) * FACE :] = jnp.zeros((group, FACE), jnp.float32)
    for k in range(3):
        for ds in range(1, nsub):
            peer_landing(ds, k).wait_recv()

    def regrid(first, k):
        for h in range(2):
            for stage, target, shift in ((stage_p, field, 1), (stage_f, mf, 0), (stage_c, mc, 0)):
                total = jnp.zeros((group, LANES), jnp.float32)
                for s, j, pick in picks:
                    total = jnp.where(pick, stage[s, j : j + 1, at_x(first, k, h)], total)
                target[:, at_x(first, k, h, shift)] = total
                if target is mc:
                    inv[:, at_x(first, k, h)] = relaxation / (6.0 + total)

    each_x(regrid)
    for ds in range(1, nsub):
        peer_landing(ds, len(inputs) - 1).wait_recv()

    start = (pos - 1) * group
    places = []
    for s in range(nsub):
        for b in range(blocks):
            for d in range(FACES):
                link = link_ref[s, b, d]
                place = jnp.where(link < 0, wall, jnp.clip(link - start, 0, wall - 1))
                places.append((s * blocks + b, d, place))

    def gather(window):
        for b, d, place in places:
            flipped = FLIP[d]
            ghosts[d, pl.ds(b, 1), :] = window[
                pl.ds(place, 1), flipped * FACE : (flipped + 1) * FACE
            ]

    strip = group_lane // SIDE
    within = group_lane % SIDE

    def interior(first, k):
        def tile(shift, h):
            return field[:, at_x(first, k, h, 1 + shift)]

        part = tile(0, 0), tile(0, 1)
        up = [pltpu.roll(v, SIDE, 1) for v in part]
        down = [pltpu.roll(v, LANES - SIDE, 1) for v in part]
        for h in range(2):
            total = jnp.where(within == 0, 0.0, pltpu.roll(part[h], 1, 1))
            total = total + jnp.where(within == SIDE - 1, 0.0, pltpu.roll(part[h], LANES - 1, 1))
            total = total + jnp.where(strip == 0, up[0] if h else 0.0, up[h])
            total = total + jnp.where(strip == half - 1, 0.0 if h else down[1], down[h])
            total = total + tile(-1, h) + tile(1, h)
            here = at_x(first, k, h)
            base[:, here] = (1.0 - relaxation) * part[h] + inv[:, here] * (mf[:, here] + total)

    def outside(x, h, ghost, at):
        strip = at // SIDE
        within = at % SIDE
        k, m = divmod(x, half)
        halves = slice(h * LANES, (h + 1) * LANES)
        total = jnp.where(within == 0, pltpu.roll(ghost(4, halves), (-x) % LANES, 1), 0.0)
        total = jnp.where(
            within == SIDE - 1, pltpu.roll(ghost(5, halves), SIDE - 1 - x, 1), total
        )
        source = slice(k * LANES, (k + 1) * LANES)
        if h == 0:
            side = pltpu.roll(ghost(2, source), (-SIDE * m) % LANES, 1)
            total = total + jnp.where(strip == 0, side, 0.0)
        else:
            side = pltpu.roll(ghost(3, source), SIDE * (half - 1 - m), 1)
            total = total + jnp.where(strip == half - 1, side, 0.0)
        if x == 0:
            total = total + ghost(0, halves)
        if x == SIDE - 1:
            total = total + ghost(1, halves)
        return total

    def group_ghost(d, at):
        return ghosts[d, :, at]

    def prepare():
        each_x(interior)

    prepare()

    size = SIDE * FACE
    links = jnp.zeros((group, LANES), jnp.int32)
    for s in range(nsub):
        for b in range(blocks):
            for d in range(FACES):
                links = jnp.where(
                    (group_row == s * blocks + b) & (group_lane == d), link_ref[s, b, d], links
                )
    links = links.astype(jnp.float32)
    added = jnp.zeros((group, LANES), jnp.float32)
    for x in range(SIDE):
        for h in range(2):
            added = added + mc[:, cells(x, h)]
    block_diag = 6.0 + jnp.sum(added, axis=1, keepdims=True) / size
    message = jnp.where(group_lane == FACES + 1, block_diag, links)

    for t in (0, -1, 1):
        if t:

            @pl.when(exists(t))
            def _(t=t):
                for ds in range(nsub):
                    raw_landing(t, ds).wait_recv()

        picks = chosen(t)
        for d in range(FACES):
            for h in range(2):
                total = jnp.zeros((group, LANES), jnp.float32)
                for s, j, pick in picks:
                    total = jnp.where(
                        pick, raw[(1 + t) * nsub + s, j : j + 1, spot(d, h)], total
                    )
                first[(1 + t) * group : (2 + t) * group, spot(d, h)] = total
    gather(first)

    def face_copy(t):
        return pltpu.make_async_remote_copy(
            src_ref=window.at[pl.ds(group, group)],
            dst_ref=window.at[pl.ds((1 - t) * group, group)],
            send_sem=face_send.at[0, 1 + t],
            recv_sem=face_recv.at[0, 1 - t],
            device_id=(pos + t, sub),
            device_id_type=MESH,
        )

    def face_landing(t):
        return pltpu.make_async_remote_copy(
            src_ref=window.at[pl.ds(group, group)],
            dst_ref=window.at[pl.ds((1 + t) * group, group)],
            send_sem=face_send.at[0, 1 + t],
            recv_sem=face_recv.at[0, 1 + t],
            device_id=(pos + t, sub),
            device_id_type=MESH,
        )

    def coarse_copy(t):
        return pltpu.make_async_remote_copy(
            src_ref=coarse.at[reach],
            dst_ref=coarse.at[reach - t],
            send_sem=coarse_send.at[reach + t],
            recv_sem=coarse_recv.at[reach - t],
            device_id=(pos + t, sub),
            device_id_type=MESH,
        )

    def coarse_landing(t):
        return pltpu.make_async_remote_copy(
            src_ref=coarse.at[reach],
            dst_ref=coarse.at[reach + t],
            send_sem=coarse_send.at[reach + t],
            recv_sem=coarse_recv.at[reach + t],
            device_id=(pos + t, sub),
            device_id_type=MESH,
        )

    def send_coarse():
        left = jnp.zeros((group, LANES), jnp.float32)
        for x in range(SIDE):
            for h in range(2):
                here = cells(x, h)
                left = left + (mf[:, here] - mc[:, here] * field[:, cells(x, h, 1)])
        block = group_lane % group == group_row
        lanes_row = lax.broadcasted_iota(jnp.int32, (8, LANES), 0)
        sums = jnp.zeros((8, LANES), jnp.float32)
        for d in range(FACES):
            both = last_faces[0:group, spot(d, 0)] + last_faces[0:group, spot(d, 1)]
            left = left - both
            total = jnp.sum(both, axis=1, keepdims=True) / size
            line = jnp.sum(jnp.where(block, total, 0.0), axis=0, keepdims=True)
            sums = jnp.where(lanes_row == d, line, sums)
        own_part = jnp.sum(left, axis=1, keepdims=True) / size
        coarse[reach, 0:group, :] = jnp.where(group_lane == FACES, own_part, message)
        coarse[reach, group : group + 8, :] = sums
        for t in sorted(far, key=lambda t: -abs(t)):
            guarded(t, lambda t=t: coarse_copy(t).start())

    def part_copy(t):
        return pltpu.make_async_remote_copy(
            src_ref=parts_out.at[(1 + t) // 2],
            dst_ref=parts_in.at[(1 - t) // 2],
            send_sem=face_send.at[1, 1 + t],
            recv_sem=face_recv.at[1, 1 - t],
            device_id=(pos + t, sub),
            device_id_type=MESH,
        )

    def part_landing(t):
        return pltpu.make_async_remote_copy(
            src_ref=parts_out.at[(1 + t) // 2],
            dst_ref=parts_in.at[(1 + t) // 2],
            send_sem=face_send.at[1, 1 + t],
            recv_sem=face_recv.at[1, 1 + t],
            device_id=(pos + t, sub),
            device_id_type=MESH,
        )

    def own_rows(link, store):
        for b in range(blocks):
            for d in range(FACES):
                place = link(b, d) - pos * group
                place = jnp.where((place < 0) | (place >= group), group, place)
                flipped = FLIP[d]
                store(
                    d * blocks + b,
                    last_faces[pl.ds(place, 1), flipped * FACE : (flipped + 1) * FACE],
                )

    def send_part(t):
        k = (1 + t) // 2

        def store(place, value):
            parts_out[k, place : place + 1, :] = value

        own_rows(lambda b, d: near_links[k, b, d], store)
        part_copy(t).start()

    def swept(x, h):
        here = cells(x, h)
        fresh = base[:, here] + inv[:, here] * outside(x, h, group_ghost, group_lane)
        field[:, cells(x, h, 1)] = fresh
        return fresh

    for step in range(PRE_SWEEPS):
        if step < PRE_SWEEPS - 1:

            def store_faces(d, h, packed):
                window[group : 2 * group, spot(d, h)] = packed

            pack(swept, group, group_lane, store_faces)
            for t in near:
                guarded(t, lambda t=t: face_copy(t).start())
            prepare()
            for t in near:

                @pl.when(exists(t))
                def _(t=t):
                    link_landing(t).wait_recv()
                    face_landing(t).wait_recv()

            gather(window)
        else:

            def store_last(d, h, packed):
                last_faces[0:group, spot(d, h)] = packed

            pack(swept, group, group_lane, store_last)
            send_coarse()
            for t in near:
                guarded(t, lambda t=t: send_part(t))
            prepare()

    def store_own(place, value):
        own_ghosts[place : place + 1, :] = value

    own_rows(lambda b, d: link_ref[sub, b, d], store_own)
    own_links = jnp.zeros((blocks, LANES), jnp.int32)
    for b in range(blocks):
        for d in range(FACES):
            own_links = jnp.where((row == b) & (lane == d), link_ref[sub, b, d], own_links)
    own_links = own_links.astype(jnp.float32)

    for t in far:
        guarded(t, lambda t=t: coarse_landing(t).wait_recv())

    count_near = 2 * reach - 1
    shown = coarse[1 : 1 + count_near, 0:group, :]
    shape = (count_near, group, LANES)
    column = lax.broadcasted_iota(jnp.int32, shape, 2)
    index = (lax.broadcasted_iota(jnp.int32, shape, 0) + 1) * group + lax.broadcasted_iota(
        jnp.int32, shape, 1
    )
    origin = ((pos - reach) * group).astype(jnp.float32)
    numbered = column.astype(jnp.float32) + origin
    face_sums = jnp.zeros((8, LANES), jnp.float32)
    narrow = lax.broadcasted_iota(jnp.int32, (8, LANES), 1)
    for k in range(2 * reach + 1):
        face_sums = jnp.where(narrow // group == k, coarse[k, group : group + 8, :], face_sums)
    linked = jnp.zeros(shape, jnp.float32)
    entering = jnp.zeros(shape, jnp.float32)
    for d in range(FACES):
        link = shown[:, :, d : d + 1]
        hit = (link == numbered) & (link >= 0.0)
        linked = linked + hit.astype(jnp.float32)
        flipped = FLIP[d]
        entering = entering + jnp.where(hit, face_sums[flipped : flipped + 1][None], 0.0)
    residuals = shown[:, :, FACES : FACES + 1] + jnp.sum(entering, axis=2, keepdims=True)
    diags = shown[:, :, FACES + 1 : FACES + 2]
    diags = jnp.where(diags > 0.0, diags, 1.0)

    def own(whole):
        result = whole[:blocks]
        for s in range(1, nsub):
            result = jnp.where(sub == s, whole[s * blocks : (s + 1) * blocks], result)
        return result

    for t in near:
        guarded(t, lambda t=t: part_landing(t).wait_recv())
    own_ghosts[...] = own_ghosts[...] + parts_in[0] + parts_in[1]

    def own_ghost(d, at):
        return own_ghosts[d * blocks : (d + 1) * blocks, at]

    for x in range(SIDE):
        for h in range(2):
            here = cells(x, h)
            out_ref[:, here] = own(base[:, here]) + own(inv[:, here]) * outside(
                x, h, own_ghost, lane
            )

    def turned(values, edge):
        kept = slice(edge, count_near - edge)
        spread = jnp.where(index[kept] == column[kept], values, 0.0)
        return jnp.sum(jnp.sum(spread, axis=0), axis=0, keepdims=True)

    scaled = relaxation / diags
    driven = scaled * residuals
    errors = driven
    for step in range(1, COARSE_SWEEPS):
        kept = slice(step, count_near - step)
        around = jnp.sum(linked[kept] * turned(errors, step - 1)[None], axis=2, keepdims=True)
        errors = (1.0 - relaxation) * errors[1:-1] + driven[kept] + scaled[kept] * around
    known = turned(errors, COARSE_SWEEPS - 1)

    own_numbered = lane.astype(jnp.float32) + origin
    own_at = reach * group + sub * blocks + row
    own_error = jnp.sum(jnp.where(lane == own_at, known, 0.0), axis=1, keepdims=True)
    jumps = []
    for d in range(FACES):
        link = own_links[:, d : d + 1]
        hit = (link == own_numbered) & (link >= 0.0)
        jumps.append(jnp.sum(jnp.where(hit, known, 0.0), axis=1, keepdims=True) - own_error)
    own_strip = lane // SIDE
    own_within = lane % SIDE
    plane = jnp.zeros((blocks, LANES), jnp.float32) + 6.0 * own_error
    plane = plane + jnp.where(own_within == 0, jumps[4], 0.0)
    plane = plane + jnp.where(own_within == SIDE - 1, jumps[5], 0.0)
    planes = (
        plane + jnp.where(own_strip == 0, jumps[2], 0.0),
        plane + jnp.where(own_strip == half - 1, jumps[3], 0.0),
    )
    kept = (1.0 - relaxation) * own_error + jnp.zeros((blocks, LANES), jnp.float32)

    for x in range(SIDE):
        for h in range(2):
            here = cells(x, h)
            extra = planes[h]
            if x == 0:
                extra = extra + jumps[0]
            if x == SIDE - 1:
                extra = extra + jumps[1]
            out_ref[:, here] = out_ref[:, here] + (kept + own(inv[:, here]) * extra)

    for k in range(len(inputs)):
        for ds in range(1, nsub):
            peer_copy(ds, k).wait_send()
    for t, ds in raw_partners:
        guarded(t, lambda t=t, ds=ds: raw_copy(t, ds).wait_send())
    for t in near:
        guarded(t, lambda t=t: link_copy(t).wait_send())
        guarded(t, lambda t=t: face_copy(t).wait_send())
        guarded(t, lambda t=t: part_copy(t).wait_send())
    for t in far:
        guarded(t, lambda t=t: coarse_copy(t).wait_send())


def on_device(pressure, source_term, coefficient, new_slot, face_links):
    blocks, size = pressure.shape
    count = lax.axis_size("curve")
    nsub = lax.axis_size("sub")
    group = nsub * blocks
    others = max(1, nsub - 1)
    stage = pltpu.VMEM((nsub, blocks, size), jnp.float32)
    field = pltpu.VMEM((group, size), jnp.float32)
    padded = pltpu.VMEM((group, size + 2 * FACE), jnp.float32)
    window = pltpu.VMEM((3 * group + 8, FACES * FACE), jnp.float32)
    dma = pltpu.SemaphoreType.DMA
    hbm = pl.BlockSpec(memory_space=pltpu.HBM)
    return pl.pallas_call(
        functools.partial(kernel, count, nsub, blocks),
        out_shape=jax.ShapeDtypeStruct((blocks, size), jnp.float32),
        in_specs=[hbm] * 5,
        out_specs=pl.BlockSpec(memory_space=pltpu.VMEM),
        scratch_shapes=[
            pltpu.SMEM((blocks,), jnp.int32),
            pltpu.SMEM((nsub, blocks, FACES), jnp.int32),
            pltpu.SMEM((2, blocks, FACES), jnp.int32),
            stage,
            stage,
            stage,
            pltpu.VMEM((3 * nsub, blocks, FACES * FACE + LANES), jnp.float32),
            window,
            window,
            pltpu.VMEM((group + 8, FACES * FACE), jnp.float32),
            pltpu.VMEM((2, FACES * blocks, FACE), jnp.float32),
            pltpu.VMEM((2, FACES * blocks, FACE), jnp.float32),
            pltpu.VMEM((FACES, group, FACE), jnp.float32),
            pltpu.VMEM((FACES * blocks, FACE), jnp.float32),
            field,
            field,
            field,
            padded,
            field,
            pltpu.VMEM((2 * COARSE_SWEEPS + 3, group + 8, LANES), jnp.float32),
            dma((5,)),
            dma((3 * nsub,)),
            dma((3 * nsub,)),
            dma((PRE_SWEEPS, 3)),
            dma((PRE_SWEEPS, 3)),
            dma((4, others)),
            dma((4, others)),
            dma((2 * COARSE_SWEEPS + 3,)),
            dma((2 * COARSE_SWEEPS + 3,)),
            dma((2,)),
            dma((2,)),
        ],
        compiler_params=pltpu.CompilerParams(
            collective_id=0, has_side_effects=True, vmem_limit_bytes=32 * 1024 * 1024
        ),
    )(
        *(
            pltpu.with_memory_space_constraint(array, pltpu.HBM)
            for array in (new_slot, face_links, pressure, source_term, coefficient)
        )
    )


def solution(mesh):
    placed = (
        P(("curve", "sub"), None),
        P(("curve", "sub"), None),
        P(("curve", "sub"), None),
        P(("curve", "sub")),
        P(("curve", "sub"), None),
    )
    return jax.shard_map(
        on_device, mesh=mesh, in_specs=placed, out_specs=P(("curve", "sub"), None), check_vma=False
    )
```

```python
import functools

import jax
import jax.numpy as jnp
from jax import lax
from jax.experimental import pallas as pl
from jax.experimental.pallas import tpu as pltpu
from jax.sharding import PartitionSpec as P

PRE_SWEEPS = 2
COARSE_SWEEPS = 4
SIDE = 16
GREETED = 3
UNROLL = 2
FACE = SIDE * SIDE
FACES = 6
LANES = 128
FLIP = (1, 0, 3, 2, 5, 4)

relaxation = 0.8
MESH = pl.DeviceIdType.MESH


def kernel(
    count,
    nsub,
    blocks,
    slot_hbm,
    link_hbm,
    p_hbm,
    f_hbm,
    c_hbm,
    out_ref,
    slot_ref,
    link_ref,
    near_links,
    stage_p,
    stage_f,
    stage_c,
    raw,
    first,
    window,
    last_faces,
    parts_out,
    parts_in,
    ghosts,
    own_ghosts,
    mf,
    mc,
    inv,
    field,
    base,
    coarse,
    local_sem,
    raw_send,
    raw_recv,
    face_send,
    face_recv,
    peer_send,
    peer_recv,
    coarse_send,
    coarse_recv,
    link_send,
    link_recv,
):
    pos = lax.axis_index("curve")
    sub = lax.axis_index("sub")
    group = nsub * blocks
    reach = COARSE_SWEEPS + 1
    greeted = GREETED
    wall = 3 * group
    near = (-1, 1)
    far = [t for t in range(-reach, reach + 1) if t]

    def exists(t):
        return (pos + t >= 0) & (pos + t < count)

    def guarded(t, action):
        if t == 0:
            action()
        else:
            pl.when(exists(t))(action)

    inputs = (
        (p_hbm, stage_p),
        (f_hbm, stage_f),
        (c_hbm, stage_c),
        (link_hbm, link_ref),
    )
    own_copies = [
        pltpu.make_async_copy(source, stage.at[sub], local_sem.at[k])
        for k, (source, stage) in enumerate(inputs)
    ]
    own_slots = pltpu.make_async_copy(slot_hbm, slot_ref, local_sem.at[len(inputs)])
    own_copies[0].start()

    barrier = pltpu.get_barrier_semaphore()
    expected = 0
    for t in sorted(range(-greeted, greeted + 1), key=abs):
        for ds in range(nsub if abs(t) <= 1 else 1):
            if t or ds:

                def greet(t=t, ds=ds):
                    pl.semaphore_signal(
                        barrier,
                        inc=1,
                        device_id=(pos + t, lax.rem(sub + ds, nsub)),
                        device_id_type=MESH,
                    )

                guarded(t, greet)
                expected = expected + (exists(t).astype(jnp.int32) if t else 1)

    own_slots.start()
    for copy in own_copies[1:]:
        copy.start()

    def clear(window, rows):
        window[rows] = jnp.zeros((rows.stop - rows.start,) + window.shape[1:], jnp.float32)

    clear(first, slice(wall, wall + 8))
    clear(window, slice(wall, wall + 8))
    clear(last_faces, slice(group, group + 8))
    for t in near:

        @pl.when(jnp.logical_not(exists(t)))
        def _(t=t):
            clear(window, slice((t + 1) * group, (t + 2) * group))
            clear(parts_in, slice((t + 1) // 2, (t + 1) // 2 + 1))
            clear(raw, slice((t + 1) * nsub, (t + 2) * nsub))

    for t in far:

        @pl.when(jnp.logical_not(exists(t)))
        def _(t=t):
            clear(coarse, slice(t + reach, t + reach + 1))

    def peer_copy(ds, k):
        source, stage = inputs[k]
        return pltpu.make_async_remote_copy(
            src_ref=source,
            dst_ref=stage.at[sub],
            send_sem=peer_send.at[k, ds - 1],
            recv_sem=peer_recv.at[k, nsub - ds - 1],
            device_id=(pos, lax.rem(sub + ds, nsub)),
            device_id_type=MESH,
        )

    def peer_landing(ds, k):
        source, stage = inputs[k]
        there = lax.rem(sub + ds, nsub)
        return pltpu.make_async_remote_copy(
            src_ref=source,
            dst_ref=stage.at[there],
            send_sem=peer_send.at[k, ds - 1],
            recv_sem=peer_recv.at[k, ds - 1],
            device_id=(pos, there),
            device_id_type=MESH,
        )

    lane = lax.broadcasted_iota(jnp.int32, (blocks, LANES), 1)
    row = lax.broadcasted_iota(jnp.int32, (blocks, LANES), 0)
    group_lane = lax.broadcasted_iota(jnp.int32, (group, LANES), 1)
    group_row = lax.broadcasted_iota(jnp.int32, (group, LANES), 0)
    half = SIDE // 2

    def pack(tile, rows, at, store):
        strip = at // SIDE
        within = at % SIDE
        zero = jnp.zeros((rows, LANES), jnp.float32)
        y_low = [zero, zero]
        y_high = [zero, zero]
        z_low = [zero, zero]
        z_high = [zero, zero]
        for x in range(SIDE):
            part = tile(x, 0), tile(x, 1)
            k, m = divmod(x, half)
            for h in range(2):
                if x == 0:
                    store(0, h, part[h])
                if x == SIDE - 1:
                    store(1, h, part[h])
                z_low[h] = jnp.where(within == x, pltpu.roll(part[h], x, 1), z_low[h])
                z_high[h] = jnp.where(
                    within == x, pltpu.roll(part[h], (x - SIDE + 1) % LANES, 1), z_high[h]
                )
            y_low[k] = jnp.where(strip == m, pltpu.roll(part[0], SIDE * m, 1), y_low[k])
            y_high[k] = jnp.where(
                strip == m, pltpu.roll(part[1], (SIDE * (m + 1)) % LANES, 1), y_high[k]
            )
        for d, packed in ((2, y_low), (3, y_high), (4, z_low), (5, z_high)):
            for h in range(2):
                store(d, h, packed[h])

    def spot(d, h):
        return slice(d * FACE + h * LANES, d * FACE + (h + 1) * LANES)

    def cells(x, h, shift=0):
        return pl.ds((x + shift) * FACE + h * LANES, LANES)

    def each_x(body):
        def several(i, carried):
            for k in range(UNROLL):
                body(pl.multiple_of(i * (UNROLL * FACE), FACE), k)
            return carried

        lax.fori_loop(0, SIDE // UNROLL, several, 0)

    def at_x(first, k, h, shift=0):
        return pl.ds(pl.multiple_of(first + (k + shift) * FACE + h * LANES, LANES), LANES)

    own_slot = nsub + sub
    own_copies[0].wait()

    def store_raw(d, h, value):
        raw[own_slot, :, spot(d, h)] = value

    pack(lambda x, h: stage_p[sub, :, cells(x, h)], blocks, lane, store_raw)
    own_slots.wait()
    slots = jnp.zeros((blocks, LANES), jnp.int32)
    for j in range(blocks):
        slots = jnp.where(row == j, slot_ref[j], slots)
    raw[own_slot, :, FACES * FACE :] = slots.astype(jnp.float32)

    def raw_copy(t, ds):
        there = lax.rem(sub + ds, nsub)
        return pltpu.make_async_remote_copy(
            src_ref=raw.at[own_slot],
            dst_ref=raw.at[(1 - t) * nsub + sub],
            send_sem=raw_send.at[(1 + t) * nsub + there],
            recv_sem=raw_recv.at[(1 - t) * nsub + sub],
            device_id=(pos + t, there),
            device_id_type=MESH,
        )

    def raw_landing(t, ds):
        there = lax.rem(sub + ds, nsub)
        slot = (1 + t) * nsub + there
        return pltpu.make_async_remote_copy(
            src_ref=raw.at[own_slot],
            dst_ref=raw.at[slot],
            send_sem=raw_send.at[slot],
            recv_sem=raw_recv.at[slot],
            device_id=(pos + t, there),
            device_id_type=MESH,
        )

    def link_copy(t):
        return pltpu.make_async_remote_copy(
            src_ref=link_hbm,
            dst_ref=near_links.at[(1 - t) // 2],
            send_sem=link_send.at[(1 + t) // 2],
            recv_sem=link_recv.at[(1 - t) // 2],
            device_id=(pos + t, sub),
            device_id_type=MESH,
        )

    def link_landing(t):
        return pltpu.make_async_remote_copy(
            src_ref=link_hbm,
            dst_ref=near_links.at[(1 + t) // 2],
            send_sem=link_send.at[(1 + t) // 2],
            recv_sem=link_recv.at[(1 + t) // 2],
            device_id=(pos + t, sub),
            device_id_type=MESH,
        )

    raw_partners = [(t, ds) for t in (-1, 1, 0) for ds in range(nsub) if t or ds]
    pl.semaphore_wait(barrier, expected)
    for t in near:

        @pl.when(exists(t))
        def _(t=t):
            for ds in range(nsub):
                raw_copy(t, ds).start()
            link_copy(t).start()

    for ds in range(1, nsub):
        raw_copy(0, ds).start()
    for k in range(len(inputs)):
        for ds in range(1, nsub):
            peer_copy(ds, k).start()

    for copy in own_copies[1:]:
        copy.wait()
    for t, ds in raw_partners:
        if t == 0:
            raw_landing(t, ds).wait_recv()
    order = group_row.astype(jnp.float32)

    def chosen(t):
        return [
            (s, j, raw[(1 + t) * nsub + s, j : j + 1, FACES * FACE :] == order)
            for s in range(nsub)
            for j in range(blocks)
        ]

    picks = chosen(0)
    field[:, 0:FACE] = jnp.zeros((group, FACE), jnp.float32)
    field[:, (SIDE + 1) * FACE :] = jnp.zeros((group, FACE), jnp.float32)
    for k in range(3):
        for ds in range(1, nsub):
            peer_landing(ds, k).wait_recv()

    def regrid(first, k):
        for h in range(2):
            for stage, target, shift in ((stage_p, field, 1), (stage_f, mf, 0), (stage_c, mc, 0)):
                total = jnp.zeros((group, LANES), jnp.float32)
                for s, j, pick in picks:
                    total = jnp.where(pick, stage[s, j : j + 1, at_x(first, k, h)], total)
                target[:, at_x(first, k, h, shift)] = total
                if target is mc:
                    inv[:, at_x(first, k, h)] = relaxation / (6.0 + total)

    each_x(regrid)
    for ds in range(1, nsub):
        peer_landing(ds, len(inputs) - 1).wait_recv()

    start = (pos - 1) * group
    places = []
    for s in range(nsub):
        for b in range(blocks):
            for d in range(FACES):
                link = link_ref[s, b, d]
                place = jnp.where(link < 0, wall, jnp.clip(link - start, 0, wall - 1))
                places.append((s * blocks + b, d, place))

    def gather(window):
        for b, d, place in places:
            flipped = FLIP[d]
            ghosts[d, pl.ds(b, 1), :] = window[
                pl.ds(place, 1), flipped * FACE : (flipped + 1) * FACE
            ]

    strip = group_lane // SIDE
    within = group_lane % SIDE

    def interior(first, k):
        def tile(shift, h):
            return field[:, at_x(first, k, h, 1 + shift)]

        part = tile(0, 0), tile(0, 1)
        up = [pltpu.roll(v, SIDE, 1) for v in part]
        down = [pltpu.roll(v, LANES - SIDE, 1) for v in part]
        for h in range(2):
            total = jnp.where(within == 0, 0.0, pltpu.roll(part[h], 1, 1))
            total = total + jnp.where(within == SIDE - 1, 0.0, pltpu.roll(part[h], LANES - 1, 1))
            total = total + jnp.where(strip == 0, up[0] if h else 0.0, up[h])
            total = total + jnp.where(strip == half - 1, 0.0 if h else down[1], down[h])
            total = total + tile(-1, h) + tile(1, h)
            here = at_x(first, k, h)
            base[:, here] = (1.0 - relaxation) * part[h] + inv[:, here] * (mf[:, here] + total)

    def outside(x, h, ghost, at):
        strip = at // SIDE
        within = at % SIDE
        k, m = divmod(x, half)
        halves = slice(h * LANES, (h + 1) * LANES)
        total = jnp.where(within == 0, pltpu.roll(ghost(4, halves), (-x) % LANES, 1), 0.0)
        total = jnp.where(
            within == SIDE - 1, pltpu.roll(ghost(5, halves), SIDE - 1 - x, 1), total
        )
        source = slice(k * LANES, (k + 1) * LANES)
        if h == 0:
            side = pltpu.roll(ghost(2, source), (-SIDE * m) % LANES, 1)
            total = total + jnp.where(strip == 0, side, 0.0)
        else:
            side = pltpu.roll(ghost(3, source), SIDE * (half - 1 - m), 1)
            total = total + jnp.where(strip == half - 1, side, 0.0)
        if x == 0:
            total = total + ghost(0, halves)
        if x == SIDE - 1:
            total = total + ghost(1, halves)
        return total

    def group_ghost(d, at):
        return ghosts[d, :, at]

    def prepare():
        each_x(interior)

    prepare()

    size = SIDE * FACE
    links = jnp.zeros((group, LANES), jnp.int32)
    for s in range(nsub):
        for b in range(blocks):
            for d in range(FACES):
                links = jnp.where(
                    (group_row == s * blocks + b) & (group_lane == d), link_ref[s, b, d], links
                )
    links = links.astype(jnp.float32)
    added = jnp.zeros((group, LANES), jnp.float32)
    for x in range(SIDE):
        for h in range(2):
            added = added + mc[:, cells(x, h)]
    block_diag = 6.0 + jnp.sum(added, axis=1, keepdims=True) / size
    message = jnp.where(group_lane == FACES + 1, block_diag, links)

    for t in (0, -1, 1):
        if t:

            @pl.when(exists(t))
            def _(t=t):
                for ds in range(nsub):
                    raw_landing(t, ds).wait_recv()

        picks = chosen(t)
        for d in range(FACES):
            for h in range(2):
                total = jnp.zeros((group, LANES), jnp.float32)
                for s, j, pick in picks:
                    total = jnp.where(
                        pick, raw[(1 + t) * nsub + s, j : j + 1, spot(d, h)], total
                    )
                first[(1 + t) * group : (2 + t) * group, spot(d, h)] = total
    gather(first)

    def face_copy(t):
        return pltpu.make_async_remote_copy(
            src_ref=window.at[pl.ds(group, group)],
            dst_ref=window.at[pl.ds((1 - t) * group, group)],
            send_sem=face_send.at[0, 1 + t],
            recv_sem=face_recv.at[0, 1 - t],
            device_id=(pos + t, sub),
            device_id_type=MESH,
        )

    def face_landing(t):
        return pltpu.make_async_remote_copy(
            src_ref=window.at[pl.ds(group, group)],
            dst_ref=window.at[pl.ds((1 + t) * group, group)],
            send_sem=face_send.at[0, 1 + t],
            recv_sem=face_recv.at[0, 1 + t],
            device_id=(pos + t, sub),
            device_id_type=MESH,
        )

    def coarse_copy(t):
        return pltpu.make_async_remote_copy(
            src_ref=coarse.at[reach],
            dst_ref=coarse.at[reach - t],
            send_sem=coarse_send.at[reach + t],
            recv_sem=coarse_recv.at[reach - t],
            device_id=(pos + t, sub),
            device_id_type=MESH,
        )

    def coarse_landing(t):
        return pltpu.make_async_remote_copy(
            src_ref=coarse.at[reach],
            dst_ref=coarse.at[reach + t],
            send_sem=coarse_send.at[reach + t],
            recv_sem=coarse_recv.at[reach + t],
            device_id=(pos + t, sub),
            device_id_type=MESH,
        )

    def send_coarse():
        left = jnp.zeros((group, LANES), jnp.float32)
        for x in range(SIDE):
            for h in range(2):
                here = cells(x, h)
                left = left + (mf[:, here] - mc[:, here] * field[:, cells(x, h, 1)])
        block = group_lane % group == group_row
        lanes_row = lax.broadcasted_iota(jnp.int32, (8, LANES), 0)
        sums = jnp.zeros((8, LANES), jnp.float32)
        for d in range(FACES):
            both = last_faces[0:group, spot(d, 0)] + last_faces[0:group, spot(d, 1)]
            left = left - both
            total = jnp.sum(both, axis=1, keepdims=True) / size
            line = jnp.sum(jnp.where(block, total, 0.0), axis=0, keepdims=True)
            sums = jnp.where(lanes_row == d, line, sums)
        own_part = jnp.sum(left, axis=1, keepdims=True) / size
        coarse[reach, 0:group, :] = jnp.where(group_lane == FACES, own_part, message)
        coarse[reach, group : group + 8, :] = sums
        for t in sorted(far, key=lambda t: -abs(t)):
            guarded(t, lambda t=t: coarse_copy(t).start())

    def part_copy(t):
        return pltpu.make_async_remote_copy(
            src_ref=parts_out.at[(1 + t) // 2],
            dst_ref=parts_in.at[(1 - t) // 2],
            send_sem=face_send.at[1, 1 + t],
            recv_sem=face_recv.at[1, 1 - t],
            device_id=(pos + t, sub),
            device_id_type=MESH,
        )

    def part_landing(t):
        return pltpu.make_async_remote_copy(
            src_ref=parts_out.at[(1 + t) // 2],
            dst_ref=parts_in.at[(1 + t) // 2],
            send_sem=face_send.at[1, 1 + t],
            recv_sem=face_recv.at[1, 1 + t],
            device_id=(pos + t, sub),
            device_id_type=MESH,
        )

    def own_rows(link, store):
        for b in range(blocks):
            for d in range(FACES):
                place = link(b, d) - pos * group
                place = jnp.where((place < 0) | (place >= group), group, place)
                flipped = FLIP[d]
                store(
                    d * blocks + b,
                    last_faces[pl.ds(place, 1), flipped * FACE : (flipped + 1) * FACE],
                )

    def send_part(t):
        k = (1 + t) // 2

        def store(place, value):
            parts_out[k, place : place + 1, :] = value

        own_rows(lambda b, d: near_links[k, b, d], store)
        part_copy(t).start()

    def swept(x, h):
        here = cells(x, h)
        fresh = base[:, here] + inv[:, here] * outside(x, h, group_ghost, group_lane)
        field[:, cells(x, h, 1)] = fresh
        return fresh

    for step in range(PRE_SWEEPS):
        if step < PRE_SWEEPS - 1:

            def store_faces(d, h, packed):
                window[group : 2 * group, spot(d, h)] = packed

            pack(swept, group, group_lane, store_faces)
            for t in near:
                guarded(t, lambda t=t: face_copy(t).start())
            prepare()
            for ds in range(1, nsub):
                for k in range(len(inputs)):
                    peer_copy(ds, k).wait_send()
                raw_copy(0, ds).wait_send()
            for t in near:

                @pl.when(exists(t))
                def _(t=t):
                    for ds in range(nsub):
                        raw_copy(t, ds).wait_send()
                    link_copy(t).wait_send()
                    link_landing(t).wait_recv()
                    face_landing(t).wait_recv()

            gather(window)
        else:

            def store_last(d, h, packed):
                last_faces[0:group, spot(d, h)] = packed

            pack(swept, group, group_lane, store_last)
            send_coarse()
            for t in near:
                guarded(t, lambda t=t: send_part(t))
            prepare()

    def store_own(place, value):
        own_ghosts[place : place + 1, :] = value

    own_rows(lambda b, d: link_ref[sub, b, d], store_own)
    own_links = jnp.zeros((blocks, LANES), jnp.int32)
    for b in range(blocks):
        for d in range(FACES):
            own_links = jnp.where((row == b) & (lane == d), link_ref[sub, b, d], own_links)
    own_links = own_links.astype(jnp.float32)

    for t in near:
        guarded(t, lambda t=t: face_copy(t).wait_send())
    for t in far:

        @pl.when(exists(t))
        def _(t=t):
            coarse_copy(t).wait_send()
            coarse_landing(t).wait_recv()


    count_near = 2 * reach - 1
    shown = coarse[1 : 1 + count_near, 0:group, :]
    shape = (count_near, group, LANES)
    column = lax.broadcasted_iota(jnp.int32, shape, 2)
    index = (lax.broadcasted_iota(jnp.int32, shape, 0) + 1) * group + lax.broadcasted_iota(
        jnp.int32, shape, 1
    )
    origin = ((pos - reach) * group).astype(jnp.float32)
    numbered = column.astype(jnp.float32) + origin
    face_sums = jnp.zeros((8, LANES), jnp.float32)
    narrow = lax.broadcasted_iota(jnp.int32, (8, LANES), 1)
    for k in range(2 * reach + 1):
        face_sums = jnp.where(narrow // group == k, coarse[k, group : group + 8, :], face_sums)
    linked = jnp.zeros(shape, jnp.float32)
    entering = jnp.zeros(shape, jnp.float32)
    for d in range(FACES):
        link = shown[:, :, d : d + 1]
        hit = (link == numbered) & (link >= 0.0)
        linked = linked + hit.astype(jnp.float32)
        flipped = FLIP[d]
        entering = entering + jnp.where(hit, face_sums[flipped : flipped + 1][None], 0.0)
    residuals = shown[:, :, FACES : FACES + 1] + jnp.sum(entering, axis=2, keepdims=True)
    diags = shown[:, :, FACES + 1 : FACES + 2]
    diags = jnp.where(diags > 0.0, diags, 1.0)

    def own(whole):
        result = whole[:blocks]
        for s in range(1, nsub):
            result = jnp.where(sub == s, whole[s * blocks : (s + 1) * blocks], result)
        return result

    for t in near:

        @pl.when(exists(t))
        def _(t=t):
            part_copy(t).wait_send()
            part_landing(t).wait_recv()

    own_ghosts[...] = own_ghosts[...] + parts_in[0] + parts_in[1]

    def own_ghost(d, at):
        return own_ghosts[d * blocks : (d + 1) * blocks, at]

    for x in range(SIDE):
        for h in range(2):
            here = cells(x, h)
            out_ref[:, here] = own(base[:, here]) + own(inv[:, here]) * outside(
                x, h, own_ghost, lane
            )

    def turned(values, edge):
        kept = slice(edge, count_near - edge)
        spread = jnp.where(index[kept] == column[kept], values, 0.0)
        return jnp.sum(jnp.sum(spread, axis=0), axis=0, keepdims=True)

    scaled = relaxation / diags
    driven = scaled * residuals
    errors = driven
    for step in range(1, COARSE_SWEEPS):
        kept = slice(step, count_near - step)
        around = jnp.sum(linked[kept] * turned(errors, step - 1)[None], axis=2, keepdims=True)
        errors = (1.0 - relaxation) * errors[1:-1] + driven[kept] + scaled[kept] * around
    known = turned(errors, COARSE_SWEEPS - 1)

    own_numbered = lane.astype(jnp.float32) + origin
    own_at = reach * group + sub * blocks + row
    own_error = jnp.sum(jnp.where(lane == own_at, known, 0.0), axis=1, keepdims=True)
    jumps = []
    for d in range(FACES):
        link = own_links[:, d : d + 1]
        hit = (link == own_numbered) & (link >= 0.0)
        jumps.append(jnp.sum(jnp.where(hit, known, 0.0), axis=1, keepdims=True) - own_error)
    own_strip = lane // SIDE
    own_within = lane % SIDE
    plane = jnp.zeros((blocks, LANES), jnp.float32) + 6.0 * own_error
    plane = plane + jnp.where(own_within == 0, jumps[4], 0.0)
    plane = plane + jnp.where(own_within == SIDE - 1, jumps[5], 0.0)
    planes = (
        plane + jnp.where(own_strip == 0, jumps[2], 0.0),
        plane + jnp.where(own_strip == half - 1, jumps[3], 0.0),
    )
    kept = (1.0 - relaxation) * own_error + jnp.zeros((blocks, LANES), jnp.float32)

    for x in range(SIDE):
        for h in range(2):
            here = cells(x, h)
            extra = planes[h]
            if x == 0:
                extra = extra + jumps[0]
            if x == SIDE - 1:
                extra = extra + jumps[1]
            out_ref[:, here] = out_ref[:, here] + (kept + own(inv[:, here]) * extra)


def on_device(pressure, source_term, coefficient, new_slot, face_links):
    blocks, size = pressure.shape
    count = lax.axis_size("curve")
    nsub = lax.axis_size("sub")
    group = nsub * blocks
    others = max(1, nsub - 1)
    stage = pltpu.VMEM((nsub, blocks, size), jnp.float32)
    field = pltpu.VMEM((group, size), jnp.float32)
    padded = pltpu.VMEM((group, size + 2 * FACE), jnp.float32)
    window = pltpu.VMEM((3 * group + 8, FACES * FACE), jnp.float32)
    dma = pltpu.SemaphoreType.DMA
    hbm = pl.BlockSpec(memory_space=pltpu.HBM)
    return pl.pallas_call(
        functools.partial(kernel, count, nsub, blocks),
        out_shape=jax.ShapeDtypeStruct((blocks, size), jnp.float32),
        in_specs=[hbm] * 5,
        out_specs=pl.BlockSpec(memory_space=pltpu.VMEM),
        scratch_shapes=[
            pltpu.SMEM((blocks,), jnp.int32),
            pltpu.SMEM((nsub, blocks, FACES), jnp.int32),
            pltpu.SMEM((2, blocks, FACES), jnp.int32),
            stage,
            stage,
            stage,
            pltpu.VMEM((3 * nsub, blocks, FACES * FACE + LANES), jnp.float32),
            window,
            window,
            pltpu.VMEM((group + 8, FACES * FACE), jnp.float32),
            pltpu.VMEM((2, FACES * blocks, FACE), jnp.float32),
            pltpu.VMEM((2, FACES * blocks, FACE), jnp.float32),
            pltpu.VMEM((FACES, group, FACE), jnp.float32),
            pltpu.VMEM((FACES * blocks, FACE), jnp.float32),
            field,
            field,
            field,
            padded,
            field,
            pltpu.VMEM((2 * COARSE_SWEEPS + 3, group + 8, LANES), jnp.float32),
            dma((5,)),
            dma((3 * nsub,)),
            dma((3 * nsub,)),
            dma((PRE_SWEEPS, 3)),
            dma((PRE_SWEEPS, 3)),
            dma((4, others)),
            dma((4, others)),
            dma((2 * COARSE_SWEEPS + 3,)),
            dma((2 * COARSE_SWEEPS + 3,)),
            dma((2,)),
            dma((2,)),
        ],
        compiler_params=pltpu.CompilerParams(
            collective_id=0, has_side_effects=True, vmem_limit_bytes=32 * 1024 * 1024
        ),
    )(
        *(
            pltpu.with_memory_space_constraint(array, pltpu.HBM)
            for array in (new_slot, face_links, pressure, source_term, coefficient)
        )
    )


def solution(mesh):
    placed = (
        P(("curve", "sub"), None),
        P(("curve", "sub"), None),
        P(("curve", "sub"), None),
        P(("curve", "sub")),
        P(("curve", "sub"), None),
    )
    return jax.shard_map(
        on_device, mesh=mesh, in_specs=placed, out_specs=P(("curve", "sub"), None), check_vma=False
    )
```

```python
import functools

import jax
import jax.numpy as jnp
from jax import lax
from jax.experimental import pallas as pl
from jax.experimental.pallas import tpu as pltpu
from jax.sharding import PartitionSpec as P

PRE_SWEEPS = 2
COARSE_SWEEPS = 4
SIDE = 16
GREETED = 3
UNROLL = 2
FACE = SIDE * SIDE
FACES = 6
LANES = 128
FLIP = (1, 0, 3, 2, 5, 4)

relaxation = 0.8
MESH = pl.DeviceIdType.MESH


def kernel(
    count,
    nsub,
    blocks,
    slot_hbm,
    link_hbm,
    p_hbm,
    f_hbm,
    c_hbm,
    out_ref,
    slot_ref,
    link_ref,
    near_links,
    stage_p,
    stage_f,
    stage_c,
    raw,
    first,
    window_low,
    window_high,
    last_faces,
    parts_out,
    parts_in,
    ghosts,
    own_ghosts,
    mf,
    mc,
    inv,
    field,
    base,
    coarse,
    local_sem,
    raw_send,
    raw_recv,
    face_send,
    face_recv,
    peer_send,
    peer_recv,
    coarse_send,
    coarse_recv,
    link_send,
    link_recv,
):
    pos = lax.axis_index("curve")
    sub = lax.axis_index("sub")
    group = nsub * blocks
    reach = COARSE_SWEEPS + 1
    greeted = GREETED
    wall = 3 * group
    windows = (window_low, window_high)
    near = (-1, 1)
    far = [t for t in range(-reach, reach + 1) if t]

    def exists(t):
        return (pos + t >= 0) & (pos + t < count)

    def guarded(t, action):
        if t == 0:
            action()
        else:
            pl.when(exists(t))(action)

    inputs = (
        (p_hbm, stage_p),
        (f_hbm, stage_f),
        (c_hbm, stage_c),
        (link_hbm, link_ref),
    )
    own_copies = [
        pltpu.make_async_copy(source, stage.at[sub], local_sem.at[k])
        for k, (source, stage) in enumerate(inputs)
    ]
    own_slots = pltpu.make_async_copy(slot_hbm, slot_ref, local_sem.at[len(inputs)])
    own_copies[0].start()

    barrier = pltpu.get_barrier_semaphore()
    expected = 0
    for t in sorted(range(-greeted, greeted + 1), key=abs):
        for ds in range(nsub if abs(t) <= 1 else 1):
            if t or ds:

                def greet(t=t, ds=ds):
                    pl.semaphore_signal(
                        barrier,
                        inc=1,
                        device_id=(pos + t, lax.rem(sub + ds, nsub)),
                        device_id_type=MESH,
                    )

                guarded(t, greet)
                expected = expected + (exists(t).astype(jnp.int32) if t else 1)

    own_slots.start()
    for copy in own_copies[1:]:
        copy.start()

    def clear(window, rows):
        window[rows] = jnp.zeros((rows.stop - rows.start,) + window.shape[1:], jnp.float32)

    clear(first, slice(wall, wall + 8))
    for window in windows:
        clear(window, slice(wall, wall + 8))
    clear(last_faces, slice(group, group + 8))
    for t in near:

        @pl.when(jnp.logical_not(exists(t)))
        def _(t=t):
            for window in windows:
                clear(window, slice((t + 1) * group, (t + 2) * group))
            clear(parts_in, slice((t + 1) // 2, (t + 1) // 2 + 1))
            clear(raw, slice((t + 1) * nsub, (t + 2) * nsub))

    for t in far:

        @pl.when(jnp.logical_not(exists(t)))
        def _(t=t):
            clear(coarse, slice(t + reach, t + reach + 1))

    def peer_copy(ds, k):
        source, stage = inputs[k]
        return pltpu.make_async_remote_copy(
            src_ref=source,
            dst_ref=stage.at[sub],
            send_sem=peer_send.at[k, ds - 1],
            recv_sem=peer_recv.at[k, nsub - ds - 1],
            device_id=(pos, lax.rem(sub + ds, nsub)),
            device_id_type=MESH,
        )

    def peer_landing(ds, k):
        source, stage = inputs[k]
        there = lax.rem(sub + ds, nsub)
        return pltpu.make_async_remote_copy(
            src_ref=source,
            dst_ref=stage.at[there],
            send_sem=peer_send.at[k, ds - 1],
            recv_sem=peer_recv.at[k, ds - 1],
            device_id=(pos, there),
            device_id_type=MESH,
        )

    lane = lax.broadcasted_iota(jnp.int32, (blocks, LANES), 1)
    row = lax.broadcasted_iota(jnp.int32, (blocks, LANES), 0)
    group_lane = lax.broadcasted_iota(jnp.int32, (group, LANES), 1)
    group_row = lax.broadcasted_iota(jnp.int32, (group, LANES), 0)
    half = SIDE // 2

    def pack_half(h, tile, rows, at, store):
        strip = at // SIDE
        within = at % SIDE
        zero = jnp.zeros((rows, LANES), jnp.float32)
        z_low = z_high = zero
        y_side = [zero, zero]
        for x in range(SIDE):
            part = tile(x, h)
            k, m = divmod(x, half)
            if x == 0:
                store(0, h, part)
            if x == SIDE - 1:
                store(1, h, part)
            z_low = jnp.where(within == x, pltpu.roll(part, x, 1), z_low)
            z_high = jnp.where(within == x, pltpu.roll(part, (x - SIDE + 1) % LANES, 1), z_high)
            shift = SIDE * (m + h) % LANES
            y_side[k] = jnp.where(strip == m, pltpu.roll(part, shift, 1), y_side[k])
        store(4, h, z_low)
        store(5, h, z_high)
        for k in range(2):
            store(2 + h, k, y_side[k])

    def pack(tile, rows, at, store):
        for h in range(2):
            pack_half(h, tile, rows, at, store)

    def half_spot(d, h):
        tile = {0: 0, 1: 1, 4: 2, 5: 3}[d] if d not in (2, 3) else 4 + h
        return slice(tile * LANES, (tile + 1) * LANES)

    def spot(d, h):
        return slice(d * FACE + h * LANES, d * FACE + (h + 1) * LANES)

    def cells(x, h, shift=0):
        return pl.ds((x + shift) * FACE + h * LANES, LANES)

    def each_x(body):
        def several(i, carried):
            for k in range(UNROLL):
                body(pl.multiple_of(i * (UNROLL * FACE), FACE), k)
            return carried

        lax.fori_loop(0, SIDE // UNROLL, several, 0)

    def at_x(first, k, h, shift=0):
        return pl.ds(pl.multiple_of(first + (k + shift) * FACE + h * LANES, LANES), LANES)

    own_slot = nsub + sub
    own_copies[0].wait()

    def store_raw(d, h, value):
        raw[own_slot, :, spot(d, h)] = value

    pack(lambda x, h: stage_p[sub, :, cells(x, h)], blocks, lane, store_raw)
    own_slots.wait()
    slots = jnp.zeros((blocks, LANES), jnp.int32)
    for j in range(blocks):
        slots = jnp.where(row == j, slot_ref[j], slots)
    raw[own_slot, :, FACES * FACE :] = slots.astype(jnp.float32)

    def raw_copy(t, ds):
        there = lax.rem(sub + ds, nsub)
        return pltpu.make_async_remote_copy(
            src_ref=raw.at[own_slot],
            dst_ref=raw.at[(1 - t) * nsub + sub],
            send_sem=raw_send.at[(1 + t) * nsub + there],
            recv_sem=raw_recv.at[(1 - t) * nsub + sub],
            device_id=(pos + t, there),
            device_id_type=MESH,
        )

    def raw_landing(t, ds):
        there = lax.rem(sub + ds, nsub)
        slot = (1 + t) * nsub + there
        return pltpu.make_async_remote_copy(
            src_ref=raw.at[own_slot],
            dst_ref=raw.at[slot],
            send_sem=raw_send.at[slot],
            recv_sem=raw_recv.at[slot],
            device_id=(pos + t, there),
            device_id_type=MESH,
        )

    def link_copy(t):
        return pltpu.make_async_remote_copy(
            src_ref=link_hbm,
            dst_ref=near_links.at[(1 - t) // 2],
            send_sem=link_send.at[(1 + t) // 2],
            recv_sem=link_recv.at[(1 - t) // 2],
            device_id=(pos + t, sub),
            device_id_type=MESH,
        )

    def link_landing(t):
        return pltpu.make_async_remote_copy(
            src_ref=link_hbm,
            dst_ref=near_links.at[(1 + t) // 2],
            send_sem=link_send.at[(1 + t) // 2],
            recv_sem=link_recv.at[(1 + t) // 2],
            device_id=(pos + t, sub),
            device_id_type=MESH,
        )

    raw_partners = [(t, ds) for t in (-1, 1, 0) for ds in range(nsub) if t or ds]
    pl.semaphore_wait(barrier, expected)
    for t in near:

        @pl.when(exists(t))
        def _(t=t):
            for ds in range(nsub):
                raw_copy(t, ds).start()
            link_copy(t).start()

    for ds in range(1, nsub):
        raw_copy(0, ds).start()
    for k in range(len(inputs)):
        for ds in range(1, nsub):
            peer_copy(ds, k).start()

    for copy in own_copies[1:]:
        copy.wait()
    for t, ds in raw_partners:
        if t == 0:
            raw_landing(t, ds).wait_recv()
    order = group_row.astype(jnp.float32)

    def chosen(t):
        return [
            (s, j, raw[(1 + t) * nsub + s, j : j + 1, FACES * FACE :] == order)
            for s in range(nsub)
            for j in range(blocks)
        ]

    picks = chosen(0)
    field[:, 0:FACE] = jnp.zeros((group, FACE), jnp.float32)
    field[:, (SIDE + 1) * FACE :] = jnp.zeros((group, FACE), jnp.float32)
    for k in range(3):
        for ds in range(1, nsub):
            peer_landing(ds, k).wait_recv()

    def regrid(first, k):
        for h in range(2):
            for stage, target, shift in ((stage_p, field, 1), (stage_f, mf, 0), (stage_c, mc, 0)):
                total = jnp.zeros((group, LANES), jnp.float32)
                for s, j, pick in picks:
                    total = jnp.where(pick, stage[s, j : j + 1, at_x(first, k, h)], total)
                target[:, at_x(first, k, h, shift)] = total
                if target is mc:
                    inv[:, at_x(first, k, h)] = relaxation / (6.0 + total)

    each_x(regrid)
    for ds in range(1, nsub):
        peer_landing(ds, len(inputs) - 1).wait_recv()

    start = (pos - 1) * group
    places = []
    for s in range(nsub):
        for b in range(blocks):
            for d in range(FACES):
                link = link_ref[s, b, d]
                place = jnp.where(link < 0, wall, jnp.clip(link - start, 0, wall - 1))
                places.append((s * blocks + b, d, place))

    def gather(window):
        for b, d, place in places:
            flipped = FLIP[d]
            ghosts[d, pl.ds(b, 1), :] = window[
                pl.ds(place, 1), flipped * FACE : (flipped + 1) * FACE
            ]

    def gather_half(h):
        for b, d, place in places:
            flipped = FLIP[d]
            if flipped in (2, 3):
                if flipped == 2 + h:
                    ghosts[d, pl.ds(b, 1), :] = windows[h][pl.ds(place, 1), 4 * LANES : 6 * LANES]
            else:
                first_lane = half_spot(flipped, h).start
                pair = windows[h][pl.ds(place, 1), first_lane : first_lane + FACE]
                ghosts[d, pl.ds(b, 1), h * LANES : (h + 1) * LANES] = pair[:, :LANES]

    strip = group_lane // SIDE
    within = group_lane % SIDE

    def interior(first, k):
        def tile(shift, h):
            return field[:, at_x(first, k, h, 1 + shift)]

        part = tile(0, 0), tile(0, 1)
        up = [pltpu.roll(v, SIDE, 1) for v in part]
        down = [pltpu.roll(v, LANES - SIDE, 1) for v in part]
        for h in range(2):
            total = jnp.where(within == 0, 0.0, pltpu.roll(part[h], 1, 1))
            total = total + jnp.where(within == SIDE - 1, 0.0, pltpu.roll(part[h], LANES - 1, 1))
            total = total + jnp.where(strip == 0, up[0] if h else 0.0, up[h])
            total = total + jnp.where(strip == half - 1, 0.0 if h else down[1], down[h])
            total = total + tile(-1, h) + tile(1, h)
            here = at_x(first, k, h)
            base[:, here] = (1.0 - relaxation) * part[h] + inv[:, here] * (mf[:, here] + total)

    def outside(x, h, ghost, at):
        strip = at // SIDE
        within = at % SIDE
        k, m = divmod(x, half)
        halves = slice(h * LANES, (h + 1) * LANES)
        total = jnp.where(within == 0, pltpu.roll(ghost(4, halves), (-x) % LANES, 1), 0.0)
        total = jnp.where(
            within == SIDE - 1, pltpu.roll(ghost(5, halves), SIDE - 1 - x, 1), total
        )
        source = slice(k * LANES, (k + 1) * LANES)
        if h == 0:
            side = pltpu.roll(ghost(2, source), (-SIDE * m) % LANES, 1)
            total = total + jnp.where(strip == 0, side, 0.0)
        else:
            side = pltpu.roll(ghost(3, source), SIDE * (half - 1 - m), 1)
            total = total + jnp.where(strip == half - 1, side, 0.0)
        if x == 0:
            total = total + ghost(0, halves)
        if x == SIDE - 1:
            total = total + ghost(1, halves)
        return total

    def group_ghost(d, at):
        return ghosts[d, :, at]

    def prepare():
        each_x(interior)

    prepare()

    size = SIDE * FACE
    links = jnp.zeros((group, LANES), jnp.int32)
    for s in range(nsub):
        for b in range(blocks):
            for d in range(FACES):
                links = jnp.where(
                    (group_row == s * blocks + b) & (group_lane == d), link_ref[s, b, d], links
                )
    links = links.astype(jnp.float32)
    added = jnp.zeros((group, LANES), jnp.float32)
    for x in range(SIDE):
        for h in range(2):
            added = added + mc[:, cells(x, h)]
    block_diag = 6.0 + jnp.sum(added, axis=1, keepdims=True) / size
    message = jnp.where(group_lane == FACES + 1, block_diag, links)

    for t in (0, -1, 1):
        if t:

            @pl.when(exists(t))
            def _(t=t):
                for ds in range(nsub):
                    raw_landing(t, ds).wait_recv()

        picks = chosen(t)
        for d in range(FACES):
            for h in range(2):
                total = jnp.zeros((group, LANES), jnp.float32)
                for s, j, pick in picks:
                    total = jnp.where(
                        pick, raw[(1 + t) * nsub + s, j : j + 1, spot(d, h)], total
                    )
                first[(1 + t) * group : (2 + t) * group, spot(d, h)] = total
    gather(first)

    def face_copy(t, h):
        return pltpu.make_async_remote_copy(
            src_ref=windows[h].at[pl.ds(group, group)],
            dst_ref=windows[h].at[pl.ds((1 - t) * group, group)],
            send_sem=face_send.at[h, 1 + t],
            recv_sem=face_recv.at[h, 1 - t],
            device_id=(pos + t, sub),
            device_id_type=MESH,
        )

    def face_landing(t, h):
        return pltpu.make_async_remote_copy(
            src_ref=windows[h].at[pl.ds(group, group)],
            dst_ref=windows[h].at[pl.ds((1 + t) * group, group)],
            send_sem=face_send.at[h, 1 + t],
            recv_sem=face_recv.at[h, 1 + t],
            device_id=(pos + t, sub),
            device_id_type=MESH,
        )

    def coarse_copy(t):
        return pltpu.make_async_remote_copy(
            src_ref=coarse.at[reach],
            dst_ref=coarse.at[reach - t],
            send_sem=coarse_send.at[reach + t],
            recv_sem=coarse_recv.at[reach - t],
            device_id=(pos + t, sub),
            device_id_type=MESH,
        )

    def coarse_landing(t):
        return pltpu.make_async_remote_copy(
            src_ref=coarse.at[reach],
            dst_ref=coarse.at[reach + t],
            send_sem=coarse_send.at[reach + t],
            recv_sem=coarse_recv.at[reach + t],
            device_id=(pos + t, sub),
            device_id_type=MESH,
        )

    def send_coarse():
        left = jnp.zeros((group, LANES), jnp.float32)
        for x in range(SIDE):
            for h in range(2):
                here = cells(x, h)
                left = left + (mf[:, here] - mc[:, here] * field[:, cells(x, h, 1)])
        block = group_lane % group == group_row
        lanes_row = lax.broadcasted_iota(jnp.int32, (8, LANES), 0)
        sums = jnp.zeros((8, LANES), jnp.float32)
        for d in range(FACES):
            both = last_faces[0:group, spot(d, 0)] + last_faces[0:group, spot(d, 1)]
            left = left - both
            total = jnp.sum(both, axis=1, keepdims=True) / size
            line = jnp.sum(jnp.where(block, total, 0.0), axis=0, keepdims=True)
            sums = jnp.where(lanes_row == d, line, sums)
        own_part = jnp.sum(left, axis=1, keepdims=True) / size
        coarse[reach, 0:group, :] = jnp.where(group_lane == FACES, own_part, message)
        coarse[reach, group : group + 8, :] = sums
        for t in sorted(far, key=lambda t: -abs(t)):
            guarded(t, lambda t=t: coarse_copy(t).start())

    def part_copy(t):
        return pltpu.make_async_remote_copy(
            src_ref=parts_out.at[(1 + t) // 2],
            dst_ref=parts_in.at[(1 - t) // 2],
            send_sem=face_send.at[2, 1 + t],
            recv_sem=face_recv.at[2, 1 - t],
            device_id=(pos + t, sub),
            device_id_type=MESH,
        )

    def part_landing(t):
        return pltpu.make_async_remote_copy(
            src_ref=parts_out.at[(1 + t) // 2],
            dst_ref=parts_in.at[(1 + t) // 2],
            send_sem=face_send.at[2, 1 + t],
            recv_sem=face_recv.at[2, 1 + t],
            device_id=(pos + t, sub),
            device_id_type=MESH,
        )

    def own_rows(link, store):
        for b in range(blocks):
            for d in range(FACES):
                place = link(b, d) - pos * group
                place = jnp.where((place < 0) | (place >= group), group, place)
                flipped = FLIP[d]
                store(
                    d * blocks + b,
                    last_faces[pl.ds(place, 1), flipped * FACE : (flipped + 1) * FACE],
                )

    def send_part(t):
        k = (1 + t) // 2

        def store(place, value):
            parts_out[k, place : place + 1, :] = value

        own_rows(lambda b, d: near_links[k, b, d], store)
        part_copy(t).start()

    def swept(x, h):
        here = cells(x, h)
        fresh = base[:, here] + inv[:, here] * outside(x, h, group_ghost, group_lane)
        field[:, cells(x, h, 1)] = fresh
        return fresh

    for step in range(PRE_SWEEPS):
        if step < PRE_SWEEPS - 1:

            for side in range(2):

                def store_faces(d, h, packed):
                    windows[side][group : 2 * group, half_spot(d, h)] = packed

                pack_half(side, swept, group, group_lane, store_faces)
                for t in near:
                    guarded(t, lambda t=t: face_copy(t, side).start())
            prepare()
            for ds in range(1, nsub):
                for k in range(len(inputs)):
                    peer_copy(ds, k).wait_send()
                raw_copy(0, ds).wait_send()
            for t in near:

                @pl.when(exists(t))
                def _(t=t):
                    for ds in range(nsub):
                        raw_copy(t, ds).wait_send()
                    link_copy(t).wait_send()
                    link_landing(t).wait_recv()
                    face_landing(t, 0).wait_recv()

            gather_half(0)
            for t in near:
                guarded(t, lambda t=t: face_landing(t, 1).wait_recv())
            gather_half(1)
        else:

            def store_last(d, h, packed):
                last_faces[0:group, spot(d, h)] = packed

            pack(swept, group, group_lane, store_last)
            send_coarse()
            for t in near:
                guarded(t, lambda t=t: send_part(t))
            prepare()

    def store_own(place, value):
        own_ghosts[place : place + 1, :] = value

    own_rows(lambda b, d: link_ref[sub, b, d], store_own)
    own_links = jnp.zeros((blocks, LANES), jnp.int32)
    for b in range(blocks):
        for d in range(FACES):
            own_links = jnp.where((row == b) & (lane == d), link_ref[sub, b, d], own_links)
    own_links = own_links.astype(jnp.float32)

    for t in near:
        for side in range(2):
            guarded(t, lambda t=t, side=side: face_copy(t, side).wait_send())
    for t in far:

        @pl.when(exists(t))
        def _(t=t):
            coarse_copy(t).wait_send()
            coarse_landing(t).wait_recv()


    count_near = 2 * reach - 1
    shown = coarse[1 : 1 + count_near, 0:group, :]
    shape = (count_near, group, LANES)
    column = lax.broadcasted_iota(jnp.int32, shape, 2)
    index = (lax.broadcasted_iota(jnp.int32, shape, 0) + 1) * group + lax.broadcasted_iota(
        jnp.int32, shape, 1
    )
    origin = ((pos - reach) * group).astype(jnp.float32)
    numbered = column.astype(jnp.float32) + origin
    face_sums = jnp.zeros((8, LANES), jnp.float32)
    narrow = lax.broadcasted_iota(jnp.int32, (8, LANES), 1)
    for k in range(2 * reach + 1):
        face_sums = jnp.where(narrow // group == k, coarse[k, group : group + 8, :], face_sums)
    linked = jnp.zeros(shape, jnp.float32)
    entering = jnp.zeros(shape, jnp.float32)
    for d in range(FACES):
        link = shown[:, :, d : d + 1]
        hit = (link == numbered) & (link >= 0.0)
        linked = linked + hit.astype(jnp.float32)
        flipped = FLIP[d]
        entering = entering + jnp.where(hit, face_sums[flipped : flipped + 1][None], 0.0)
    residuals = shown[:, :, FACES : FACES + 1] + jnp.sum(entering, axis=2, keepdims=True)
    diags = shown[:, :, FACES + 1 : FACES + 2]
    diags = jnp.where(diags > 0.0, diags, 1.0)

    def own(whole):
        result = whole[:blocks]
        for s in range(1, nsub):
            result = jnp.where(sub == s, whole[s * blocks : (s + 1) * blocks], result)
        return result

    for t in near:

        @pl.when(exists(t))
        def _(t=t):
            part_copy(t).wait_send()
            part_landing(t).wait_recv()

    own_ghosts[...] = own_ghosts[...] + parts_in[0] + parts_in[1]

    def own_ghost(d, at):
        return own_ghosts[d * blocks : (d + 1) * blocks, at]

    for x in range(SIDE):
        for h in range(2):
            here = cells(x, h)
            out_ref[:, here] = own(base[:, here]) + own(inv[:, here]) * outside(
                x, h, own_ghost, lane
            )

    def turned(values, edge):
        kept = slice(edge, count_near - edge)
        spread = jnp.where(index[kept] == column[kept], values, 0.0)
        return jnp.sum(jnp.sum(spread, axis=0), axis=0, keepdims=True)

    scaled = relaxation / diags
    driven = scaled * residuals
    errors = driven
    for step in range(1, COARSE_SWEEPS):
        kept = slice(step, count_near - step)
        around = jnp.sum(linked[kept] * turned(errors, step - 1)[None], axis=2, keepdims=True)
        errors = (1.0 - relaxation) * errors[1:-1] + driven[kept] + scaled[kept] * around
    known = turned(errors, COARSE_SWEEPS - 1)

    own_numbered = lane.astype(jnp.float32) + origin
    own_at = reach * group + sub * blocks + row
    own_error = jnp.sum(jnp.where(lane == own_at, known, 0.0), axis=1, keepdims=True)
    jumps = []
    for d in range(FACES):
        link = own_links[:, d : d + 1]
        hit = (link == own_numbered) & (link >= 0.0)
        jumps.append(jnp.sum(jnp.where(hit, known, 0.0), axis=1, keepdims=True) - own_error)
    own_strip = lane // SIDE
    own_within = lane % SIDE
    plane = jnp.zeros((blocks, LANES), jnp.float32) + 6.0 * own_error
    plane = plane + jnp.where(own_within == 0, jumps[4], 0.0)
    plane = plane + jnp.where(own_within == SIDE - 1, jumps[5], 0.0)
    planes = (
        plane + jnp.where(own_strip == 0, jumps[2], 0.0),
        plane + jnp.where(own_strip == half - 1, jumps[3], 0.0),
    )
    kept = (1.0 - relaxation) * own_error + jnp.zeros((blocks, LANES), jnp.float32)

    for x in range(SIDE):
        for h in range(2):
            here = cells(x, h)
            extra = planes[h]
            if x == 0:
                extra = extra + jumps[0]
            if x == SIDE - 1:
                extra = extra + jumps[1]
            out_ref[:, here] = out_ref[:, here] + (kept + own(inv[:, here]) * extra)


def on_device(pressure, source_term, coefficient, new_slot, face_links):
    blocks, size = pressure.shape
    count = lax.axis_size("curve")
    nsub = lax.axis_size("sub")
    group = nsub * blocks
    others = max(1, nsub - 1)
    stage = pltpu.VMEM((nsub, blocks, size), jnp.float32)
    field = pltpu.VMEM((group, size), jnp.float32)
    padded = pltpu.VMEM((group, size + 2 * FACE), jnp.float32)
    window = pltpu.VMEM((3 * group + 8, FACES * FACE), jnp.float32)
    half_window = pltpu.VMEM((3 * group + 8, FACES * LANES), jnp.float32)
    dma = pltpu.SemaphoreType.DMA
    hbm = pl.BlockSpec(memory_space=pltpu.HBM)
    return pl.pallas_call(
        functools.partial(kernel, count, nsub, blocks),
        out_shape=jax.ShapeDtypeStruct((blocks, size), jnp.float32),
        in_specs=[hbm] * 5,
        out_specs=pl.BlockSpec(memory_space=pltpu.VMEM),
        scratch_shapes=[
            pltpu.SMEM((blocks,), jnp.int32),
            pltpu.SMEM((nsub, blocks, FACES), jnp.int32),
            pltpu.SMEM((2, blocks, FACES), jnp.int32),
            stage,
            stage,
            stage,
            pltpu.VMEM((3 * nsub, blocks, FACES * FACE + LANES), jnp.float32),
            window,
            half_window,
            half_window,
            pltpu.VMEM((group + 8, FACES * FACE), jnp.float32),
            pltpu.VMEM((2, FACES * blocks, FACE), jnp.float32),
            pltpu.VMEM((2, FACES * blocks, FACE), jnp.float32),
            pltpu.VMEM((FACES, group, FACE), jnp.float32),
            pltpu.VMEM((FACES * blocks, FACE), jnp.float32),
            field,
            field,
            field,
            padded,
            field,
            pltpu.VMEM((2 * COARSE_SWEEPS + 3, group + 8, LANES), jnp.float32),
            dma((5,)),
            dma((3 * nsub,)),
            dma((3 * nsub,)),
            dma((3, 3)),
            dma((3, 3)),
            dma((4, others)),
            dma((4, others)),
            dma((2 * COARSE_SWEEPS + 3,)),
            dma((2 * COARSE_SWEEPS + 3,)),
            dma((2,)),
            dma((2,)),
        ],
        compiler_params=pltpu.CompilerParams(
            collective_id=0, has_side_effects=True, vmem_limit_bytes=32 * 1024 * 1024
        ),
    )(
        *(
            pltpu.with_memory_space_constraint(array, pltpu.HBM)
            for array in (new_slot, face_links, pressure, source_term, coefficient)
        )
    )


def solution(mesh):
    placed = (
        P(("curve", "sub"), None),
        P(("curve", "sub"), None),
        P(("curve", "sub"), None),
        P(("curve", "sub")),
        P(("curve", "sub"), None),
    )
    return jax.shard_map(
        on_device, mesh=mesh, in_specs=placed, out_specs=P(("curve", "sub"), None), check_vma=False
    )
```

```python
import functools

import jax
import jax.numpy as jnp
from jax import lax
from jax.experimental import pallas as pl
from jax.experimental.pallas import tpu as pltpu
from jax.sharding import PartitionSpec as P

PRE_SWEEPS = 2
COARSE_SWEEPS = 4
SIDE = 16
GREETED = 3
UNROLL = 4
FACE = SIDE * SIDE
FACES = 6
LANES = 128
FLIP = (1, 0, 3, 2, 5, 4)

relaxation = 0.8
MESH = pl.DeviceIdType.MESH


def kernel(
    count,
    nsub,
    blocks,
    slot_hbm,
    link_hbm,
    p_hbm,
    f_hbm,
    c_hbm,
    out_ref,
    slot_ref,
    link_ref,
    near_links,
    stage_p,
    stage_f,
    stage_c,
    raw,
    first,
    window,
    last_faces,
    parts_out,
    parts_in,
    ghosts,
    own_ghosts,
    mf,
    mc,
    inv,
    field,
    base,
    coarse,
    local_sem,
    raw_send,
    raw_recv,
    face_send,
    face_recv,
    peer_send,
    peer_recv,
    coarse_send,
    coarse_recv,
    link_send,
    link_recv,
):
    pos = lax.axis_index("curve")
    sub = lax.axis_index("sub")
    group = nsub * blocks
    reach = COARSE_SWEEPS + 1
    greeted = GREETED
    wall = 3 * group
    near = (-1, 1)
    far = [t for t in range(-reach, reach + 1) if t]

    def exists(t):
        return (pos + t >= 0) & (pos + t < count)

    def guarded(t, action):
        if t == 0:
            action()
        else:
            pl.when(exists(t))(action)

    inputs = (
        (p_hbm, stage_p),
        (f_hbm, stage_f),
        (c_hbm, stage_c),
        (link_hbm, link_ref),
    )
    own_copies = [
        pltpu.make_async_copy(source, stage.at[sub], local_sem.at[k])
        for k, (source, stage) in enumerate(inputs)
    ]
    own_slots = pltpu.make_async_copy(slot_hbm, slot_ref, local_sem.at[len(inputs)])
    own_copies[0].start()

    barrier = pltpu.get_barrier_semaphore()
    expected = 0
    for t in sorted(range(-greeted, greeted + 1), key=abs):
        for ds in range(nsub if abs(t) <= 1 else 1):
            if t or ds:

                def greet(t=t, ds=ds):
                    pl.semaphore_signal(
                        barrier,
                        inc=1,
                        device_id=(pos + t, lax.rem(sub + ds, nsub)),
                        device_id_type=MESH,
                    )

                guarded(t, greet)
                expected = expected + (exists(t).astype(jnp.int32) if t else 1)

    own_slots.start()
    for copy in own_copies[1:]:
        copy.start()

    def clear(window, rows):
        window[rows] = jnp.zeros((rows.stop - rows.start,) + window.shape[1:], jnp.float32)

    clear(first, slice(wall, wall + 8))
    clear(window, slice(wall, wall + 8))
    clear(last_faces, slice(group, group + 8))
    for t in near:

        @pl.when(jnp.logical_not(exists(t)))
        def _(t=t):
            clear(window, slice((t + 1) * group, (t + 2) * group))
            clear(parts_in, slice((t + 1) // 2, (t + 1) // 2 + 1))
            clear(raw, slice((t + 1) * nsub, (t + 2) * nsub))

    for t in far:

        @pl.when(jnp.logical_not(exists(t)))
        def _(t=t):
            clear(coarse, slice(t + reach, t + reach + 1))

    def peer_copy(ds, k):
        source, stage = inputs[k]
        return pltpu.make_async_remote_copy(
            src_ref=source,
            dst_ref=stage.at[sub],
            send_sem=peer_send.at[k, ds - 1],
            recv_sem=peer_recv.at[k, nsub - ds - 1],
            device_id=(pos, lax.rem(sub + ds, nsub)),
            device_id_type=MESH,
        )

    def peer_landing(ds, k):
        source, stage = inputs[k]
        there = lax.rem(sub + ds, nsub)
        return pltpu.make_async_remote_copy(
            src_ref=source,
            dst_ref=stage.at[there],
            send_sem=peer_send.at[k, ds - 1],
            recv_sem=peer_recv.at[k, ds - 1],
            device_id=(pos, there),
            device_id_type=MESH,
        )

    lane = lax.broadcasted_iota(jnp.int32, (blocks, LANES), 1)
    row = lax.broadcasted_iota(jnp.int32, (blocks, LANES), 0)
    group_lane = lax.broadcasted_iota(jnp.int32, (group, LANES), 1)
    group_row = lax.broadcasted_iota(jnp.int32, (group, LANES), 0)
    half = SIDE // 2

    def pack(tile, rows, at, store):
        strip = at // SIDE
        within = at % SIDE
        zero = jnp.zeros((rows, LANES), jnp.float32)
        y_low = [zero, zero]
        y_high = [zero, zero]
        z_low = [zero, zero]
        z_high = [zero, zero]
        for x in range(SIDE):
            part = tile(x, 0), tile(x, 1)
            k, m = divmod(x, half)
            for h in range(2):
                if x == 0:
                    store(0, h, part[h])
                if x == SIDE - 1:
                    store(1, h, part[h])
                z_low[h] = jnp.where(within == x, pltpu.roll(part[h], x, 1), z_low[h])
                z_high[h] = jnp.where(
                    within == x, pltpu.roll(part[h], (x - SIDE + 1) % LANES, 1), z_high[h]
                )
            y_low[k] = jnp.where(strip == m, pltpu.roll(part[0], SIDE * m, 1), y_low[k])
            y_high[k] = jnp.where(
                strip == m, pltpu.roll(part[1], (SIDE * (m + 1)) % LANES, 1), y_high[k]
            )
        for d, packed in ((2, y_low), (3, y_high), (4, z_low), (5, z_high)):
            for h in range(2):
                store(d, h, packed[h])

    def spot(d, h):
        return slice(d * FACE + h * LANES, d * FACE + (h + 1) * LANES)

    def cells(x, h, shift=0):
        return pl.ds((x + shift) * FACE + h * LANES, LANES)

    def each_x(body):
        def several(i, carried):
            for k in range(UNROLL):
                body(pl.multiple_of(i * (UNROLL * FACE), FACE), k)
            return carried

        lax.fori_loop(0, SIDE // UNROLL, several, 0)

    def at_x(first, k, h, shift=0):
        return pl.ds(pl.multiple_of(first + (k + shift) * FACE + h * LANES, LANES), LANES)

    own_slot = nsub + sub
    own_copies[0].wait()

    def store_raw(d, h, value):
        raw[own_slot, :, spot(d, h)] = value

    pack(lambda x, h: stage_p[sub, :, cells(x, h)], blocks, lane, store_raw)
    own_slots.wait()
    slots = jnp.zeros((blocks, LANES), jnp.int32)
    for j in range(blocks):
        slots = jnp.where(row == j, slot_ref[j], slots)
    raw[own_slot, :, FACES * FACE :] = slots.astype(jnp.float32)

    def raw_copy(t, ds):
        there = lax.rem(sub + ds, nsub)
        return pltpu.make_async_remote_copy(
            src_ref=raw.at[own_slot],
            dst_ref=raw.at[(1 - t) * nsub + sub],
            send_sem=raw_send.at[(1 + t) * nsub + there],
            recv_sem=raw_recv.at[(1 - t) * nsub + sub],
            device_id=(pos + t, there),
            device_id_type=MESH,
        )

    def raw_landing(t, ds):
        there = lax.rem(sub + ds, nsub)
        slot = (1 + t) * nsub + there
        return pltpu.make_async_remote_copy(
            src_ref=raw.at[own_slot],
            dst_ref=raw.at[slot],
            send_sem=raw_send.at[slot],
            recv_sem=raw_recv.at[slot],
            device_id=(pos + t, there),
            device_id_type=MESH,
        )

    def link_copy(t):
        return pltpu.make_async_remote_copy(
            src_ref=link_hbm,
            dst_ref=near_links.at[(1 - t) // 2],
            send_sem=link_send.at[(1 + t) // 2],
            recv_sem=link_recv.at[(1 - t) // 2],
            device_id=(pos + t, sub),
            device_id_type=MESH,
        )

    def link_landing(t):
        return pltpu.make_async_remote_copy(
            src_ref=link_hbm,
            dst_ref=near_links.at[(1 + t) // 2],
            send_sem=link_send.at[(1 + t) // 2],
            recv_sem=link_recv.at[(1 + t) // 2],
            device_id=(pos + t, sub),
            device_id_type=MESH,
        )

    raw_partners = [(t, ds) for t in (-1, 1, 0) for ds in range(nsub) if t or ds]
    pl.semaphore_wait(barrier, expected)
    for t in near:

        @pl.when(exists(t))
        def _(t=t):
            for ds in range(nsub):
                raw_copy(t, ds).start()
            link_copy(t).start()

    for ds in range(1, nsub):
        raw_copy(0, ds).start()
    for k in range(len(inputs)):
        for ds in range(1, nsub):
            peer_copy(ds, k).start()

    for copy in own_copies[1:]:
        copy.wait()
    for t, ds in raw_partners:
        if t == 0:
            raw_landing(t, ds).wait_recv()
    order = group_row.astype(jnp.float32)

    def chosen(t):
        return [
            (s, j, raw[(1 + t) * nsub + s, j : j + 1, FACES * FACE :] == order)
            for s in range(nsub)
            for j in range(blocks)
        ]

    picks = chosen(0)
    field[:, 0:FACE] = jnp.zeros((group, FACE), jnp.float32)
    field[:, (SIDE + 1) * FACE :] = jnp.zeros((group, FACE), jnp.float32)
    for k in range(3):
        for ds in range(1, nsub):
            peer_landing(ds, k).wait_recv()

    def regrid(first, k):
        for h in range(2):
            for stage, target, shift in ((stage_p, field, 1), (stage_f, mf, 0), (stage_c, mc, 0)):
                total = jnp.zeros((group, LANES), jnp.float32)
                for s, j, pick in picks:
                    total = jnp.where(pick, stage[s, j : j + 1, at_x(first, k, h)], total)
                target[:, at_x(first, k, h, shift)] = total
                if target is mc:
                    inv[:, at_x(first, k, h)] = relaxation / (6.0 + total)

    each_x(regrid)
    for ds in range(1, nsub):
        peer_landing(ds, len(inputs) - 1).wait_recv()

    start = (pos - 1) * group
    places = []
    for s in range(nsub):
        for b in range(blocks):
            for d in range(FACES):
                link = link_ref[s, b, d]
                place = jnp.where(link < 0, wall, jnp.clip(link - start, 0, wall - 1))
                places.append((s * blocks + b, d, place))

    def gather(window):
        for b, d, place in places:
            flipped = FLIP[d]
            ghosts[d, pl.ds(b, 1), :] = window[
                pl.ds(place, 1), flipped * FACE : (flipped + 1) * FACE
            ]

    strip = group_lane // SIDE
    within = group_lane % SIDE

    def interior(first, k):
        def tile(shift, h):
            return field[:, at_x(first, k, h, 1 + shift)]

        part = tile(0, 0), tile(0, 1)
        up = [pltpu.roll(v, SIDE, 1) for v in part]
        down = [pltpu.roll(v, LANES - SIDE, 1) for v in part]
        for h in range(2):
            total = jnp.where(within == 0, 0.0, pltpu.roll(part[h], 1, 1))
            total = total + jnp.where(within == SIDE - 1, 0.0, pltpu.roll(part[h], LANES - 1, 1))
            total = total + jnp.where(strip == 0, up[0] if h else 0.0, up[h])
            total = total + jnp.where(strip == half - 1, 0.0 if h else down[1], down[h])
            total = total + tile(-1, h) + tile(1, h)
            here = at_x(first, k, h)
            base[:, here] = (1.0 - relaxation) * part[h] + inv[:, here] * (mf[:, here] + total)

    def outside(x, h, ghost, at):
        strip = at // SIDE
        within = at % SIDE
        k, m = divmod(x, half)
        halves = slice(h * LANES, (h + 1) * LANES)
        total = jnp.where(within == 0, pltpu.roll(ghost(4, halves), (-x) % LANES, 1), 0.0)
        total = jnp.where(
            within == SIDE - 1, pltpu.roll(ghost(5, halves), SIDE - 1 - x, 1), total
        )
        source = slice(k * LANES, (k + 1) * LANES)
        if h == 0:
            side = pltpu.roll(ghost(2, source), (-SIDE * m) % LANES, 1)
            total = total + jnp.where(strip == 0, side, 0.0)
        else:
            side = pltpu.roll(ghost(3, source), SIDE * (half - 1 - m), 1)
            total = total + jnp.where(strip == half - 1, side, 0.0)
        if x == 0:
            total = total + ghost(0, halves)
        if x == SIDE - 1:
            total = total + ghost(1, halves)
        return total

    def group_ghost(d, at):
        return ghosts[d, :, at]

    def prepare():
        each_x(interior)

    prepare()

    size = SIDE * FACE
    links = jnp.zeros((group, LANES), jnp.int32)
    for s in range(nsub):
        for b in range(blocks):
            for d in range(FACES):
                links = jnp.where(
                    (group_row == s * blocks + b) & (group_lane == d), link_ref[s, b, d], links
                )
    links = links.astype(jnp.float32)
    added = jnp.zeros((group, LANES), jnp.float32)
    for x in range(SIDE):
        for h in range(2):
            added = added + mc[:, cells(x, h)]
    block_diag = 6.0 + jnp.sum(added, axis=1, keepdims=True) / size
    message = jnp.where(group_lane == FACES + 1, block_diag, links)

    for t in (0, -1, 1):
        if t:

            @pl.when(exists(t))
            def _(t=t):
                for ds in range(nsub):
                    raw_landing(t, ds).wait_recv()

        picks = chosen(t)
        for d in range(FACES):
            for h in range(2):
                total = jnp.zeros((group, LANES), jnp.float32)
                for s, j, pick in picks:
                    total = jnp.where(
                        pick, raw[(1 + t) * nsub + s, j : j + 1, spot(d, h)], total
                    )
                first[(1 + t) * group : (2 + t) * group, spot(d, h)] = total
    gather(first)

    def face_copy(t):
        return pltpu.make_async_remote_copy(
            src_ref=window.at[pl.ds(group, group)],
            dst_ref=window.at[pl.ds((1 - t) * group, group)],
            send_sem=face_send.at[0, 1 + t],
            recv_sem=face_recv.at[0, 1 - t],
            device_id=(pos + t, sub),
            device_id_type=MESH,
        )

    def face_landing(t):
        return pltpu.make_async_remote_copy(
            src_ref=window.at[pl.ds(group, group)],
            dst_ref=window.at[pl.ds((1 + t) * group, group)],
            send_sem=face_send.at[0, 1 + t],
            recv_sem=face_recv.at[0, 1 + t],
            device_id=(pos + t, sub),
            device_id_type=MESH,
        )

    def coarse_copy(t):
        return pltpu.make_async_remote_copy(
            src_ref=coarse.at[reach],
            dst_ref=coarse.at[reach - t],
            send_sem=coarse_send.at[reach + t],
            recv_sem=coarse_recv.at[reach - t],
            device_id=(pos + t, sub),
            device_id_type=MESH,
        )

    def coarse_landing(t):
        return pltpu.make_async_remote_copy(
            src_ref=coarse.at[reach],
            dst_ref=coarse.at[reach + t],
            send_sem=coarse_send.at[reach + t],
            recv_sem=coarse_recv.at[reach + t],
            device_id=(pos + t, sub),
            device_id_type=MESH,
        )

    def send_coarse():
        left = jnp.zeros((group, LANES), jnp.float32)
        for x in range(SIDE):
            for h in range(2):
                here = cells(x, h)
                left = left + (mf[:, here] - mc[:, here] * field[:, cells(x, h, 1)])
        block = group_lane % group == group_row
        lanes_row = lax.broadcasted_iota(jnp.int32, (8, LANES), 0)
        sums = jnp.zeros((8, LANES), jnp.float32)
        for d in range(FACES):
            both = last_faces[0:group, spot(d, 0)] + last_faces[0:group, spot(d, 1)]
            left = left - both
            total = jnp.sum(both, axis=1, keepdims=True) / size
            line = jnp.sum(jnp.where(block, total, 0.0), axis=0, keepdims=True)
            sums = jnp.where(lanes_row == d, line, sums)
        own_part = jnp.sum(left, axis=1, keepdims=True) / size
        coarse[reach, 0:group, :] = jnp.where(group_lane == FACES, own_part, message)
        coarse[reach, group : group + 8, :] = sums
        for t in sorted(far, key=lambda t: -abs(t)):
            guarded(t, lambda t=t: coarse_copy(t).start())

    def part_copy(t):
        return pltpu.make_async_remote_copy(
            src_ref=parts_out.at[(1 + t) // 2],
            dst_ref=parts_in.at[(1 - t) // 2],
            send_sem=face_send.at[1, 1 + t],
            recv_sem=face_recv.at[1, 1 - t],
            device_id=(pos + t, sub),
            device_id_type=MESH,
        )

    def part_landing(t):
        return pltpu.make_async_remote_copy(
            src_ref=parts_out.at[(1 + t) // 2],
            dst_ref=parts_in.at[(1 + t) // 2],
            send_sem=face_send.at[1, 1 + t],
            recv_sem=face_recv.at[1, 1 + t],
            device_id=(pos + t, sub),
            device_id_type=MESH,
        )

    def own_rows(link, store):
        for b in range(blocks):
            for d in range(FACES):
                place = link(b, d) - pos * group
                place = jnp.where((place < 0) | (place >= group), group, place)
                flipped = FLIP[d]
                store(
                    d * blocks + b,
                    last_faces[pl.ds(place, 1), flipped * FACE : (flipped + 1) * FACE],
                )

    def send_part(t):
        k = (1 + t) // 2

        def store(place, value):
            parts_out[k, place : place + 1, :] = value

        own_rows(lambda b, d: near_links[k, b, d], store)
        part_copy(t).start()

    def swept(x, h):
        here = cells(x, h)
        fresh = base[:, here] + inv[:, here] * outside(x, h, group_ghost, group_lane)
        field[:, cells(x, h, 1)] = fresh
        return fresh

    for step in range(PRE_SWEEPS):
        if step < PRE_SWEEPS - 1:

            def store_faces(d, h, packed):
                window[group : 2 * group, spot(d, h)] = packed

            pack(swept, group, group_lane, store_faces)
            for t in near:
                guarded(t, lambda t=t: face_copy(t).start())
            prepare()
            for ds in range(1, nsub):
                for k in range(len(inputs)):
                    peer_copy(ds, k).wait_send()
                raw_copy(0, ds).wait_send()
            for t in near:

                @pl.when(exists(t))
                def _(t=t):
                    for ds in range(nsub):
                        raw_copy(t, ds).wait_send()
                    link_copy(t).wait_send()
                    link_landing(t).wait_recv()
                    face_landing(t).wait_recv()

            gather(window)
        else:

            def store_last(d, h, packed):
                last_faces[0:group, spot(d, h)] = packed

            pack(swept, group, group_lane, store_last)
            send_coarse()
            for t in near:
                guarded(t, lambda t=t: send_part(t))
            prepare()

    def store_own(place, value):
        own_ghosts[place : place + 1, :] = value

    own_rows(lambda b, d: link_ref[sub, b, d], store_own)
    own_links = jnp.zeros((blocks, LANES), jnp.int32)
    for b in range(blocks):
        for d in range(FACES):
            own_links = jnp.where((row == b) & (lane == d), link_ref[sub, b, d], own_links)
    own_links = own_links.astype(jnp.float32)

    for t in near:
        guarded(t, lambda t=t: face_copy(t).wait_send())
    for t in far:

        @pl.when(exists(t))
        def _(t=t):
            coarse_copy(t).wait_send()
            coarse_landing(t).wait_recv()


    count_near = 2 * reach - 1
    shown = coarse[1 : 1 + count_near, 0:group, :]
    shape = (count_near, group, LANES)
    column = lax.broadcasted_iota(jnp.int32, shape, 2)
    index = (lax.broadcasted_iota(jnp.int32, shape, 0) + 1) * group + lax.broadcasted_iota(
        jnp.int32, shape, 1
    )
    origin = ((pos - reach) * group).astype(jnp.float32)
    numbered = column.astype(jnp.float32) + origin
    face_sums = jnp.zeros((8, LANES), jnp.float32)
    narrow = lax.broadcasted_iota(jnp.int32, (8, LANES), 1)
    for k in range(2 * reach + 1):
        face_sums = jnp.where(narrow // group == k, coarse[k, group : group + 8, :], face_sums)
    linked = jnp.zeros(shape, jnp.float32)
    entering = jnp.zeros(shape, jnp.float32)
    for d in range(FACES):
        link = shown[:, :, d : d + 1]
        hit = (link == numbered) & (link >= 0.0)
        linked = linked + hit.astype(jnp.float32)
        flipped = FLIP[d]
        entering = entering + jnp.where(hit, face_sums[flipped : flipped + 1][None], 0.0)
    residuals = shown[:, :, FACES : FACES + 1] + jnp.sum(entering, axis=2, keepdims=True)
    diags = shown[:, :, FACES + 1 : FACES + 2]
    diags = jnp.where(diags > 0.0, diags, 1.0)

    def own(whole):
        result = whole[:blocks]
        for s in range(1, nsub):
            result = jnp.where(sub == s, whole[s * blocks : (s + 1) * blocks], result)
        return result

    for t in near:

        @pl.when(exists(t))
        def _(t=t):
            part_copy(t).wait_send()
            part_landing(t).wait_recv()

    own_ghosts[...] = own_ghosts[...] + parts_in[0] + parts_in[1]

    def own_ghost(d, at):
        return own_ghosts[d * blocks : (d + 1) * blocks, at]

    for x in range(SIDE):
        for h in range(2):
            here = cells(x, h)
            out_ref[:, here] = own(base[:, here]) + own(inv[:, here]) * outside(
                x, h, own_ghost, lane
            )

    def turned(values, edge):
        kept = slice(edge, count_near - edge)
        spread = jnp.where(index[kept] == column[kept], values, 0.0)
        return jnp.sum(jnp.sum(spread, axis=0), axis=0, keepdims=True)

    scaled = relaxation / diags
    driven = scaled * residuals
    errors = driven
    for step in range(1, COARSE_SWEEPS):
        kept = slice(step, count_near - step)
        around = jnp.sum(linked[kept] * turned(errors, step - 1)[None], axis=2, keepdims=True)
        errors = (1.0 - relaxation) * errors[1:-1] + driven[kept] + scaled[kept] * around
    known = turned(errors, COARSE_SWEEPS - 1)

    own_numbered = lane.astype(jnp.float32) + origin
    own_at = reach * group + sub * blocks + row
    own_error = jnp.sum(jnp.where(lane == own_at, known, 0.0), axis=1, keepdims=True)
    jumps = []
    for d in range(FACES):
        link = own_links[:, d : d + 1]
        hit = (link == own_numbered) & (link >= 0.0)
        jumps.append(jnp.sum(jnp.where(hit, known, 0.0), axis=1, keepdims=True) - own_error)
    own_strip = lane // SIDE
    own_within = lane % SIDE
    plane = jnp.zeros((blocks, LANES), jnp.float32) + 6.0 * own_error
    plane = plane + jnp.where(own_within == 0, jumps[4], 0.0)
    plane = plane + jnp.where(own_within == SIDE - 1, jumps[5], 0.0)
    planes = (
        plane + jnp.where(own_strip == 0, jumps[2], 0.0),
        plane + jnp.where(own_strip == half - 1, jumps[3], 0.0),
    )
    kept = (1.0 - relaxation) * own_error + jnp.zeros((blocks, LANES), jnp.float32)

    for x in range(SIDE):
        for h in range(2):
            here = cells(x, h)
            extra = planes[h]
            if x == 0:
                extra = extra + jumps[0]
            if x == SIDE - 1:
                extra = extra + jumps[1]
            out_ref[:, here] = out_ref[:, here] + (kept + own(inv[:, here]) * extra)


def on_device(pressure, source_term, coefficient, new_slot, face_links):
    blocks, size = pressure.shape
    count = lax.axis_size("curve")
    nsub = lax.axis_size("sub")
    group = nsub * blocks
    others = max(1, nsub - 1)
    stage = pltpu.VMEM((nsub, blocks, size), jnp.float32)
    field = pltpu.VMEM((group, size), jnp.float32)
    padded = pltpu.VMEM((group, size + 2 * FACE), jnp.float32)
    window = pltpu.VMEM((3 * group + 8, FACES * FACE), jnp.float32)
    dma = pltpu.SemaphoreType.DMA
    hbm = pl.BlockSpec(memory_space=pltpu.HBM)
    return pl.pallas_call(
        functools.partial(kernel, count, nsub, blocks),
        out_shape=jax.ShapeDtypeStruct((blocks, size), jnp.float32),
        in_specs=[hbm] * 5,
        out_specs=pl.BlockSpec(memory_space=pltpu.VMEM),
        scratch_shapes=[
            pltpu.SMEM((blocks,), jnp.int32),
            pltpu.SMEM((nsub, blocks, FACES), jnp.int32),
            pltpu.SMEM((2, blocks, FACES), jnp.int32),
            stage,
            stage,
            stage,
            pltpu.VMEM((3 * nsub, blocks, FACES * FACE + LANES), jnp.float32),
            window,
            window,
            pltpu.VMEM((group + 8, FACES * FACE), jnp.float32),
            pltpu.VMEM((2, FACES * blocks, FACE), jnp.float32),
            pltpu.VMEM((2, FACES * blocks, FACE), jnp.float32),
            pltpu.VMEM((FACES, group, FACE), jnp.float32),
            pltpu.VMEM((FACES * blocks, FACE), jnp.float32),
            field,
            field,
            field,
            padded,
            field,
            pltpu.VMEM((2 * COARSE_SWEEPS + 3, group + 8, LANES), jnp.float32),
            dma((5,)),
            dma((3 * nsub,)),
            dma((3 * nsub,)),
            dma((PRE_SWEEPS, 3)),
            dma((PRE_SWEEPS, 3)),
            dma((4, others)),
            dma((4, others)),
            dma((2 * COARSE_SWEEPS + 3,)),
            dma((2 * COARSE_SWEEPS + 3,)),
            dma((2,)),
            dma((2,)),
        ],
        compiler_params=pltpu.CompilerParams(
            collective_id=0, has_side_effects=True, vmem_limit_bytes=32 * 1024 * 1024
        ),
    )(
        *(
            pltpu.with_memory_space_constraint(array, pltpu.HBM)
            for array in (new_slot, face_links, pressure, source_term, coefficient)
        )
    )


def solution(mesh):
    placed = (
        P(("curve", "sub"), None),
        P(("curve", "sub"), None),
        P(("curve", "sub"), None),
        P(("curve", "sub")),
        P(("curve", "sub"), None),
    )
    return jax.shard_map(
        on_device, mesh=mesh, in_specs=placed, out_specs=P(("curve", "sub"), None), check_vma=False
    )
```

```python
import functools

import jax
import jax.numpy as jnp
from jax import lax
from jax.experimental import pallas as pl
from jax.experimental.pallas import tpu as pltpu
from jax.sharding import PartitionSpec as P

PRE_SWEEPS = 2
COARSE_SWEEPS = 4
SIDE = 16
GREETED = 3
UNROLL = 8
FACE = SIDE * SIDE
FACES = 6
LANES = 128
FLIP = (1, 0, 3, 2, 5, 4)

relaxation = 0.8
MESH = pl.DeviceIdType.MESH


def kernel(
    count,
    nsub,
    blocks,
    slot_hbm,
    link_hbm,
    p_hbm,
    f_hbm,
    c_hbm,
    out_ref,
    slot_ref,
    link_ref,
    near_links,
    stage_p,
    stage_f,
    stage_c,
    raw,
    first,
    window,
    last_faces,
    parts_out,
    parts_in,
    ghosts,
    own_ghosts,
    mf,
    mc,
    inv,
    field,
    base,
    coarse,
    local_sem,
    raw_send,
    raw_recv,
    face_send,
    face_recv,
    peer_send,
    peer_recv,
    coarse_send,
    coarse_recv,
    link_send,
    link_recv,
):
    pos = lax.axis_index("curve")
    sub = lax.axis_index("sub")
    group = nsub * blocks
    reach = COARSE_SWEEPS + 1
    greeted = GREETED
    wall = 3 * group
    near = (-1, 1)
    far = [t for t in range(-reach, reach + 1) if t]

    def exists(t):
        return (pos + t >= 0) & (pos + t < count)

    def guarded(t, action):
        if t == 0:
            action()
        else:
            pl.when(exists(t))(action)

    inputs = (
        (p_hbm, stage_p),
        (f_hbm, stage_f),
        (c_hbm, stage_c),
        (link_hbm, link_ref),
    )
    own_copies = [
        pltpu.make_async_copy(source, stage.at[sub], local_sem.at[k])
        for k, (source, stage) in enumerate(inputs)
    ]
    own_slots = pltpu.make_async_copy(slot_hbm, slot_ref, local_sem.at[len(inputs)])
    own_copies[0].start()

    barrier = pltpu.get_barrier_semaphore()
    expected = 0
    for t in sorted(range(-greeted, greeted + 1), key=abs):
        for ds in range(nsub if abs(t) <= 1 else 1):
            if t or ds:

                def greet(t=t, ds=ds):
                    pl.semaphore_signal(
                        barrier,
                        inc=1,
                        device_id=(pos + t, lax.rem(sub + ds, nsub)),
                        device_id_type=MESH,
                    )

                guarded(t, greet)
                expected = expected + (exists(t).astype(jnp.int32) if t else 1)

    own_slots.start()
    for copy in own_copies[1:]:
        copy.start()

    def clear(window, rows):
        window[rows] = jnp.zeros((rows.stop - rows.start,) + window.shape[1:], jnp.float32)

    clear(first, slice(wall, wall + 8))
    clear(window, slice(wall, wall + 8))
    clear(last_faces, slice(group, group + 8))
    for t in near:

        @pl.when(jnp.logical_not(exists(t)))
        def _(t=t):
            clear(window, slice((t + 1) * group, (t + 2) * group))
            clear(parts_in, slice((t + 1) // 2, (t + 1) // 2 + 1))
            clear(raw, slice((t + 1) * nsub, (t + 2) * nsub))

    for t in far:

        @pl.when(jnp.logical_not(exists(t)))
        def _(t=t):
            clear(coarse, slice(t + reach, t + reach + 1))

    def peer_copy(ds, k):
        source, stage = inputs[k]
        return pltpu.make_async_remote_copy(
            src_ref=source,
            dst_ref=stage.at[sub],
            send_sem=peer_send.at[k, ds - 1],
            recv_sem=peer_recv.at[k, nsub - ds - 1],
            device_id=(pos, lax.rem(sub + ds, nsub)),
            device_id_type=MESH,
        )

    def peer_landing(ds, k):
        source, stage = inputs[k]
        there = lax.rem(sub + ds, nsub)
        return pltpu.make_async_remote_copy(
            src_ref=source,
            dst_ref=stage.at[there],
            send_sem=peer_send.at[k, ds - 1],
            recv_sem=peer_recv.at[k, ds - 1],
            device_id=(pos, there),
            device_id_type=MESH,
        )

    lane = lax.broadcasted_iota(jnp.int32, (blocks, LANES), 1)
    row = lax.broadcasted_iota(jnp.int32, (blocks, LANES), 0)
    group_lane = lax.broadcasted_iota(jnp.int32, (group, LANES), 1)
    group_row = lax.broadcasted_iota(jnp.int32, (group, LANES), 0)
    half = SIDE // 2

    def pack(tile, rows, at, store):
        strip = at // SIDE
        within = at % SIDE
        zero = jnp.zeros((rows, LANES), jnp.float32)
        y_low = [zero, zero]
        y_high = [zero, zero]
        z_low = [zero, zero]
        z_high = [zero, zero]
        for x in range(SIDE):
            part = tile(x, 0), tile(x, 1)
            k, m = divmod(x, half)
            for h in range(2):
                if x == 0:
                    store(0, h, part[h])
                if x == SIDE - 1:
                    store(1, h, part[h])
                z_low[h] = jnp.where(within == x, pltpu.roll(part[h], x, 1), z_low[h])
                z_high[h] = jnp.where(
                    within == x, pltpu.roll(part[h], (x - SIDE + 1) % LANES, 1), z_high[h]
                )
            y_low[k] = jnp.where(strip == m, pltpu.roll(part[0], SIDE * m, 1), y_low[k])
            y_high[k] = jnp.where(
                strip == m, pltpu.roll(part[1], (SIDE * (m + 1)) % LANES, 1), y_high[k]
            )
        for d, packed in ((2, y_low), (3, y_high), (4, z_low), (5, z_high)):
            for h in range(2):
                store(d, h, packed[h])

    def spot(d, h):
        return slice(d * FACE + h * LANES, d * FACE + (h + 1) * LANES)

    def cells(x, h, shift=0):
        return pl.ds((x + shift) * FACE + h * LANES, LANES)

    def each_x(body):
        def several(i, carried):
            for k in range(UNROLL):
                body(pl.multiple_of(i * (UNROLL * FACE), FACE), k)
            return carried

        lax.fori_loop(0, SIDE // UNROLL, several, 0)

    def at_x(first, k, h, shift=0):
        return pl.ds(pl.multiple_of(first + (k + shift) * FACE + h * LANES, LANES), LANES)

    own_slot = nsub + sub
    own_copies[0].wait()

    def store_raw(d, h, value):
        raw[own_slot, :, spot(d, h)] = value

    pack(lambda x, h: stage_p[sub, :, cells(x, h)], blocks, lane, store_raw)
    own_slots.wait()
    slots = jnp.zeros((blocks, LANES), jnp.int32)
    for j in range(blocks):
        slots = jnp.where(row == j, slot_ref[j], slots)
    raw[own_slot, :, FACES * FACE :] = slots.astype(jnp.float32)

    def raw_copy(t, ds):
        there = lax.rem(sub + ds, nsub)
        return pltpu.make_async_remote_copy(
            src_ref=raw.at[own_slot],
            dst_ref=raw.at[(1 - t) * nsub + sub],
            send_sem=raw_send.at[(1 + t) * nsub + there],
            recv_sem=raw_recv.at[(1 - t) * nsub + sub],
            device_id=(pos + t, there),
            device_id_type=MESH,
        )

    def raw_landing(t, ds):
        there = lax.rem(sub + ds, nsub)
        slot = (1 + t) * nsub + there
        return pltpu.make_async_remote_copy(
            src_ref=raw.at[own_slot],
            dst_ref=raw.at[slot],
            send_sem=raw_send.at[slot],
            recv_sem=raw_recv.at[slot],
            device_id=(pos + t, there),
            device_id_type=MESH,
        )

    def link_copy(t):
        return pltpu.make_async_remote_copy(
            src_ref=link_hbm,
            dst_ref=near_links.at[(1 - t) // 2],
            send_sem=link_send.at[(1 + t) // 2],
            recv_sem=link_recv.at[(1 - t) // 2],
            device_id=(pos + t, sub),
            device_id_type=MESH,
        )

    def link_landing(t):
        return pltpu.make_async_remote_copy(
            src_ref=link_hbm,
            dst_ref=near_links.at[(1 + t) // 2],
            send_sem=link_send.at[(1 + t) // 2],
            recv_sem=link_recv.at[(1 + t) // 2],
            device_id=(pos + t, sub),
            device_id_type=MESH,
        )

    raw_partners = [(t, ds) for t in (-1, 1, 0) for ds in range(nsub) if t or ds]
    pl.semaphore_wait(barrier, expected)
    for t in near:

        @pl.when(exists(t))
        def _(t=t):
            for ds in range(nsub):
                raw_copy(t, ds).start()
            link_copy(t).start()

    for ds in range(1, nsub):
        raw_copy(0, ds).start()
    for k in range(len(inputs)):
        for ds in range(1, nsub):
            peer_copy(ds, k).start()

    for copy in own_copies[1:]:
        copy.wait()
    for t, ds in raw_partners:
        if t == 0:
            raw_landing(t, ds).wait_recv()
    order = group_row.astype(jnp.float32)

    def chosen(t):
        return [
            (s, j, raw[(1 + t) * nsub + s, j : j + 1, FACES * FACE :] == order)
            for s in range(nsub)
            for j in range(blocks)
        ]

    picks = chosen(0)
    field[:, 0:FACE] = jnp.zeros((group, FACE), jnp.float32)
    field[:, (SIDE + 1) * FACE :] = jnp.zeros((group, FACE), jnp.float32)
    for k in range(3):
        for ds in range(1, nsub):
            peer_landing(ds, k).wait_recv()

    def regrid(first, k):
        for h in range(2):
            for stage, target, shift in ((stage_p, field, 1), (stage_f, mf, 0), (stage_c, mc, 0)):
                total = jnp.zeros((group, LANES), jnp.float32)
                for s, j, pick in picks:
                    total = jnp.where(pick, stage[s, j : j + 1, at_x(first, k, h)], total)
                target[:, at_x(first, k, h, shift)] = total
                if target is mc:
                    inv[:, at_x(first, k, h)] = relaxation / (6.0 + total)

    each_x(regrid)
    for ds in range(1, nsub):
        peer_landing(ds, len(inputs) - 1).wait_recv()

    start = (pos - 1) * group
    places = []
    for s in range(nsub):
        for b in range(blocks):
            for d in range(FACES):
                link = link_ref[s, b, d]
                place = jnp.where(link < 0, wall, jnp.clip(link - start, 0, wall - 1))
                places.append((s * blocks + b, d, place))

    def gather(window):
        for b, d, place in places:
            flipped = FLIP[d]
            ghosts[d, pl.ds(b, 1), :] = window[
                pl.ds(place, 1), flipped * FACE : (flipped + 1) * FACE
            ]

    strip = group_lane // SIDE
    within = group_lane % SIDE

    def interior(first, k):
        def tile(shift, h):
            return field[:, at_x(first, k, h, 1 + shift)]

        part = tile(0, 0), tile(0, 1)
        up = [pltpu.roll(v, SIDE, 1) for v in part]
        down = [pltpu.roll(v, LANES - SIDE, 1) for v in part]
        for h in range(2):
            total = jnp.where(within == 0, 0.0, pltpu.roll(part[h], 1, 1))
            total = total + jnp.where(within == SIDE - 1, 0.0, pltpu.roll(part[h], LANES - 1, 1))
            total = total + jnp.where(strip == 0, up[0] if h else 0.0, up[h])
            total = total + jnp.where(strip == half - 1, 0.0 if h else down[1], down[h])
            total = total + tile(-1, h) + tile(1, h)
            here = at_x(first, k, h)
            base[:, here] = (1.0 - relaxation) * part[h] + inv[:, here] * (mf[:, here] + total)

    def outside(x, h, ghost, at):
        strip = at // SIDE
        within = at % SIDE
        k, m = divmod(x, half)
        halves = slice(h * LANES, (h + 1) * LANES)
        total = jnp.where(within == 0, pltpu.roll(ghost(4, halves), (-x) % LANES, 1), 0.0)
        total = jnp.where(
            within == SIDE - 1, pltpu.roll(ghost(5, halves), SIDE - 1 - x, 1), total
        )
        source = slice(k * LANES, (k + 1) * LANES)
        if h == 0:
            side = pltpu.roll(ghost(2, source), (-SIDE * m) % LANES, 1)
            total = total + jnp.where(strip == 0, side, 0.0)
        else:
            side = pltpu.roll(ghost(3, source), SIDE * (half - 1 - m), 1)
            total = total + jnp.where(strip == half - 1, side, 0.0)
        if x == 0:
            total = total + ghost(0, halves)
        if x == SIDE - 1:
            total = total + ghost(1, halves)
        return total

    def group_ghost(d, at):
        return ghosts[d, :, at]

    def prepare():
        each_x(interior)

    prepare()

    size = SIDE * FACE
    links = jnp.zeros((group, LANES), jnp.int32)
    for s in range(nsub):
        for b in range(blocks):
            for d in range(FACES):
                links = jnp.where(
                    (group_row == s * blocks + b) & (group_lane == d), link_ref[s, b, d], links
                )
    links = links.astype(jnp.float32)
    added = jnp.zeros((group, LANES), jnp.float32)
    for x in range(SIDE):
        for h in range(2):
            added = added + mc[:, cells(x, h)]
    block_diag = 6.0 + jnp.sum(added, axis=1, keepdims=True) / size
    message = jnp.where(group_lane == FACES + 1, block_diag, links)

    for t in (0, -1, 1):
        if t:

            @pl.when(exists(t))
            def _(t=t):
                for ds in range(nsub):
                    raw_landing(t, ds).wait_recv()

        picks = chosen(t)
        for d in range(FACES):
            for h in range(2):
                total = jnp.zeros((group, LANES), jnp.float32)
                for s, j, pick in picks:
                    total = jnp.where(
                        pick, raw[(1 + t) * nsub + s, j : j + 1, spot(d, h)], total
                    )
                first[(1 + t) * group : (2 + t) * group, spot(d, h)] = total
    gather(first)

    def face_copy(t):
        return pltpu.make_async_remote_copy(
            src_ref=window.at[pl.ds(group, group)],
            dst_ref=window.at[pl.ds((1 - t) * group, group)],
            send_sem=face_send.at[0, 1 + t],
            recv_sem=face_recv.at[0, 1 - t],
            device_id=(pos + t, sub),
            device_id_type=MESH,
        )

    def face_landing(t):
        return pltpu.make_async_remote_copy(
            src_ref=window.at[pl.ds(group, group)],
            dst_ref=window.at[pl.ds((1 + t) * group, group)],
            send_sem=face_send.at[0, 1 + t],
            recv_sem=face_recv.at[0, 1 + t],
            device_id=(pos + t, sub),
            device_id_type=MESH,
        )

    def coarse_copy(t):
        return pltpu.make_async_remote_copy(
            src_ref=coarse.at[reach],
            dst_ref=coarse.at[reach - t],
            send_sem=coarse_send.at[reach + t],
            recv_sem=coarse_recv.at[reach - t],
            device_id=(pos + t, sub),
            device_id_type=MESH,
        )

    def coarse_landing(t):
        return pltpu.make_async_remote_copy(
            src_ref=coarse.at[reach],
            dst_ref=coarse.at[reach + t],
            send_sem=coarse_send.at[reach + t],
            recv_sem=coarse_recv.at[reach + t],
            device_id=(pos + t, sub),
            device_id_type=MESH,
        )

    def send_coarse():
        left = jnp.zeros((group, LANES), jnp.float32)
        for x in range(SIDE):
            for h in range(2):
                here = cells(x, h)
                left = left + (mf[:, here] - mc[:, here] * field[:, cells(x, h, 1)])
        block = group_lane % group == group_row
        lanes_row = lax.broadcasted_iota(jnp.int32, (8, LANES), 0)
        sums = jnp.zeros((8, LANES), jnp.float32)
        for d in range(FACES):
            both = last_faces[0:group, spot(d, 0)] + last_faces[0:group, spot(d, 1)]
            left = left - both
            total = jnp.sum(both, axis=1, keepdims=True) / size
            line = jnp.sum(jnp.where(block, total, 0.0), axis=0, keepdims=True)
            sums = jnp.where(lanes_row == d, line, sums)
        own_part = jnp.sum(left, axis=1, keepdims=True) / size
        coarse[reach, 0:group, :] = jnp.where(group_lane == FACES, own_part, message)
        coarse[reach, group : group + 8, :] = sums
        for t in sorted(far, key=lambda t: -abs(t)):
            guarded(t, lambda t=t: coarse_copy(t).start())

    def part_copy(t):
        return pltpu.make_async_remote_copy(
            src_ref=parts_out.at[(1 + t) // 2],
            dst_ref=parts_in.at[(1 - t) // 2],
            send_sem=face_send.at[1, 1 + t],
            recv_sem=face_recv.at[1, 1 - t],
            device_id=(pos + t, sub),
            device_id_type=MESH,
        )

    def part_landing(t):
        return pltpu.make_async_remote_copy(
            src_ref=parts_out.at[(1 + t) // 2],
            dst_ref=parts_in.at[(1 + t) // 2],
            send_sem=face_send.at[1, 1 + t],
            recv_sem=face_recv.at[1, 1 + t],
            device_id=(pos + t, sub),
            device_id_type=MESH,
        )

    def own_rows(link, store):
        for b in range(blocks):
            for d in range(FACES):
                place = link(b, d) - pos * group
                place = jnp.where((place < 0) | (place >= group), group, place)
                flipped = FLIP[d]
                store(
                    d * blocks + b,
                    last_faces[pl.ds(place, 1), flipped * FACE : (flipped + 1) * FACE],
                )

    def send_part(t):
        k = (1 + t) // 2

        def store(place, value):
            parts_out[k, place : place + 1, :] = value

        own_rows(lambda b, d: near_links[k, b, d], store)
        part_copy(t).start()

    def swept(x, h):
        here = cells(x, h)
        fresh = base[:, here] + inv[:, here] * outside(x, h, group_ghost, group_lane)
        field[:, cells(x, h, 1)] = fresh
        return fresh

    for step in range(PRE_SWEEPS):
        if step < PRE_SWEEPS - 1:

            def store_faces(d, h, packed):
                window[group : 2 * group, spot(d, h)] = packed

            pack(swept, group, group_lane, store_faces)
            for t in near:
                guarded(t, lambda t=t: face_copy(t).start())
            prepare()
            for ds in range(1, nsub):
                for k in range(len(inputs)):
                    peer_copy(ds, k).wait_send()
                raw_copy(0, ds).wait_send()
            for t in near:

                @pl.when(exists(t))
                def _(t=t):
                    for ds in range(nsub):
                        raw_copy(t, ds).wait_send()
                    link_copy(t).wait_send()
                    link_landing(t).wait_recv()
                    face_landing(t).wait_recv()

            gather(window)
        else:

            def store_last(d, h, packed):
                last_faces[0:group, spot(d, h)] = packed

            pack(swept, group, group_lane, store_last)
            send_coarse()
            for t in near:
                guarded(t, lambda t=t: send_part(t))
            prepare()

    def store_own(place, value):
        own_ghosts[place : place + 1, :] = value

    own_rows(lambda b, d: link_ref[sub, b, d], store_own)
    own_links = jnp.zeros((blocks, LANES), jnp.int32)
    for b in range(blocks):
        for d in range(FACES):
            own_links = jnp.where((row == b) & (lane == d), link_ref[sub, b, d], own_links)
    own_links = own_links.astype(jnp.float32)

    for t in near:
        guarded(t, lambda t=t: face_copy(t).wait_send())
    for t in far:

        @pl.when(exists(t))
        def _(t=t):
            coarse_copy(t).wait_send()
            coarse_landing(t).wait_recv()


    count_near = 2 * reach - 1
    shown = coarse[1 : 1 + count_near, 0:group, :]
    shape = (count_near, group, LANES)
    column = lax.broadcasted_iota(jnp.int32, shape, 2)
    index = (lax.broadcasted_iota(jnp.int32, shape, 0) + 1) * group + lax.broadcasted_iota(
        jnp.int32, shape, 1
    )
    origin = ((pos - reach) * group).astype(jnp.float32)
    numbered = column.astype(jnp.float32) + origin
    face_sums = jnp.zeros((8, LANES), jnp.float32)
    narrow = lax.broadcasted_iota(jnp.int32, (8, LANES), 1)
    for k in range(2 * reach + 1):
        face_sums = jnp.where(narrow // group == k, coarse[k, group : group + 8, :], face_sums)
    linked = jnp.zeros(shape, jnp.float32)
    entering = jnp.zeros(shape, jnp.float32)
    for d in range(FACES):
        link = shown[:, :, d : d + 1]
        hit = (link == numbered) & (link >= 0.0)
        linked = linked + hit.astype(jnp.float32)
        flipped = FLIP[d]
        entering = entering + jnp.where(hit, face_sums[flipped : flipped + 1][None], 0.0)
    residuals = shown[:, :, FACES : FACES + 1] + jnp.sum(entering, axis=2, keepdims=True)
    diags = shown[:, :, FACES + 1 : FACES + 2]
    diags = jnp.where(diags > 0.0, diags, 1.0)

    def own(whole):
        result = whole[:blocks]
        for s in range(1, nsub):
            result = jnp.where(sub == s, whole[s * blocks : (s + 1) * blocks], result)
        return result

    for t in near:

        @pl.when(exists(t))
        def _(t=t):
            part_copy(t).wait_send()
            part_landing(t).wait_recv()

    own_ghosts[...] = own_ghosts[...] + parts_in[0] + parts_in[1]

    def own_ghost(d, at):
        return own_ghosts[d * blocks : (d + 1) * blocks, at]

    for x in range(SIDE):
        for h in range(2):
            here = cells(x, h)
            out_ref[:, here] = own(base[:, here]) + own(inv[:, here]) * outside(
                x, h, own_ghost, lane
            )

    def turned(values, edge):
        kept = slice(edge, count_near - edge)
        spread = jnp.where(index[kept] == column[kept], values, 0.0)
        return jnp.sum(jnp.sum(spread, axis=0), axis=0, keepdims=True)

    scaled = relaxation / diags
    driven = scaled * residuals
    errors = driven
    for step in range(1, COARSE_SWEEPS):
        kept = slice(step, count_near - step)
        around = jnp.sum(linked[kept] * turned(errors, step - 1)[None], axis=2, keepdims=True)
        errors = (1.0 - relaxation) * errors[1:-1] + driven[kept] + scaled[kept] * around
    known = turned(errors, COARSE_SWEEPS - 1)

    own_numbered = lane.astype(jnp.float32) + origin
    own_at = reach * group + sub * blocks + row
    own_error = jnp.sum(jnp.where(lane == own_at, known, 0.0), axis=1, keepdims=True)
    jumps = []
    for d in range(FACES):
        link = own_links[:, d : d + 1]
        hit = (link == own_numbered) & (link >= 0.0)
        jumps.append(jnp.sum(jnp.where(hit, known, 0.0), axis=1, keepdims=True) - own_error)
    own_strip = lane // SIDE
    own_within = lane % SIDE
    plane = jnp.zeros((blocks, LANES), jnp.float32) + 6.0 * own_error
    plane = plane + jnp.where(own_within == 0, jumps[4], 0.0)
    plane = plane + jnp.where(own_within == SIDE - 1, jumps[5], 0.0)
    planes = (
        plane + jnp.where(own_strip == 0, jumps[2], 0.0),
        plane + jnp.where(own_strip == half - 1, jumps[3], 0.0),
    )
    kept = (1.0 - relaxation) * own_error + jnp.zeros((blocks, LANES), jnp.float32)

    for x in range(SIDE):
        for h in range(2):
            here = cells(x, h)
            extra = planes[h]
            if x == 0:
                extra = extra + jumps[0]
            if x == SIDE - 1:
                extra = extra + jumps[1]
            out_ref[:, here] = out_ref[:, here] + (kept + own(inv[:, here]) * extra)


def on_device(pressure, source_term, coefficient, new_slot, face_links):
    blocks, size = pressure.shape
    count = lax.axis_size("curve")
    nsub = lax.axis_size("sub")
    group = nsub * blocks
    others = max(1, nsub - 1)
    stage = pltpu.VMEM((nsub, blocks, size), jnp.float32)
    field = pltpu.VMEM((group, size), jnp.float32)
    padded = pltpu.VMEM((group, size + 2 * FACE), jnp.float32)
    window = pltpu.VMEM((3 * group + 8, FACES * FACE), jnp.float32)
    dma = pltpu.SemaphoreType.DMA
    hbm = pl.BlockSpec(memory_space=pltpu.HBM)
    return pl.pallas_call(
        functools.partial(kernel, count, nsub, blocks),
        out_shape=jax.ShapeDtypeStruct((blocks, size), jnp.float32),
        in_specs=[hbm] * 5,
        out_specs=pl.BlockSpec(memory_space=pltpu.VMEM),
        scratch_shapes=[
            pltpu.SMEM((blocks,), jnp.int32),
            pltpu.SMEM((nsub, blocks, FACES), jnp.int32),
            pltpu.SMEM((2, blocks, FACES), jnp.int32),
            stage,
            stage,
            stage,
            pltpu.VMEM((3 * nsub, blocks, FACES * FACE + LANES), jnp.float32),
            window,
            window,
            pltpu.VMEM((group + 8, FACES * FACE), jnp.float32),
            pltpu.VMEM((2, FACES * blocks, FACE), jnp.float32),
            pltpu.VMEM((2, FACES * blocks, FACE), jnp.float32),
            pltpu.VMEM((FACES, group, FACE), jnp.float32),
            pltpu.VMEM((FACES * blocks, FACE), jnp.float32),
            field,
            field,
            field,
            padded,
            field,
            pltpu.VMEM((2 * COARSE_SWEEPS + 3, group + 8, LANES), jnp.float32),
            dma((5,)),
            dma((3 * nsub,)),
            dma((3 * nsub,)),
            dma((PRE_SWEEPS, 3)),
            dma((PRE_SWEEPS, 3)),
            dma((4, others)),
            dma((4, others)),
            dma((2 * COARSE_SWEEPS + 3,)),
            dma((2 * COARSE_SWEEPS + 3,)),
            dma((2,)),
            dma((2,)),
        ],
        compiler_params=pltpu.CompilerParams(
            collective_id=0, has_side_effects=True, vmem_limit_bytes=32 * 1024 * 1024
        ),
    )(
        *(
            pltpu.with_memory_space_constraint(array, pltpu.HBM)
            for array in (new_slot, face_links, pressure, source_term, coefficient)
        )
    )


def solution(mesh):
    placed = (
        P(("curve", "sub"), None),
        P(("curve", "sub"), None),
        P(("curve", "sub"), None),
        P(("curve", "sub")),
        P(("curve", "sub"), None),
    )
    return jax.shard_map(
        on_device, mesh=mesh, in_specs=placed, out_specs=P(("curve", "sub"), None), check_vma=False
    )
```
